32 devices in a mesh: rep: 2 (over y), tp: 8 (over z, x), dp: 2 (over core).
Axes of the slice: x: 2, y: 2, z: 4, core: 2. Of those that a mesh axis runs over, the one named last changes fastest.
Arguments:
- state_hidden: bfloat16 [8, 8192], P(('rep', 'dp'), 'tp'), parts along dimension 0, may hold values from -40 to 40
- action_seeds: int32 [8, 64], P(('rep', 'dp')), parts along dimension 0, may hold values from 0 to 65520
- action_mean: float32 [256], P('rep'), parts along dimension 0, may hold values from -4 to 4
- action_spread: float32 [256], P('rep'), parts along dimension 0, may hold values from 0.5 to 2
- action_weight: bfloat16 [128, 8192], P(None, 'tp'), may hold values from -0.5 to 0.5
- norm_gain: float32 [8192], P('tp'), may hold values from 0.1 to 1.9
- gate_weight: bfloat16 [8192, 24576], P('dp', 'tp'), may hold values from -0.0625 to 0.0625
- up_weight: bfloat16 [8192, 24576], P('dp', 'tp'), may hold values from -0.0625 to 0.0625
- down_weight: bfloat16 [24576, 8192], P('tp', 'dp'), may hold values from -0.0546875 to 0.0546875
- head_gain: float32 [8192], P('tp'), may hold values from 0.1 to 1.9
- value_weight: float32 [8192], P('tp'), may hold values from -0.0625 to 0.0625
Outputs:
- output_rows: bfloat16 [8, 64, 8192], P(('rep', 'dp'), None, 'tp'), parts along dimension 0
- values: float32 [8, 64], P(('rep', 'dp')), parts along dimension 0
The draws below stay inside these ranges and needn't reach their ends.
There are 2 independent parts, one for each index of `rep`. The reference program is written for one: setup_inputs(seed, part) draws one part's arguments, and reference() takes and returns one part's arrays. A program takes and returns all parts, laid end to end along the dimension named above; an argument that names none is the same for every part. Nothing has to cross between parts.
All inputs are finite; a program needn't handle non-finite values.
Results may differ from the reference program's by a relative error of at most 0.014.
Values may be sent and summed in bfloat16 or wider, within the bound.
No kernel may reach another device: no remote copies, remote signals or barrier semaphores. Data moves between devices by JAX's collectives and lax.ppermute only.
A program may use at most 448 MiB of HBM per device.

```python
import math
import jax
import jax.numpy as jnp
from jax import lax

D = 8192
FF = 24576
ACT = 128
CAND = 64
STATES = 4


def draw_state_hidden(key, part):
    key = jax.random.fold_in(key, 7)
    row_key, col_key, base_key = jax.random.split(key, 3)
    column_ramp = jnp.arange(D, dtype=jnp.float32) / (D - 1)
    col_scale = jnp.exp(math.log(3.0) * column_ramp + math.log(10.0) * 0.5 * jax.random.uniform(col_key, (D,), dtype=jnp.float32)) / 3.0
    base_values = jnp.clip(jax.random.normal(base_key, (STATES, D), dtype=jnp.float32), -4.0, 4.0)
    row_scale = 0.3 * jnp.exp(math.log(10.0) * jax.random.uniform(row_key, (STATES, 1), dtype=jnp.float32))
    return (base_values * row_scale * col_scale).astype(jnp.bfloat16)


def set_ends(array, own_key, smallest, largest):
    longest = array.shape.index(max(array.shape))
    spots = []
    for shift in (0, 1):
        where = [jax.random.randint(jax.random.fold_in(own_key, axis), (), 0, length) for axis, length in enumerate(array.shape)]
        where[longest] = (where[longest] + shift) % array.shape[longest]
        spots.append(tuple(where))
    return array.at[spots[0]].set(smallest).at[spots[1]].set(largest)


def strengthened(array, key, source, target, parts, factor):
    def block_of(dim):
        return (jnp.arange(array.shape[dim]) // (array.shape[dim] // parts)).reshape((-1,) + (1,) * (array.ndim - 1 - dim))

    near = jax.random.permutation(key, parts)[block_of(target)]
    far = (block_of(target) + parts // 2) % parts
    return jnp.where((block_of(source) == near) | (block_of(source) == far), factor * array, array)


def steps_of(key, dims, pieces, smallest, high):
    level = 1.0
    for position, parts in pieces:
        steps = jax.random.uniform(jax.random.fold_in(jax.random.fold_in(key, 6), position), (parts,), jnp.float32, smallest / len(pieces), high / len(pieces))
        level = level * jnp.repeat(jnp.exp(steps), dims[position] // parts).reshape((-1,) + (1,) * (len(dims) - 1 - position))
    return level


def scatter_about(stream_key, dims, deviation, most, pieces=(), held_as=jnp.bfloat16):
    array = jax.random.normal(stream_key, dims, jnp.float32) * deviation
    if len(pieces) > 0:
        array = steps_of(stream_key, dims, pieces, -0.22, 0.18) * array
    return jnp.clip(array, min=-most, max=most).astype(held_as)


def gaussian_with(rng, dims, deviation, limit, shards, heavy, kind=jnp.bfloat16):
    entries = deviation * jax.random.normal(rng, dims, jnp.float32)
    if shards:
        entries = entries * steps_of(rng, dims, shards, -0.22, 0.18)
    return jnp.clip(strengthened(entries, jax.random.fold_in(rng, 3), *heavy), -limit, limit).astype(kind)


def setup_inputs(seed: int = 0, part: int = 0) -> dict:
    keys = jax.random.split(jax.random.key(seed), 12)
    part_splits = jax.random.split(jax.random.fold_in(keys[11], part), 12)
    return {
        "state_hidden": draw_state_hidden(jax.random.fold_in(jax.random.fold_in(keys[11], part), 71), part),
        "action_seeds": set_ends(jax.random.randint(part_splits[1], (STATES, CAND), 0, 65521), jax.random.fold_in(part_splits[1], 1), 0, 65520).astype(jnp.int32),
        "action_mean": scatter_about(part_splits[2], (ACT,), 1.0, 4.0, (), jnp.float32),
        "action_spread": jnp.clip(jnp.exp(jax.random.uniform(part_splits[3], (ACT,), jnp.float32, math.log(0.5), math.log(2.0))), 0.5, 2.0),
        "action_weight": scatter_about(keys[4], (ACT, D), ACT ** -0.5, 0.5, ((1, 8),)),
        "norm_gain": jnp.clip(1.0 + 0.18 * jax.random.normal(keys[5], (D,), jnp.float32), 0.1, 1.9),
        "gate_weight": scatter_about(keys[6], (D, FF), D ** -0.5, 0.0625, ((0, 2), (1, 8))),
        "up_weight": scatter_about(keys[7], (D, FF), D ** -0.5, 0.0625, ((0, 2), (1, 8))),
        "down_weight": gaussian_with(keys[8], (FF, D), FF ** -0.5, 0.0546875, ((0, 8), (1, 2)), (0, 1, 8, 2.0)),
        "head_gain": jnp.clip(1.0 + 0.18 * jax.random.normal(keys[9], (D,), jnp.float32), 0.1, 1.9),
        "value_weight": scatter_about(keys[10], (D,), D ** -0.5, 0.0625, ((0, 8),), jnp.float32),
    }


epsilon = 1e-05
modulus = 251

def action_features(action_seeds, action_mean, action_spread):
    harmonic = jnp.arange(1, action_mean.shape[0] + 1, dtype=jnp.int32)
    phases = action_seeds[:, :, None] * harmonic % modulus
    angles = phases.astype(jnp.float32) * (2.0 * math.pi / modulus)
    return (action_mean + action_spread * jnp.cos(angles)).astype(jnp.bfloat16)

def head_value(output_rows, head_gain, value_weight):
    wide_out = output_rows.astype(jnp.float32)
    scale = lax.rsqrt(lax.optimization_barrier(jnp.mean(wide_out * wide_out, axis=1)) + epsilon)
    return lax.optimization_barrier(jnp.sum(wide_out * (head_gain * value_weight), axis=1)) * scale

def reference(state_hidden, action_seeds, action_mean, action_spread, action_weight, norm_gain, gate_weight, up_weight, down_weight, head_gain, value_weight):
    features = action_features(action_seeds, action_mean, action_spread)
    embedded = jnp.dot(features.reshape(STATES * CAND, ACT), action_weight, preferred_element_type=jnp.float32)
    inputs = (state_hidden.astype(jnp.float32)[:, None, :] + embedded.reshape(STATES, CAND, D)).reshape(STATES * CAND, D).astype(jnp.bfloat16)
    wide_in = inputs.astype(jnp.float32)
    scale = lax.rsqrt(lax.optimization_barrier(jnp.mean(wide_in * wide_in, axis=1, keepdims=True)) + epsilon)
    normed = (wide_in * scale * norm_gain).astype(jnp.bfloat16)
    gate_sum = jnp.dot(normed, gate_weight, preferred_element_type=jnp.float32)
    up_sum = jnp.dot(normed, up_weight, preferred_element_type=jnp.float32)
    hidden = (jax.nn.silu(gate_sum) * up_sum).astype(jnp.bfloat16)
    summed = jnp.dot(hidden, down_weight, preferred_element_type=jnp.float32)
    output_rows = (wide_in + summed).astype(jnp.bfloat16)
    values = head_value(output_rows, head_gain, value_weight)
    return (output_rows.reshape(STATES, CAND, D), values.reshape(STATES, CAND))
```

```python
import math

import jax
import jax.numpy as jnp
from jax import lax
from jax.sharding import PartitionSpec as P

epsilon = 1e-05
modulus = 251
PAD = 8


def action_features(action_seeds, action_mean, action_spread):
    harmonic = jnp.arange(1, action_mean.shape[0] + 1, dtype=jnp.int32)
    phases = action_seeds[:, :, None] * harmonic % modulus
    angles = phases.astype(jnp.float32) * (2.0 * math.pi / modulus)
    return (action_mean + action_spread * jnp.cos(angles)).astype(jnp.bfloat16)


def head_value(output_rows, head_gain, value_weight):
    wide_out = output_rows.astype(jnp.float32)
    scale = lax.rsqrt(jnp.mean(wide_out * wide_out, axis=1) + epsilon)
    return jnp.sum(wide_out * (head_gain * value_weight), axis=1) * scale


def local_gathered(
    state_hidden,
    action_seeds,
    action_mean,
    action_spread,
    action_weight,
    norm_gain,
    gate_weight,
    up_weight,
    down_weight,
    head_gain,
    value_weight,
):
    state_count, cand_count = action_seeds.shape
    row_count = state_count * cand_count
    local_cols = action_weight.shape[1]
    features = action_features(action_seeds, action_mean, action_spread)
    embedded = jnp.dot(
        features.reshape(row_count, features.shape[2]),
        action_weight,
        preferred_element_type=jnp.float32,
    )
    inputs_local = (
        (
            state_hidden.astype(jnp.float32)[:, None, :]
            + embedded.reshape(state_count, cand_count, local_cols)
        )
        .reshape(row_count, local_cols)
        .astype(jnp.bfloat16)
    )
    gathered, gain_full = (
        lax.all_gather(inputs_local, "tp", axis=1, tiled=True),
        lax.all_gather(norm_gain.astype(jnp.bfloat16), "tp", axis=0, tiled=True).astype(
            norm_gain.dtype
        ),
    )
    scale = lax.rsqrt(
        jnp.mean(jnp.square(gathered.astype(jnp.float32)), axis=1, keepdims=True) + epsilon
    )
    normed = (gathered.astype(jnp.float32) * scale * gain_full).astype(jnp.bfloat16)
    gate_sum = jnp.dot(
        normed,
        lax.all_gather(gate_weight, "dp", axis=0, tiled=True),
        preferred_element_type=jnp.float32,
    )
    up_sum = jnp.dot(
        normed,
        lax.all_gather(up_weight, "dp", axis=0, tiled=True),
        preferred_element_type=jnp.float32,
    )
    hidden = (jax.nn.silu(gate_sum) * up_sum).astype(jnp.bfloat16)
    partial_terms = jnp.dot(
        hidden,
        lax.all_gather(down_weight, "dp", axis=1, tiled=True),
        preferred_element_type=jnp.float32,
    )
    summed_local = lax.psum_scatter(partial_terms, "tp", scatter_dimension=1, tiled=True)
    output_local = (inputs_local.astype(jnp.float32) + summed_local).astype(jnp.bfloat16)
    output_full, head_full, value_full = (
        lax.all_gather(output_local, "tp", axis=1, tiled=True),
        lax.all_gather(head_gain.astype(jnp.bfloat16), "tp", axis=0, tiled=True).astype(
            head_gain.dtype
        ),
        lax.all_gather(value_weight.astype(jnp.bfloat16), "tp", axis=0, tiled=True).astype(
            value_weight.dtype
        ),
    )
    values = head_value(output_full, head_full, value_full)
    return (
        output_local.reshape(state_count, cand_count, local_cols),
        values.reshape(state_count, cand_count),
    )


RING = 8


def chip_of(pos):
    pos = pos % RING
    z, x = (pos, 0) if pos < 4 else (7 - pos, 1)
    return 2 * z + x


def core_of(pos):
    return chip_of(pos) // 4


def send(array, pairs):
    return lax.ppermute(
        array, ("tp", "dp"), [(2 * st + sd, 2 * dt + dd) for (st, sd), (dt, dd) in pairs]
    )


def local_ring(
    state_hidden,
    action_seeds,
    action_mean,
    action_spread,
    action_weight,
    norm_gain,
    gate_weight,
    up_weight,
    down_weight,
    head_gain,
    value_weight,
):
    f32, bf16 = jnp.float32, jnp.bfloat16
    states, cands = action_seeds.shape
    rows = states * cands
    act, cols = action_weight.shape
    half = act // 2
    full_width = gate_weight.shape[0] * 2
    tp, dp = lax.axis_index("tp"), lax.axis_index("dp")
    z, x = tp // 2, tp % 2
    swap_core = [((t, d), (t, 1 - d)) for t in range(8) for d in range(2)]
    swap_x = [((t, d), (t ^ 1, d)) for t in range(8) for d in range(2)]

    piece = jnp.concatenate(
        [
            lax.dynamic_slice_in_dim(action_weight, dp * half, half, 0),
            state_hidden,
            norm_gain.astype(bf16)[None],
            jnp.zeros((PAD - states - 1, cols), bf16),
        ],
        axis=0,
    )
    own, across = [], []
    for j in range(4):
        pairs = []
        for t in range(8):
            for d in range(2):
                zz, xx = t // 2, t % 2
                to = (2 * (zz % 2) + d) ^ j
                pairs.append(((t, d), (2 * to + xx, zz // 2)))
        got = send(piece, pairs)
        own.append(got)
        across.append(send(got, swap_x))
    own, across = jnp.stack(own), jnp.stack(across)
    blocks = jnp.stack([jnp.where(x == 0, own, across), jnp.where(x == 0, across, own)])
    order = jnp.stack([z ^ k for k in range(4)])
    blocks = jnp.take(blocks, order, axis=1)
    blocks = blocks.reshape(2, 2, 2, half + PAD, cols)
    blocks = blocks.transpose(2, 3, 1, 0, 4).reshape(2, half + PAD, 4 * cols)
    weight_half = blocks[:, :half].reshape(act, 4 * cols)
    state_half = blocks[:, half : half + states].reshape(2 * states, 4 * cols)
    gain_half = blocks[0, half + states]

    features = action_features(action_seeds, action_mean, action_spread).reshape(rows, act)
    other_features = send(features, swap_core)
    all_features = jnp.where(
        dp == 0,
        jnp.concatenate([features, other_features]),
        jnp.concatenate([other_features, features]),
    )
    row_state = jnp.arange(2 * rows) // cands
    onehot = (row_state[:, None] == jnp.arange(PAD)[None]).astype(bf16)
    wide_features = jnp.concatenate([all_features, onehot], axis=1)

    basis = jnp.concatenate(
        [weight_half, state_half, jnp.zeros((PAD - 2 * states, 4 * cols), bf16)]
    )
    lhs = (basis.astype(f32) * gain_half.astype(f32)[None]).astype(bf16)

    gate_own = jnp.dot(lhs, gate_weight, preferred_element_type=f32)
    gate_other = send(gate_own.astype(bf16), swap_core)
    up_own = jnp.dot(lhs, up_weight, preferred_element_type=f32)
    up_other = send(up_own.astype(bf16), swap_core)

    inputs_half = jnp.dot(wide_features, basis, preferred_element_type=f32).astype(bf16)
    squares = jnp.sum(jnp.square(inputs_half.astype(f32)), axis=1)
    squares = squares + send(squares, swap_core)
    scale = lax.rsqrt(squares / full_width + epsilon)[:, None]

    gate_basis = (gate_own + gate_other.astype(f32)).astype(bf16)
    up_basis = (up_own + up_other.astype(f32)).astype(bf16)
    gate_sum = scale * jnp.dot(wide_features, gate_basis, preferred_element_type=f32)
    up_sum = scale * jnp.dot(wide_features, up_basis, preferred_element_type=f32)
    hidden = (jax.nn.silu(gate_sum) * up_sum).astype(bf16)

    partial = jnp.dot(hidden, down_weight, preferred_element_type=f32).astype(bf16)

    embedded = jnp.dot(features, action_weight, preferred_element_type=f32)
    inputs_local = (
        (state_hidden.astype(f32)[:, None, :] + embedded.reshape(states, cands, cols))
        .reshape(rows, cols)
        .astype(bf16)
    )

    pos = jnp.where(x == 0, z, 7 - z)

    def share(to, part):
        to = to % RING
        chip = jnp.where(to < 4, 2 * to, 2 * (7 - to) + 1)
        block = jnp.clip(chip - 4 * dp, 0, 3)
        return lax.dynamic_slice(partial, (part * rows, block * cols), (rows, cols))

    chains = [(1, 0, 4), (-1, 1, 4), (1, 1, 3), (-1, 0, 3)]
    held = [None] * len(chains)
    for step in range(4):
        for index, (way, part, hops) in enumerate(chains):
            at = step - (4 - hops)
            if at < 0:
                continue
            left = hops - at
            value = share(pos + way * left, part)
            if held[index] is not None:
                value = (value.astype(f32) + held[index].astype(f32)).astype(bf16)
            pairs = []
            for p in range(RING):
                to = (p + way * left) % RING
                core = core_of(to)
                pairs.append(
                    ((chip_of(p), core), (chip_of(p + way), part if left == 1 else core))
                )
            held[index] = send(value, pairs)
    mine = z // 2 == dp
    crossing = share(pos, 1 - dp)
    crossed = send(crossing, [((t, t // 4), (t, 1 - t // 4)) for t in range(8)])
    summed = jnp.where(mine, share(pos, dp), crossed).astype(f32)
    for got in held:
        summed = summed + got.astype(f32)
    output_local = (inputs_local.astype(f32) + summed).astype(bf16)

    wide_out = output_local.astype(f32)
    sums = jnp.stack(
        [
            jnp.sum(wide_out * wide_out, axis=1),
            jnp.sum(wide_out * (head_gain * value_weight), axis=1),
        ]
    )
    total = sums
    for k in range(1, 8):
        total = total + send(sums, [((t, d), (t ^ k, d)) for t in range(8) for d in range(2)])
    values = total[1] * lax.rsqrt(total[0] / full_width + epsilon)
    return (
        output_local.reshape(states, cands, cols),
        values.reshape(states, cands),
    )


def solution(mesh):
    local = local_ring if mesh.shape["tp"] == RING and mesh.shape["dp"] == 2 else local_gathered
    return jax.shard_map(
        local,
        mesh=mesh,
        in_specs=(
            P(("rep", "dp"), "tp"),
            P(("rep", "dp"), None),
            P("rep"),
            P("rep"),
            P(None, "tp"),
            P("tp"),
            P("dp", "tp"),
            P("dp", "tp"),
            P("tp", "dp"),
            P("tp"),
            P("tp"),
        ),
        out_specs=(P(("rep", "dp"), None, "tp"), P(("rep", "dp"), None)),
        check_vma=False,
    )
```

```python
import functools
import math

import jax
import jax.numpy as jnp
from jax import lax
from jax.experimental import pallas as pl
from jax.experimental.pallas import tpu as pltpu
from jax.sharding import PartitionSpec as P

epsilon = 1e-05
modulus = 251


def action_features(action_seeds, action_mean, action_spread):
    harmonic = jnp.arange(1, action_mean.shape[0] + 1, dtype=jnp.int32)
    phases = action_seeds[:, :, None] * harmonic % modulus
    angles = phases.astype(jnp.float32) * (2.0 * math.pi / modulus)
    return (action_mean + action_spread * jnp.cos(angles)).astype(jnp.bfloat16)


def head_value(output_rows, head_gain, value_weight):
    wide_out = output_rows.astype(jnp.float32)
    scale = lax.rsqrt(jnp.mean(wide_out * wide_out, axis=1) + epsilon)
    return jnp.sum(wide_out * (head_gain * value_weight), axis=1) * scale


def local_gathered(
    state_hidden,
    action_seeds,
    action_mean,
    action_spread,
    action_weight,
    norm_gain,
    gate_weight,
    up_weight,
    down_weight,
    head_gain,
    value_weight,
):
    state_count, cand_count = action_seeds.shape
    row_count = state_count * cand_count
    local_cols = action_weight.shape[1]
    features = action_features(action_seeds, action_mean, action_spread)
    embedded = jnp.dot(
        features.reshape(row_count, features.shape[2]),
        action_weight,
        preferred_element_type=jnp.float32,
    )
    inputs_local = (
        (
            state_hidden.astype(jnp.float32)[:, None, :]
            + embedded.reshape(state_count, cand_count, local_cols)
        )
        .reshape(row_count, local_cols)
        .astype(jnp.bfloat16)
    )
    gathered, gain_full = (
        lax.all_gather(inputs_local, "tp", axis=1, tiled=True),
        lax.all_gather(norm_gain.astype(jnp.bfloat16), "tp", axis=0, tiled=True).astype(
            norm_gain.dtype
        ),
    )
    scale = lax.rsqrt(
        jnp.mean(jnp.square(gathered.astype(jnp.float32)), axis=1, keepdims=True) + epsilon
    )
    normed = (gathered.astype(jnp.float32) * scale * gain_full).astype(jnp.bfloat16)
    gate_sum = jnp.dot(
        normed,
        lax.all_gather(gate_weight, "dp", axis=0, tiled=True),
        preferred_element_type=jnp.float32,
    )
    up_sum = jnp.dot(
        normed,
        lax.all_gather(up_weight, "dp", axis=0, tiled=True),
        preferred_element_type=jnp.float32,
    )
    hidden = (jax.nn.silu(gate_sum) * up_sum).astype(jnp.bfloat16)
    partial_terms = jnp.dot(
        hidden,
        lax.all_gather(down_weight, "dp", axis=1, tiled=True),
        preferred_element_type=jnp.float32,
    )
    summed_local = lax.psum_scatter(partial_terms, "tp", scatter_dimension=1, tiled=True)
    output_local = (inputs_local.astype(jnp.float32) + summed_local).astype(jnp.bfloat16)
    output_full, head_full, value_full = (
        lax.all_gather(output_local, "tp", axis=1, tiled=True),
        lax.all_gather(head_gain.astype(jnp.bfloat16), "tp", axis=0, tiled=True).astype(
            head_gain.dtype
        ),
        lax.all_gather(value_weight.astype(jnp.bfloat16), "tp", axis=0, tiled=True).astype(
            value_weight.dtype
        ),
    )
    values = head_value(output_full, head_full, value_full)
    return (
        output_local.reshape(state_count, cand_count, local_cols),
        values.reshape(state_count, cand_count),
    )


TP = 8
SMALL = 16
MIB = 1024 * 1024


def send(array, pairs):
    return lax.ppermute(
        array, ("tp", "dp"), [(2 * st + sd, 2 * dt + dd) for (st, sd), (dt, dd) in pairs]
    )


def basis_body(block_count, accumulate, square, narrow, *refs):
    refs = list(refs)
    refs.pop(0)
    blocks = [refs.pop(0) for _ in range(block_count)]
    features = refs.pop(0) if square else None
    gate_ref, up_ref = refs.pop(0), refs.pop(0)
    before = refs.pop(0) if accumulate else None
    total = refs.pop(0)
    narrow_ref = refs.pop(0) if narrow else None
    square_ref = refs.pop(0) if square else None
    lhs = refs.pop(0)
    tile, block = pl.program_id(0), pl.program_id(1)
    states_at = features.shape[1] - SMALL if square else blocks[0].shape[0] - SMALL

    for index, ref in enumerate(blocks):

        @pl.when((tile == 0) & (block == index))
        def _(index=index, ref=ref):
            gain = ref[states_at + 4 : states_at + 5, :].astype(jnp.float32)
            lhs[index] = (ref[...].astype(jnp.float32) * gain).astype(jnp.bfloat16)
            if square:
                rows = jnp.dot(features[...], ref[...], preferred_element_type=jnp.float32)
                rows = rows.astype(jnp.bfloat16).astype(jnp.float32)
                rows = rows * rows
                part = rows[:, :128]
                for at in range(128, rows.shape[1], 128):
                    part += rows[:, at : at + 128]
                if index == 0:
                    square_ref[...] = part
                else:
                    square_ref[...] += part

    gate = jnp.dot(lhs[block], gate_ref[...], preferred_element_type=jnp.float32)
    up = jnp.dot(lhs[block], up_ref[...], preferred_element_type=jnp.float32)

    def first():
        if accumulate:
            total[0] = before[0] + gate
            total[1] = before[1] + up
        else:
            total[0] = gate
            total[1] = up

    def later():
        total[0] += gate
        total[1] += up

    if block_count == 1:
        first()
    else:
        pl.when(block == 0)(first)
        pl.when(block > 0)(later)
    if narrow:

        @pl.when(block == block_count - 1)
        def _():
            narrow_ref[...] = total[...].astype(jnp.bfloat16)


def basis_products(
    blocks, which, features, gate_weight, up_weight, before, columns, square, narrow, tile
):
    count = len(blocks)
    m, k = blocks[0].shape
    start, stop = columns
    width = stop - start
    tiles, base = width // tile, start // tile
    whole = lambda *shape: pl.BlockSpec(shape, lambda j, b, s: (0,) * len(shape))
    weight = pl.BlockSpec((k, tile), lambda j, b, s: (s[b], base + j))
    specs, operands = [whole(m, k)] * count, list(blocks)
    if square:
        specs.append(whole(*features.shape))
        operands.append(features)
    specs += [weight, weight]
    operands += [gate_weight, up_weight]
    if before is not None:
        specs.append(pl.BlockSpec((2, m, tile), lambda j, b, s: (0, 0, base + j)))
        operands.append(before)
    part = pl.BlockSpec((2, m, tile), lambda j, b, s: (0, 0, j))
    outs = [jax.ShapeDtypeStruct((2, m, width), jnp.float32)]
    out_specs = [part]
    if narrow:
        outs.append(jax.ShapeDtypeStruct((2, m, width), jnp.bfloat16))
        out_specs.append(part)
    if square:
        outs.append(jax.ShapeDtypeStruct((features.shape[0], 128), jnp.float32))
        out_specs.append(whole(features.shape[0], 128))
    return pl.pallas_call(
        functools.partial(basis_body, count, before is not None, square, narrow),
        out_shape=outs,
        grid_spec=pltpu.PrefetchScalarGridSpec(
            num_scalar_prefetch=1,
            grid=(tiles, count),
            in_specs=specs,
            out_specs=out_specs,
            scratch_shapes=[pltpu.VMEM((count, m, k), jnp.bfloat16)],
        ),
        compiler_params=pltpu.CompilerParams(
            dimension_semantics=("arbitrary", "arbitrary"), vmem_limit_bytes=32 * MIB
        ),
        cost_estimate=pl.CostEstimate(
            flops=4 * m * k * width * count,
            bytes_accessed=4 * k * width * count,
            transcendentals=0,
        ),
    )(which, *operands)


def hidden_body(width, own, other, features, square_own, square_other, hidden):
    squares = jnp.sum(square_own[...] + square_other[...], axis=1, keepdims=True)
    scale = lax.rsqrt(squares / width + epsilon)
    basis = (own[...] + other[...].astype(jnp.float32)).astype(jnp.bfloat16)
    gate = scale * jnp.dot(features[...], basis[0], preferred_element_type=jnp.float32)
    up = scale * jnp.dot(features[...], basis[1], preferred_element_type=jnp.float32)
    hidden[...] = (gate / (1.0 + jnp.exp(-gate)) * up).astype(jnp.bfloat16)


def hidden_units(own, other, features, square_own, square_other, width, tile):
    _, m, units = own.shape
    rows = features.shape[0]
    whole = lambda *shape: pl.BlockSpec(shape, lambda j: (0,) * len(shape))
    part = pl.BlockSpec((2, m, tile), lambda j: (0, 0, j))
    return pl.pallas_call(
        functools.partial(hidden_body, width),
        out_shape=jax.ShapeDtypeStruct((rows, units), jnp.bfloat16),
        grid=(units // tile,),
        in_specs=[part, part, whole(rows, m), whole(rows, 128), whole(rows, 128)],
        out_specs=pl.BlockSpec((rows, tile), lambda j: (0, j)),
        compiler_params=pltpu.CompilerParams(vmem_limit_bytes=16 * MIB),
        cost_estimate=pl.CostEstimate(
            flops=4 * m * rows * units, bytes_accessed=12 * m * units, transcendentals=rows * units
        ),
    )(own, other, features, square_own, square_other)


def down_body(count, which, *refs):
    hidden = refs[:count]
    weight, *outs = refs[count:]
    total = None
    at = 0
    for ref in hidden:
        depth = ref.shape[1]
        term = jnp.dot(ref[...], weight[at : at + depth, :], preferred_element_type=jnp.float32)
        total = term if total is None else total + term
        at += depth
    rows = total.shape[0] // 2
    for part in range(2):
        outs[part][...] = total[part * rows : (part + 1) * rows].astype(jnp.bfloat16)


def down_products(hidden, down_weight, which, width, tile):
    rows = hidden[0].shape[0]
    depth = down_weight.shape[0]
    tiles = width // tile
    half = pl.BlockSpec((rows // 2, tile), lambda j, s: (0, j))
    return pl.pallas_call(
        functools.partial(down_body, len(hidden)),
        out_shape=[jax.ShapeDtypeStruct((rows // 2, width), jnp.bfloat16)] * 2,
        grid_spec=pltpu.PrefetchScalarGridSpec(
            num_scalar_prefetch=1,
            grid=(tiles,),
            in_specs=[pl.BlockSpec(h.shape, lambda j, s: (0, 0)) for h in hidden]
            + [pl.BlockSpec((depth, tile), lambda j, s: (0, s[0] * tiles + j))],
            out_specs=[half, half],
        ),
        compiler_params=pltpu.CompilerParams(vmem_limit_bytes=32 * MIB),
        cost_estimate=pl.CostEstimate(
            flops=2 * rows * depth * width, bytes_accessed=2 * depth * width, transcendentals=0
        ),
    )(which, *hidden, down_weight)


def local_blocks(
    state_hidden,
    action_seeds,
    action_mean,
    action_spread,
    action_weight,
    norm_gain,
    gate_weight,
    up_weight,
    down_weight,
    head_gain,
    value_weight,
):
    f32, bf16 = jnp.float32, jnp.bfloat16
    states, cands = action_seeds.shape
    rows = states * cands
    act, cols = action_weight.shape
    half = act // 2
    units = gate_weight.shape[1]
    full_width = gate_weight.shape[0] * 2
    tp, dp = lax.axis_index("tp"), lax.axis_index("dp")
    home = tp // 4 == dp
    place = tp % 4
    every = [(t, d) for t in range(TP) for d in range(2)]
    swap_core = [((t, d), (t, 1 - d)) for t, d in every]

    seeds = jnp.concatenate([action_seeds // 256, action_seeds % 256]).astype(bf16)
    seeds_row = jnp.pad(seeds.reshape(1, -1), ((0, 0), (0, cols - seeds.size)))
    piece = jnp.concatenate(
        [
            lax.dynamic_slice_in_dim(action_weight, dp * half, half, 0),
            state_hidden,
            norm_gain.astype(bf16)[None],
            seeds_row,
            jnp.zeros((SMALL - states - 2, cols), bf16),
        ],
        axis=0,
    )
    first = send(
        piece,
        [((t, t // 4), (t ^ 4, t // 4)) for t in range(TP)]
        + [((t, 1 - t // 4), (t, t // 4)) for t in range(TP)],
    )
    second = send(piece, [((t, 1 - t // 4), (t ^ 4, t // 4)) for t in range(TP)])
    same = jnp.where(home, piece, first)
    other = jnp.where(home, first, second)
    low = jnp.where(dp == 0, same, other)
    high = jnp.where(dp == 0, other, same)
    block = jnp.concatenate(
        [
            low[:half],
            high[:half],
            low[half : half + states],
            high[half : half + states],
            low[half + states : half + states + 1],
            jnp.zeros((SMALL - 2 * states - 1, cols), bf16),
        ]
    )

    near = {k: send(block, [((t, d), (t ^ k, d)) for t, d in every]) for k in (2, 1, 3)}

    all_seeds = jnp.concatenate(
        [part[half + states + 1, : seeds.size].reshape(2, states, cands) for part in (low, high)],
        axis=1,
    ).astype(jnp.int32)
    all_seeds = all_seeds[0] * 256 + all_seeds[1]
    features = action_features(all_seeds, action_mean, action_spread).reshape(2 * rows, act)
    row_state = jnp.arange(2 * rows) // cands
    onehot = (row_state[:, None] == jnp.arange(SMALL)[None]).astype(bf16)
    features = jnp.concatenate([features, onehot], axis=1)

    index = lambda *ks: jnp.stack([place ^ k for k in ks]).astype(jnp.int32)
    weights = (gate_weight, up_weight)
    tile = 512
    basis, square0 = basis_products(
        [block], index(0), features, *weights, None, (0, units), True, False, tile
    )
    basis, square2 = basis_products(
        [near[2]], index(2), features, *weights, basis, (0, units), True, False, tile
    )
    cut = units // 2
    rest = [near[1], near[3]]
    own_a, narrow_a, square13 = basis_products(
        rest, index(1, 3), features, *weights, basis, (0, cut), True, True, tile
    )
    square = square0 + square2 + square13
    other_a = send(narrow_a, swap_core)
    other_square = send(square, swap_core)
    own_b, narrow_b = basis_products(
        rest, index(1, 3), features, *weights, basis, (cut, units), False, True, tile
    )
    other_b = send(narrow_b, swap_core)
    hidden = [
        hidden_units(own, other, features, square, other_square, full_width, tile)
        for own, other in ((own_a, other_a), (own_b, other_b))
    ]

    partial = {
        k: down_products(hidden, down_weight, index(k), cols, 256) for k in (3, 1, 2, 0)
    }
    sums = []
    for part in range(2):
        total = partial[0][part].astype(f32)
        for k in (3, 1, 2):
            got = send(partial[k][part], [((t, d), (t ^ k, d)) for t, d in every])
            total = total + got.astype(f32)
        sums.append(total.astype(bf16))
    far = [
        send(sums[part], [((t, 1 - t // 4), (t ^ 4, part)) for t in range(TP)])
        for part in range(2)
    ]
    crossed = send(
        jnp.where(dp == 0, sums[1], sums[0]), [((t, t // 4), (t, 1 - t // 4)) for t in range(TP)]
    )

    own_features = lax.dynamic_slice(features, (dp * rows, 0), (rows, act))
    embedded = jnp.dot(own_features, action_weight, preferred_element_type=f32)
    inputs_local = (
        (state_hidden.astype(f32)[:, None, :] + embedded.reshape(states, cands, cols))
        .reshape(rows, cols)
        .astype(bf16)
    )
    mine = jnp.where(home, jnp.where(dp == 0, sums[0], sums[1]), crossed).astype(f32)
    summed = mine + jnp.where(dp == 0, far[0], far[1]).astype(f32)
    output_local = (inputs_local.astype(f32) + summed).astype(bf16)

    wide_out = output_local.astype(f32)
    totals = jnp.stack(
        [
            jnp.sum(wide_out * wide_out, axis=1),
            jnp.sum(wide_out * (head_gain * value_weight), axis=1),
        ]
    )
    totals = lax.all_to_all(jnp.broadcast_to(totals, (TP, 2, rows)), "tp", 0, 0)
    totals = jnp.sum(totals, axis=0)
    values = totals[1] * lax.rsqrt(totals[0] / full_width + epsilon)
    return (
        output_local.reshape(states, cands, cols),
        values.reshape(states, cands),
    )


def solution(mesh):
    local = local_blocks if mesh.shape["tp"] == TP and mesh.shape["dp"] == 2 else local_gathered
    return jax.shard_map(
        local,
        mesh=mesh,
        in_specs=(
            P(("rep", "dp"), "tp"),
            P(("rep", "dp"), None),
            P("rep"),
            P("rep"),
            P(None, "tp"),
            P("tp"),
            P("dp", "tp"),
            P("dp", "tp"),
            P("tp", "dp"),
            P("tp"),
            P("tp"),
        ),
        out_specs=(P(("rep", "dp"), None, "tp"), P(("rep", "dp"), None)),
        check_vma=False,
    )
```

```python
import functools
import math

import jax
import jax.numpy as jnp
from jax import lax
from jax.experimental import pallas as pl
from jax.experimental.pallas import tpu as pltpu
from jax.sharding import PartitionSpec as P

epsilon = 1e-05
modulus = 251


def action_features(action_seeds, action_mean, action_spread):
    harmonic = jnp.arange(1, action_mean.shape[0] + 1, dtype=jnp.int32)
    phases = action_seeds[:, :, None] * harmonic % modulus
    angles = phases.astype(jnp.float32) * (2.0 * math.pi / modulus)
    return (action_mean + action_spread * jnp.cos(angles)).astype(jnp.bfloat16)


def head_value(output_rows, head_gain, value_weight):
    wide_out = output_rows.astype(jnp.float32)
    scale = lax.rsqrt(jnp.mean(wide_out * wide_out, axis=1) + epsilon)
    return jnp.sum(wide_out * (head_gain * value_weight), axis=1) * scale


def local_gathered(
    state_hidden,
    action_seeds,
    action_mean,
    action_spread,
    action_weight,
    norm_gain,
    gate_weight,
    up_weight,
    down_weight,
    head_gain,
    value_weight,
):
    state_count, cand_count = action_seeds.shape
    row_count = state_count * cand_count
    local_cols = action_weight.shape[1]
    features = action_features(action_seeds, action_mean, action_spread)
    embedded = jnp.dot(
        features.reshape(row_count, features.shape[2]),
        action_weight,
        preferred_element_type=jnp.float32,
    )
    inputs_local = (
        (
            state_hidden.astype(jnp.float32)[:, None, :]
            + embedded.reshape(state_count, cand_count, local_cols)
        )
        .reshape(row_count, local_cols)
        .astype(jnp.bfloat16)
    )
    gathered, gain_full = (
        lax.all_gather(inputs_local, "tp", axis=1, tiled=True),
        lax.all_gather(norm_gain.astype(jnp.bfloat16), "tp", axis=0, tiled=True).astype(
            norm_gain.dtype
        ),
    )
    scale = lax.rsqrt(
        jnp.mean(jnp.square(gathered.astype(jnp.float32)), axis=1, keepdims=True) + epsilon
    )
    normed = (gathered.astype(jnp.float32) * scale * gain_full).astype(jnp.bfloat16)
    gate_sum = jnp.dot(
        normed,
        lax.all_gather(gate_weight, "dp", axis=0, tiled=True),
        preferred_element_type=jnp.float32,
    )
    up_sum = jnp.dot(
        normed,
        lax.all_gather(up_weight, "dp", axis=0, tiled=True),
        preferred_element_type=jnp.float32,
    )
    hidden = (jax.nn.silu(gate_sum) * up_sum).astype(jnp.bfloat16)
    partial_terms = jnp.dot(
        hidden,
        lax.all_gather(down_weight, "dp", axis=1, tiled=True),
        preferred_element_type=jnp.float32,
    )
    summed_local = lax.psum_scatter(partial_terms, "tp", scatter_dimension=1, tiled=True)
    output_local = (inputs_local.astype(jnp.float32) + summed_local).astype(jnp.bfloat16)
    output_full, head_full, value_full = (
        lax.all_gather(output_local, "tp", axis=1, tiled=True),
        lax.all_gather(head_gain.astype(jnp.bfloat16), "tp", axis=0, tiled=True).astype(
            head_gain.dtype
        ),
        lax.all_gather(value_weight.astype(jnp.bfloat16), "tp", axis=0, tiled=True).astype(
            value_weight.dtype
        ),
    )
    values = head_value(output_full, head_full, value_full)
    return (
        output_local.reshape(state_count, cand_count, local_cols),
        values.reshape(state_count, cand_count),
    )


TP = 8
SMALL = 16
MIB = 1024 * 1024


def send(array, pairs):
    return lax.ppermute(
        array, ("tp", "dp"), [(2 * st + sd, 2 * dt + dd) for (st, sd), (dt, dd) in pairs]
    )


def basis_body(block_count, accumulate, square, narrow, load, *refs):
    refs = list(refs)
    which = refs.pop(0)
    blocks = [refs.pop(0) for _ in range(block_count)]
    features = refs.pop(0) if square else None
    gate_ref, up_ref = refs.pop(0), refs.pop(0)
    before = refs.pop(0) if accumulate else None
    source = refs.pop(0) if load else None
    total = refs.pop(0)
    narrow_ref = refs.pop(0) if narrow else None
    square_ref = refs.pop(0) if square else None
    loaded = refs.pop(0) if load else None
    lhs = refs.pop(0)
    arrived = refs.pop(0) if load else None
    tile, block = pl.program_id(0), pl.program_id(1)

    def copies():
        cols = loaded.shape[1] // load
        for at in range(load):
            begin = pl.multiple_of(which[block_count + at] * cols, 128)
            yield pltpu.make_async_copy(
                source.at[:, pl.ds(begin, cols)],
                loaded.at[:, at * cols : (at + 1) * cols],
                arrived.at[at],
            )

    if load:

        @pl.when((tile == 0) & (block == 0))
        def _():
            for copy in copies():
                copy.start()

    states_at = features.shape[1] - SMALL if square else blocks[0].shape[0] - SMALL

    for index, ref in enumerate(blocks):

        @pl.when((tile == 0) & (block == index))
        def _(index=index, ref=ref):
            gain = ref[states_at + 4 : states_at + 5, :].astype(jnp.float32)
            lhs[index] = (ref[...].astype(jnp.float32) * gain).astype(jnp.bfloat16)
            if square:
                rows = jnp.dot(features[...], ref[...], preferred_element_type=jnp.float32)
                rows = rows.astype(jnp.bfloat16).astype(jnp.float32)
                rows = rows * rows
                part = rows[:, :128]
                for at in range(128, rows.shape[1], 128):
                    part += rows[:, at : at + 128]
                if index == 0:
                    square_ref[...] = part
                else:
                    square_ref[...] += part

    gate = jnp.dot(lhs[block], gate_ref[...], preferred_element_type=jnp.float32)
    up = jnp.dot(lhs[block], up_ref[...], preferred_element_type=jnp.float32)

    def first():
        if accumulate:
            total[0] = before[0] + gate
            total[1] = before[1] + up
        else:
            total[0] = gate
            total[1] = up

    def later():
        total[0] += gate
        total[1] += up

    if block_count == 1:
        first()
    else:
        pl.when(block == 0)(first)
        pl.when(block > 0)(later)
    if narrow:

        @pl.when(block == block_count - 1)
        def _():
            narrow_ref[...] = total[...].astype(jnp.bfloat16)

    if load:

        @pl.when((tile == pl.num_programs(0) - 1) & (block == block_count - 1))
        def _():
            for copy in copies():
                copy.wait()


def basis_products(
    blocks, which, features, gate_weight, up_weight, before, columns, square, narrow, tile, load=None
):
    count = len(blocks)
    m, k = blocks[0].shape
    start, stop = columns
    width = stop - start
    tiles, base = width // tile, start // tile
    whole = lambda *shape: pl.BlockSpec(shape, lambda j, b, s: (0,) * len(shape))
    weight = pl.BlockSpec((k, tile), lambda j, b, s: (s[b], base + j))
    specs, operands = [whole(m, k)] * count, list(blocks)
    if square:
        specs.append(whole(*features.shape))
        operands.append(features)
    specs += [weight, weight]
    operands += [gate_weight, up_weight]
    if before is not None:
        specs.append(pl.BlockSpec((2, m, tile), lambda j, b, s: (0, 0, base + j)))
        operands.append(before)
    if load is not None:
        specs.append(pl.BlockSpec(memory_space=pl.ANY))
        operands.append(load[0])
    part = pl.BlockSpec((2, m, tile), lambda j, b, s: (0, 0, j))
    outs = [jax.ShapeDtypeStruct((2, m, width), jnp.float32)]
    out_specs = [part]
    if narrow:
        outs.append(jax.ShapeDtypeStruct((2, m, width), jnp.bfloat16))
        out_specs.append(part)
    if square:
        outs.append(jax.ShapeDtypeStruct((features.shape[0], 128), jnp.float32))
        out_specs.append(whole(features.shape[0], 128))
    scratch = [pltpu.VMEM((count, m, k), jnp.bfloat16)]
    loads = 0
    if load is not None:
        loads = which.shape[0] - count
        outs.append(jax.ShapeDtypeStruct((load[0].shape[0], loads * load[1]), jnp.bfloat16))
        out_specs.append(pl.BlockSpec(memory_space=pltpu.VMEM))
        scratch.append(pltpu.SemaphoreType.DMA((loads,)))
    return pl.pallas_call(
        functools.partial(basis_body, count, before is not None, square, narrow, loads),
        out_shape=outs,
        grid_spec=pltpu.PrefetchScalarGridSpec(
            num_scalar_prefetch=1,
            grid=(tiles, count),
            in_specs=specs,
            out_specs=out_specs,
            scratch_shapes=scratch,
        ),
        compiler_params=pltpu.CompilerParams(
            dimension_semantics=("arbitrary", "arbitrary"), vmem_limit_bytes=16 * MIB
        ),
        cost_estimate=pl.CostEstimate(
            flops=4 * m * k * width * count,
            bytes_accessed=4 * k * width * count,
            transcendentals=0,
        ),
    )(which, *operands)


def hidden_body(width, own, other, features, square_own, square_other, hidden):
    squares = jnp.sum(square_own[...] + square_other[...], axis=1, keepdims=True)
    scale = lax.rsqrt(squares / width + epsilon)
    basis = (own[...] + other[...].astype(jnp.float32)).astype(jnp.bfloat16)
    gate = scale * jnp.dot(features[...], basis[0], preferred_element_type=jnp.float32)
    up = scale * jnp.dot(features[...], basis[1], preferred_element_type=jnp.float32)
    hidden[...] = (gate / (1.0 + jnp.exp(-gate)) * up).astype(jnp.bfloat16)


def hidden_units(own, other, features, square_own, square_other, width, tile):
    _, m, units = own.shape
    rows = features.shape[0]
    whole = lambda *shape: pl.BlockSpec(shape, lambda j: (0,) * len(shape))
    part = pl.BlockSpec((2, m, tile), lambda j: (0, 0, j))
    return pl.pallas_call(
        functools.partial(hidden_body, width),
        out_shape=jax.ShapeDtypeStruct((rows, units), jnp.bfloat16),
        grid=(units // tile,),
        in_specs=[part, part, whole(rows, m), whole(rows, 128), whole(rows, 128)],
        out_specs=pl.BlockSpec((rows, tile), lambda j: (0, j)),
        compiler_params=pltpu.CompilerParams(vmem_limit_bytes=16 * MIB),
        cost_estimate=pl.CostEstimate(
            flops=4 * m * rows * units, bytes_accessed=12 * m * units, transcendentals=rows * units
        ),
    )(own, other, features, square_own, square_other)


def down_body(places, cols, hidden, weights, outs):
    half = hidden[0].shape[0] // 2
    tile = 512
    for rows, which, block, targets in places:
        low, high = rows[0] * half, rows[-1] * half + half
        for j in range(cols // tile):
            at = block * cols + j * tile
            total = None
            depth_at = 0
            for ref in hidden:
                depth = ref.shape[1]
                term = jnp.dot(
                    ref[low:high, :],
                    weights[which][depth_at : depth_at + depth, at : at + tile],
                    preferred_element_type=jnp.float32,
                )
                total = term if total is None else total + term
                depth_at += depth
            total = total.astype(jnp.bfloat16)
            for index, (out, column) in enumerate(targets):
                to = column + j * tile
                outs[out][:, to : to + tile] = total[index * half : (index + 1) * half]


def down_products(hidden, weights, cols, places, widths, copies=()):
    rows = hidden[0].shape[0]
    depth = weights[0].shape[0]
    flops = sum(len(r) * rows * depth * cols for r, *_ in places)
    vmem = pl.BlockSpec(memory_space=pltpu.VMEM)
    counts = (len(hidden), len(weights), len(copies))

    def body(*refs):
        groups, at = [], 0
        for count in counts:
            groups.append(refs[at : at + count])
            at += count
        outs = refs[at:]
        down_body(places, cols, groups[0], groups[1], outs)
        for source, (_, out) in zip(groups[2], copies):
            outs[out][:, : source.shape[1]] = source[...]

    return pl.pallas_call(
        body,
        out_shape=[jax.ShapeDtypeStruct((rows // 2, width), jnp.bfloat16) for width in widths],
        in_specs=[vmem] * sum(counts),
        out_specs=[vmem] * len(widths),
        compiler_params=pltpu.CompilerParams(vmem_limit_bytes=12 * MIB),
        cost_estimate=pl.CostEstimate(flops=flops // 16, bytes_accessed=0, transcendentals=0),
    )(*hidden, *weights, *[c[0] for c in copies])


def local_blocks(
    state_hidden,
    action_seeds,
    action_mean,
    action_spread,
    action_weight,
    norm_gain,
    gate_weight,
    up_weight,
    down_weight,
    head_gain,
    value_weight,
):
    f32, bf16 = jnp.float32, jnp.bfloat16
    states, cands = action_seeds.shape
    rows = states * cands
    act, cols = action_weight.shape
    half = act // 2
    units = gate_weight.shape[1]
    full_width = gate_weight.shape[0] * 2
    tp, dp = lax.axis_index("tp"), lax.axis_index("dp")
    home = tp // 4 == dp
    place = tp % 4
    every = [(t, d) for t in range(TP) for d in range(2)]
    swap_core = [((t, d), (t, 1 - d)) for t, d in every]

    seeds = jnp.concatenate([action_seeds // 256, action_seeds % 256]).astype(bf16)
    seeds_row = jnp.pad(seeds.reshape(1, -1), ((0, 0), (0, cols - seeds.size)))
    piece = jnp.concatenate(
        [
            lax.dynamic_slice_in_dim(action_weight, dp * half, half, 0),
            state_hidden,
            norm_gain.astype(bf16)[None],
            seeds_row,
            jnp.zeros((SMALL - states - 2, cols), bf16),
        ],
        axis=0,
    )
    first = send(
        piece,
        [((t, t // 4), (t ^ 4, t // 4)) for t in range(TP)]
        + [((t, 1 - t // 4), (t, t // 4)) for t in range(TP)],
    )
    second = send(piece, [((t, 1 - t // 4), (t ^ 4, t // 4)) for t in range(TP)])
    same = jnp.where(home, piece, first)
    other = jnp.where(home, first, second)
    low = jnp.where(dp == 0, same, other)
    high = jnp.where(dp == 0, other, same)
    block = jnp.concatenate(
        [
            low[:half],
            high[:half],
            low[half : half + states],
            high[half : half + states],
            low[half + states : half + states + 1],
            jnp.zeros((SMALL - 2 * states - 1, cols), bf16),
        ]
    )

    near = {k: send(block, [((t, d), (t ^ k, d)) for t, d in every]) for k in (2, 1, 3)}

    all_seeds = jnp.concatenate(
        [part[half + states + 1, : seeds.size].reshape(2, states, cands) for part in (low, high)],
        axis=1,
    ).astype(jnp.int32)
    all_seeds = all_seeds[0] * 256 + all_seeds[1]
    features = action_features(all_seeds, action_mean, action_spread).reshape(2 * rows, act)
    row_state = jnp.arange(2 * rows) // cands
    onehot = (row_state[:, None] == jnp.arange(SMALL)[None]).astype(bf16)
    features = jnp.concatenate([features, onehot], axis=1)

    index = lambda *ks: jnp.stack([place ^ k for k in ks]).astype(jnp.int32)
    gate_weight, up_weight, down_weight = (
        pltpu.with_memory_space_constraint(weight, pltpu.HBM)
        for weight in (gate_weight, up_weight, down_weight)
    )
    weights = (gate_weight, up_weight)
    tile = 512
    load = (down_weight, cols)
    basis, square0, down_first = basis_products(
        [block], index(0, 3, 1), features, *weights, None, (0, units), True, False, tile, load
    )
    basis, square2, down_second = basis_products(
        [near[2]], index(2, 2, 0), features, *weights, basis, (0, units), True, False, tile, load
    )
    cut = units // 2
    rest = [near[1], near[3]]
    own_a, narrow_a, square13 = basis_products(
        rest, index(1, 3), features, *weights, basis, (0, cut), True, True, tile
    )
    square = square0 + square2 + square13
    other_a = send(narrow_a, swap_core)
    other_square = send(square, swap_core)
    own_b, narrow_b = basis_products(
        rest, index(1, 3), features, *weights, basis, (cut, units), False, True, tile
    )
    other_b = send(narrow_b, swap_core)
    hidden = [
        hidden_units(own, other, features, square, other_square, full_width, tile)
        for own, other in ((own_a, other_a), (own_b, other_b))
    ]

    both, lower, upper = (0, 1), (0,), (1,)
    step = lambda array, k: send(array, [((t, d), (t ^ k, d)) for t, d in every])
    x_pair, diagonal_upper = down_products(
        hidden,
        [down_first],
        cols,
        [(both, 0, 0, [(0, 0), (1, 0)]), (lower, 0, 1, [(0, cols)])],
        [2 * cols, cols],
    )
    got_x = step(x_pair, 1)
    (z_pair,) = down_products(
        hidden,
        [down_second],
        cols,
        [(upper, 0, 0, [(0, cols)])],
        [2 * cols],
        [(diagonal_upper, 0)],
    )
    got_z = step(z_pair, 2)
    z_lower, x_upper, own_lower, own_upper = down_products(
        hidden,
        [down_first, down_second],
        cols,
        [(lower, 1, 0, [(0, 0)]), (upper, 0, 1, [(1, 0)]), (both, 1, 1, [(2, 0), (3, 0)])],
        [cols] * 4,
    )
    add = lambda *parts: sum(part.astype(f32) for part in parts).astype(bf16)
    got_lower = step(add(z_lower, got_x[:, :cols]), 2)
    got_upper = step(add(x_upper, got_z[:, :cols]), 1)
    sums = [
        add(own_lower, got_x[:, cols:], got_lower),
        add(own_upper, got_z[:, cols:], got_upper),
    ]
    far = [
        send(sums[part], [((t, 1 - t // 4), (t ^ 4, part)) for t in range(TP)])
        for part in range(2)
    ]
    crossed = send(
        jnp.where(dp == 0, sums[1], sums[0]), [((t, t // 4), (t, 1 - t // 4)) for t in range(TP)]
    )

    own_features = lax.dynamic_slice(features, (dp * rows, 0), (rows, act))
    embedded = jnp.dot(own_features, action_weight, preferred_element_type=f32)
    inputs_local = (
        (state_hidden.astype(f32)[:, None, :] + embedded.reshape(states, cands, cols))
        .reshape(rows, cols)
        .astype(bf16)
    )
    mine = jnp.where(home, jnp.where(dp == 0, sums[0], sums[1]), crossed).astype(f32)
    summed = mine + jnp.where(dp == 0, far[0], far[1]).astype(f32)
    output_local = (inputs_local.astype(f32) + summed).astype(bf16)

    wide_out = output_local.astype(f32)
    totals = jnp.stack(
        [
            jnp.sum(wide_out * wide_out, axis=1),
            jnp.sum(wide_out * (head_gain * value_weight), axis=1),
        ]
    )
    for k in (1, 2, 4):
        totals = totals + step(totals, k)
    values = totals[1] * lax.rsqrt(totals[0] / full_width + epsilon)
    return (
        output_local.reshape(states, cands, cols),
        values.reshape(states, cands),
    )


def solution(mesh):
    local = local_blocks if mesh.shape["tp"] == TP and mesh.shape["dp"] == 2 else local_gathered
    return jax.shard_map(
        local,
        mesh=mesh,
        in_specs=(
            P(("rep", "dp"), "tp"),
            P(("rep", "dp"), None),
            P("rep"),
            P("rep"),
            P(None, "tp"),
            P("tp"),
            P("dp", "tp"),
            P("dp", "tp"),
            P("tp", "dp"),
            P("tp"),
            P("tp"),
        ),
        out_specs=(P(("rep", "dp"), None, "tp"), P(("rep", "dp"), None)),
        check_vma=False,
    )
```

```python
import functools
import math

import jax
import jax.numpy as jnp
from jax import lax
from jax.experimental import pallas as pl
from jax.experimental.pallas import tpu as pltpu
from jax.sharding import PartitionSpec as P

epsilon = 1e-05
modulus = 251


def action_features(action_seeds, action_mean, action_spread):
    harmonic = jnp.arange(1, action_mean.shape[0] + 1, dtype=jnp.int32)
    phases = action_seeds[:, :, None] * harmonic % modulus
    angles = phases.astype(jnp.float32) * (2.0 * math.pi / modulus)
    return (action_mean + action_spread * jnp.cos(angles)).astype(jnp.bfloat16)


def head_value(output_rows, head_gain, value_weight):
    wide_out = output_rows.astype(jnp.float32)
    scale = lax.rsqrt(jnp.mean(wide_out * wide_out, axis=1) + epsilon)
    return jnp.sum(wide_out * (head_gain * value_weight), axis=1) * scale


def local_gathered(
    state_hidden,
    action_seeds,
    action_mean,
    action_spread,
    action_weight,
    norm_gain,
    gate_weight,
    up_weight,
    down_weight,
    head_gain,
    value_weight,
):
    state_count, cand_count = action_seeds.shape
    row_count = state_count * cand_count
    local_cols = action_weight.shape[1]
    features = action_features(action_seeds, action_mean, action_spread)
    embedded = jnp.dot(
        features.reshape(row_count, features.shape[2]),
        action_weight,
        preferred_element_type=jnp.float32,
    )
    inputs_local = (
        (
            state_hidden.astype(jnp.float32)[:, None, :]
            + embedded.reshape(state_count, cand_count, local_cols)
        )
        .reshape(row_count, local_cols)
        .astype(jnp.bfloat16)
    )
    gathered, gain_full = (
        lax.all_gather(inputs_local, "tp", axis=1, tiled=True),
        lax.all_gather(norm_gain.astype(jnp.bfloat16), "tp", axis=0, tiled=True).astype(
            norm_gain.dtype
        ),
    )
    scale = lax.rsqrt(
        jnp.mean(jnp.square(gathered.astype(jnp.float32)), axis=1, keepdims=True) + epsilon
    )
    normed = (gathered.astype(jnp.float32) * scale * gain_full).astype(jnp.bfloat16)
    gate_sum = jnp.dot(
        normed,
        lax.all_gather(gate_weight, "dp", axis=0, tiled=True),
        preferred_element_type=jnp.float32,
    )
    up_sum = jnp.dot(
        normed,
        lax.all_gather(up_weight, "dp", axis=0, tiled=True),
        preferred_element_type=jnp.float32,
    )
    hidden = (jax.nn.silu(gate_sum) * up_sum).astype(jnp.bfloat16)
    partial_terms = jnp.dot(
        hidden,
        lax.all_gather(down_weight, "dp", axis=1, tiled=True),
        preferred_element_type=jnp.float32,
    )
    summed_local = lax.psum_scatter(partial_terms, "tp", scatter_dimension=1, tiled=True)
    output_local = (inputs_local.astype(jnp.float32) + summed_local).astype(jnp.bfloat16)
    output_full, head_full, value_full = (
        lax.all_gather(output_local, "tp", axis=1, tiled=True),
        lax.all_gather(head_gain.astype(jnp.bfloat16), "tp", axis=0, tiled=True).astype(
            head_gain.dtype
        ),
        lax.all_gather(value_weight.astype(jnp.bfloat16), "tp", axis=0, tiled=True).astype(
            value_weight.dtype
        ),
    )
    values = head_value(output_full, head_full, value_full)
    return (
        output_local.reshape(state_count, cand_count, local_cols),
        values.reshape(state_count, cand_count),
    )


TP = 8
SMALL = 16
MIB = 1024 * 1024


def send(array, pairs):
    return lax.ppermute(
        array, ("tp", "dp"), [(2 * st + sd, 2 * dt + dd) for (st, sd), (dt, dd) in pairs]
    )


SPLIT = 4


def copies_of(which, loads, sources, targets, arrived):
    made = []
    for at, (kind, size) in enumerate(loads):
        source, target = sources[at], targets[at]
        part = target.shape[0] // SPLIT
        for cut in range(SPLIT):
            rows = pl.ds(cut * part, part)
            if kind == "rows":
                begin = pl.multiple_of(which[at] * size + cut * part, 16)
                view = source.at[pl.ds(begin, part), :]
            else:
                view = source.at[rows, pl.ds(pl.multiple_of(which[at] * size, 128), size)]
            made.append(
                pltpu.make_async_copy(view, target.at[rows, :], arrived.at[at * SPLIT + cut])
            )
    return made


def stage(which, loads, ins, outs, compute, scratch=(), limit=6, flops=0):
    vmem = pl.BlockSpec(memory_space=pltpu.VMEM)
    n, count = len(loads), len(ins)
    kinds = [(kind, size) for kind, size, _ in loads]
    shapes = list(outs)
    for kind, size, array in loads:
        shape = (size, array.shape[1]) if kind == "rows" else (array.shape[0], size)
        shapes.append(jax.ShapeDtypeStruct(shape, array.dtype))

    def body(which_ref, *refs):
        sources, inputs = refs[:n], refs[n : n + count]
        results = refs[n + count : n + count + len(outs)]
        targets = refs[n + count + len(outs) : n + count + len(shapes)]
        extra = refs[n + count + len(shapes) :]
        made = copies_of(which_ref, kinds, sources, targets, extra[0]) if n else []
        for copy in made:
            copy.start()
        if compute is not None:
            compute(inputs, results, extra[1:] if n else extra)
        for copy in made:
            copy.wait()

    loaded = sum(2 * math.prod(shape.shape) for shape in shapes[len(outs) :])
    return pl.pallas_call(
        body,
        out_shape=shapes,
        in_specs=[pl.BlockSpec(memory_space=pltpu.SMEM)]
        + [pl.BlockSpec(memory_space=pl.ANY)] * n
        + [vmem] * count,
        out_specs=[vmem] * len(shapes),
        scratch_shapes=([pltpu.SemaphoreType.DMA((n * SPLIT,))] if n else []) + list(scratch),
        compiler_params=pltpu.CompilerParams(vmem_limit_bytes=limit * MIB),
        cost_estimate=pl.CostEstimate(
            flops=flops, bytes_accessed=loaded, transcendentals=0
        ),
    )(which, *[array for _, _, array in loads], *ins)


def basis_stage(which, loads, blocks, held, before, columns, features, squared, narrow):
    m, k = blocks[0].shape
    start, stop = columns
    width = stop - start
    tile = 512
    count = len(blocks)
    ins = list(blocks) + [part for pair in held for part in pair]
    if before is not None:
        ins.append(before)
    ins += list(squared) + ([features] if squared else [])
    outs = [jax.ShapeDtypeStruct((2, m, width), jnp.float32)]
    if narrow:
        outs.append(jax.ShapeDtypeStruct((2, m, width), jnp.bfloat16))
    if squared:
        outs.append(jax.ShapeDtypeStruct((features.shape[0], 128), jnp.float32))

    def compute(inputs, results, extra):
        refs = list(inputs)
        lhs = extra[0]
        rows = [refs.pop(0) for _ in range(count)]
        weights = [(refs.pop(0), refs.pop(0)) for _ in range(count)]
        old = refs.pop(0) if before is not None else None
        for index, ref in enumerate(rows):
            gain = ref[m - SMALL + 4 : m - SMALL + 5, :].astype(jnp.float32)
            lhs[index] = (ref[...].astype(jnp.float32) * gain).astype(jnp.bfloat16)

        @pl.loop(0, width // tile)
        def _(j):
            at = pl.ds(pl.multiple_of(start + j * tile, tile), tile)
            to = pl.ds(pl.multiple_of(j * tile, tile), tile)
            for side in range(2):
                total = old[side, :, at] if old is not None else None
                for index in range(count):
                    term = jnp.dot(
                        lhs[index],
                        weights[index][side][:, at],
                        preferred_element_type=jnp.float32,
                    )
                    total = term if total is None else total + term
                results[0][side, :, to] = total
                if narrow:
                    results[1][side, :, to] = total.astype(jnp.bfloat16)

        if squared:
            feature_rows = refs.pop()
            part = None
            for ref in refs:
                wide = jnp.dot(feature_rows[...], ref[...], preferred_element_type=jnp.float32)
                wide = wide.astype(jnp.bfloat16).astype(jnp.float32)
                wide = wide * wide
                for at in range(0, k, 128):
                    piece = wide[:, at : at + 128]
                    part = piece if part is None else part + piece
            results[-1][...] = part

    return stage(
        which,
        loads,
        ins,
        outs,
        compute,
        [pltpu.VMEM((count, m, k), jnp.bfloat16)],
        flops=4 * m * k * width * count,
    )


def hidden_stage(which, loads, own, other, features, square_own, square_other, width):
    _, m, units = own.shape
    rows = features.shape[0]
    tile = 512

    def compute(inputs, results, extra):
        own, other, features, square_own, square_other = inputs
        squares = jnp.sum(square_own[...] + square_other[...], axis=1, keepdims=True)
        scale = lax.rsqrt(squares / width + epsilon)

        @pl.loop(0, units // tile)
        def _(j):
            at = pl.ds(pl.multiple_of(j * tile, tile), tile)
            sums = []
            for side in range(2):
                basis = own[side, :, at] + other[side, :, at].astype(jnp.float32)
                sums.append(
                    scale
                    * jnp.dot(
                        features[...],
                        basis.astype(jnp.bfloat16),
                        preferred_element_type=jnp.float32,
                    )
                )
            gate, up = sums
            results[0][:, at] = (gate / (1.0 + jnp.exp(-gate)) * up).astype(jnp.bfloat16)

    return stage(
        which,
        loads,
        [own, other, features, square_own, square_other],
        [jax.ShapeDtypeStruct((rows, units), jnp.bfloat16)],
        compute,
        flops=4 * m * rows * units,
    )


def down_body(places, cols, hidden, weights, outs):
    half = hidden[0].shape[0] // 2
    tile = 512
    for rows, which, targets in places:
        low, high = rows[0] * half, rows[-1] * half + half
        for j in range(cols // tile):
            at = j * tile
            total = None
            depth_at = 0
            for ref in hidden:
                depth = ref.shape[1]
                term = jnp.dot(
                    ref[low:high, :],
                    weights[which][depth_at : depth_at + depth, at : at + tile],
                    preferred_element_type=jnp.float32,
                )
                total = term if total is None else total + term
                depth_at += depth
            total = total.astype(jnp.bfloat16)
            for index, (out, column) in enumerate(targets):
                to = column + j * tile
                outs[out][:, to : to + tile] = total[index * half : (index + 1) * half]


def down_products(hidden, weights, cols, places, widths, copies=()):
    rows = hidden[0].shape[0]
    depth = weights[0].shape[0]
    flops = sum(len(r) * rows * depth * cols for r, *_ in places)
    vmem = pl.BlockSpec(memory_space=pltpu.VMEM)
    counts = (len(hidden), len(weights), len(copies))

    def body(*refs):
        groups, at = [], 0
        for count in counts:
            groups.append(refs[at : at + count])
            at += count
        outs = refs[at:]
        down_body(places, cols, groups[0], groups[1], outs)
        for source, (_, out) in zip(groups[2], copies):
            outs[out][:, : source.shape[1]] = source[...]

    return pl.pallas_call(
        body,
        out_shape=[jax.ShapeDtypeStruct((rows // 2, width), jnp.bfloat16) for width in widths],
        in_specs=[vmem] * sum(counts),
        out_specs=[vmem] * len(widths),
        compiler_params=pltpu.CompilerParams(vmem_limit_bytes=6 * MIB),
        cost_estimate=pl.CostEstimate(flops=flops // 16, bytes_accessed=0, transcendentals=0),
    )(*hidden, *weights, *[c[0] for c in copies])


def local_blocks(
    state_hidden,
    action_seeds,
    action_mean,
    action_spread,
    action_weight,
    norm_gain,
    gate_weight,
    up_weight,
    down_weight,
    head_gain,
    value_weight,
):
    f32, bf16 = jnp.float32, jnp.bfloat16
    states, cands = action_seeds.shape
    rows = states * cands
    act, cols = action_weight.shape
    half = act // 2
    units = gate_weight.shape[1]
    full_width = gate_weight.shape[0] * 2
    tp, dp = lax.axis_index("tp"), lax.axis_index("dp")
    home = tp // 4 == dp
    place = tp % 4
    every = [(t, d) for t in range(TP) for d in range(2)]
    swap_core = [((t, d), (t, 1 - d)) for t, d in every]

    head = head_gain * value_weight
    seeds = jnp.concatenate([action_seeds // 256, action_seeds % 256]).astype(bf16)
    seeds_row = jnp.pad(seeds.reshape(1, -1), ((0, 0), (0, cols - seeds.size)))
    small = jnp.concatenate([state_hidden, seeds_row, jnp.zeros((5, cols), bf16)])
    small, head = lax.optimization_barrier((small, head))
    other_small = send(small, swap_core)
    low = jnp.where(dp == 0, small, other_small)
    high = jnp.where(dp == 0, other_small, small)
    own_block = jnp.concatenate(
        [
            action_weight,
            low[:states],
            high[:states],
            norm_gain.astype(bf16)[None],
            jnp.zeros((SMALL - 2 * states - 1, cols), bf16),
        ]
    )

    far_block = send(own_block, [((t, t // 4), (t ^ 4, t // 4)) for t in range(TP)])
    near_home = {
        k: send(own_block, [((t, t // 4), (t ^ k, t // 4)) for t in range(TP)]) for k in (2, 1, 3)
    }
    block = jnp.where(home, own_block, far_block)
    near = {}
    for k in (2, 1, 3):
        got = send(block, [((t, 1 - t // 4), (t ^ k, 1 - t // 4)) for t in range(TP)])
        near[k] = jnp.where(home, near_home[k], got)

    all_seeds = jnp.concatenate(
        [part[states, : seeds.size].reshape(2, states, cands) for part in (low, high)],
        axis=1,
    ).astype(jnp.int32)
    all_seeds = all_seeds[0] * 256 + all_seeds[1]
    features = action_features(all_seeds, action_mean, action_spread).reshape(2 * rows, act)
    row_state = jnp.arange(2 * rows) // cands
    onehot = (row_state[:, None] == jnp.arange(SMALL)[None]).astype(bf16)
    features = jnp.concatenate([features, onehot], axis=1)
    own_features = lax.dynamic_slice(features, (dp * rows, 0), (rows, act))
    embedded = jnp.dot(own_features, action_weight, preferred_element_type=f32)
    inputs_local = (
        (state_hidden.astype(f32)[:, None, :] + embedded.reshape(states, cands, cols))
        .reshape(rows, cols)
        .astype(bf16)
    )

    gate_weight, up_weight, down_weight = (
        pltpu.with_memory_space_constraint(weight, pltpu.HBM)
        for weight in (gate_weight, up_weight, down_weight)
    )
    index = lambda *ks: jnp.stack([place ^ k for k in ks]).astype(jnp.int32)
    pair = [("rows", cols, gate_weight), ("rows", cols, up_weight)]
    column = [("cols", cols, down_weight)]
    held = stage(index(0, 0), pair, [], [], None)
    basis, *held = basis_stage(
        index(2, 2), pair, [block], [held], None, (0, units), features, [], False
    )
    basis, *held = basis_stage(
        index(1, 1), pair, [near[2]], [held], basis, (0, units), features, [], False
    )
    basis, square, *held = basis_stage(
        index(3, 3),
        pair,
        [near[1]],
        [held],
        basis,
        (0, units),
        features,
        [block, near[2], near[1]],
        False,
    )
    cut = units // 2
    none = index(0)
    own_a, narrow_a, square_last = basis_stage(
        none, [], [near[3]], [held], basis, (0, cut), features, [near[3]], True
    )
    other_a = send(narrow_a, swap_core)
    square = square + square_last
    other_square = send(square, swap_core)
    own_b, narrow_b = basis_stage(
        none, [], [near[3]], [held], basis, (cut, units), features, [], True
    )
    other_b = send(narrow_b, swap_core)
    down_first = stage(index(3, 1), column * 2, [], [], None)
    hidden_a, down_z = hidden_stage(
        index(2), column, own_a, other_a, features, square, other_square, full_width
    )
    hidden_b, down_own = hidden_stage(
        index(0), column, own_b, other_b, features, square, other_square, full_width
    )
    hidden_a, inputs_local, head = lax.optimization_barrier((hidden_a, inputs_local, head))
    hidden = [hidden_a, hidden_b]

    both, lower, upper = (0, 1), (0,), (1,)
    step = lambda array, k: send(array, [((t, d), (t ^ k, d)) for t, d in every])
    x_pair, diagonal_upper = down_products(
        hidden,
        down_first,
        cols,
        [(both, 0, [(0, 0), (1, 0)]), (lower, 1, [(0, cols)])],
        [2 * cols, cols],
    )
    got_x = step(x_pair, 1)
    (z_pair,) = down_products(
        hidden,
        [down_z],
        cols,
        [(upper, 0, [(0, cols)])],
        [2 * cols],
        [(diagonal_upper, 0)],
    )
    got_z = step(z_pair, 2)
    z_lower, x_upper, own_lower, own_upper = down_products(
        hidden,
        [down_z, down_first[1], down_own],
        cols,
        [(lower, 0, [(0, 0)]), (upper, 1, [(1, 0)]), (both, 2, [(2, 0), (3, 0)])],
        [cols] * 4,
    )
    add = lambda *parts: sum(part.astype(f32) for part in parts).astype(bf16)
    got_lower = step(add(z_lower, got_x[:, :cols]), 2)
    got_upper = step(add(x_upper, got_z[:, :cols]), 1)
    sums = [
        add(own_lower, got_x[:, cols:], got_lower),
        add(own_upper, got_z[:, cols:], got_upper),
    ]
    swapped = send(jnp.where(dp == 0, sums[1], sums[0]), swap_core)
    stays = jnp.where(dp == 0, sums[0], sums[1])
    got_far = step(jnp.where(home, swapped, stays), 4)
    kept = jnp.where(home, stays, swapped)

    summed = kept.astype(f32) + got_far.astype(f32)
    output_local = (inputs_local.astype(f32) + summed).astype(bf16)

    wide_out = output_local.astype(f32)
    totals = jnp.stack(
        [
            jnp.sum(wide_out * wide_out, axis=1),
            jnp.sum(wide_out * head, axis=1),
        ]
    )
    for k in (1, 2, 4):
        totals = totals + step(totals, k)
    values = totals[1] * lax.rsqrt(totals[0] / full_width + epsilon)
    return (
        output_local.reshape(states, cands, cols),
        values.reshape(states, cands),
    )


def solution(mesh):
    local = local_blocks if mesh.shape["tp"] == TP and mesh.shape["dp"] == 2 else local_gathered
    return jax.shard_map(
        local,
        mesh=mesh,
        in_specs=(
            P(("rep", "dp"), "tp"),
            P(("rep", "dp"), None),
            P("rep"),
            P("rep"),
            P(None, "tp"),
            P("tp"),
            P("dp", "tp"),
            P("dp", "tp"),
            P("tp", "dp"),
            P("tp"),
            P("tp"),
        ),
        out_specs=(P(("rep", "dp"), None, "tp"), P(("rep", "dp"), None)),
        check_vma=False,
    )
```

```python
import functools
import math

import jax
import jax.numpy as jnp
from jax import lax
from jax.experimental import pallas as pl
from jax.experimental.pallas import tpu as pltpu
from jax.sharding import PartitionSpec as P

epsilon = 1e-05
modulus = 251


def action_features(action_seeds, action_mean, action_spread):
    harmonic = jnp.arange(1, action_mean.shape[0] + 1, dtype=jnp.int32)
    phases = action_seeds[:, :, None] * harmonic % modulus
    angles = phases.astype(jnp.float32) * (2.0 * math.pi / modulus)
    return (action_mean + action_spread * jnp.cos(angles)).astype(jnp.bfloat16)


def head_value(output_rows, head_gain, value_weight):
    wide_out = output_rows.astype(jnp.float32)
    scale = lax.rsqrt(jnp.mean(wide_out * wide_out, axis=1) + epsilon)
    return jnp.sum(wide_out * (head_gain * value_weight), axis=1) * scale


def local_gathered(
    state_hidden,
    action_seeds,
    action_mean,
    action_spread,
    action_weight,
    norm_gain,
    gate_weight,
    up_weight,
    down_weight,
    head_gain,
    value_weight,
):
    state_count, cand_count = action_seeds.shape
    row_count = state_count * cand_count
    local_cols = action_weight.shape[1]
    features = action_features(action_seeds, action_mean, action_spread)
    embedded = jnp.dot(
        features.reshape(row_count, features.shape[2]),
        action_weight,
        preferred_element_type=jnp.float32,
    )
    inputs_local = (
        (
            state_hidden.astype(jnp.float32)[:, None, :]
            + embedded.reshape(state_count, cand_count, local_cols)
        )
        .reshape(row_count, local_cols)
        .astype(jnp.bfloat16)
    )
    gathered, gain_full = (
        lax.all_gather(inputs_local, "tp", axis=1, tiled=True),
        lax.all_gather(norm_gain.astype(jnp.bfloat16), "tp", axis=0, tiled=True).astype(
            norm_gain.dtype
        ),
    )
    scale = lax.rsqrt(
        jnp.mean(jnp.square(gathered.astype(jnp.float32)), axis=1, keepdims=True) + epsilon
    )
    normed = (gathered.astype(jnp.float32) * scale * gain_full).astype(jnp.bfloat16)
    gate_sum = jnp.dot(
        normed,
        lax.all_gather(gate_weight, "dp", axis=0, tiled=True),
        preferred_element_type=jnp.float32,
    )
    up_sum = jnp.dot(
        normed,
        lax.all_gather(up_weight, "dp", axis=0, tiled=True),
        preferred_element_type=jnp.float32,
    )
    hidden = (jax.nn.silu(gate_sum) * up_sum).astype(jnp.bfloat16)
    partial_terms = jnp.dot(
        hidden,
        lax.all_gather(down_weight, "dp", axis=1, tiled=True),
        preferred_element_type=jnp.float32,
    )
    summed_local = lax.psum_scatter(partial_terms, "tp", scatter_dimension=1, tiled=True)
    output_local = (inputs_local.astype(jnp.float32) + summed_local).astype(jnp.bfloat16)
    output_full, head_full, value_full = (
        lax.all_gather(output_local, "tp", axis=1, tiled=True),
        lax.all_gather(head_gain.astype(jnp.bfloat16), "tp", axis=0, tiled=True).astype(
            head_gain.dtype
        ),
        lax.all_gather(value_weight.astype(jnp.bfloat16), "tp", axis=0, tiled=True).astype(
            value_weight.dtype
        ),
    )
    values = head_value(output_full, head_full, value_full)
    return (
        output_local.reshape(state_count, cand_count, local_cols),
        values.reshape(state_count, cand_count),
    )


TP = 8
SMALL = 16
MIB = 1024 * 1024


def send(array, pairs):
    return lax.ppermute(
        array, ("tp", "dp"), [(2 * st + sd, 2 * dt + dd) for (st, sd), (dt, dd) in pairs]
    )


SPLIT = 4


def copies_of(which, loads, sources, targets, arrived):
    made = []
    for at, (kind, size, place) in enumerate(loads):
        source, target = sources[at], targets[at]
        part = target.shape[0] // SPLIT
        for cut in range(SPLIT):
            rows = pl.ds(cut * part, part)
            if kind == "rows":
                begin = pl.multiple_of(which[place] * size + cut * part, 16)
                view = source.at[pl.ds(begin, part), :]
            else:
                view = source.at[rows, pl.ds(pl.multiple_of(which[place] * size, 128), size)]
            made.append(
                pltpu.make_async_copy(view, target.at[rows, :], arrived.at[at * SPLIT + cut])
            )
    return made


def stage(which, loads, ins, outs, compute, scratch=(), limit=6, flops=0):
    vmem = pl.BlockSpec(memory_space=pltpu.VMEM)
    n, count = len(loads), len(ins)
    kinds = [load[:3] for load in loads]
    shapes = list(outs)
    for kind, size, _, array in loads:
        shape = (size, array.shape[1]) if kind == "rows" else (array.shape[0], size)
        shapes.append(jax.ShapeDtypeStruct(shape, array.dtype))

    def body(which_ref, *refs):
        sources, inputs = refs[:n], refs[n : n + count]
        results = refs[n + count : n + count + len(outs)]
        targets = refs[n + count + len(outs) : n + count + len(shapes)]
        extra = refs[n + count + len(shapes) :]
        made = copies_of(which_ref, kinds, sources, targets, extra[0]) if n else []
        for copy in made:
            copy.start()
        if compute is not None:
            compute(inputs, results, extra[1:] if n else extra)
        for copy in made:
            copy.wait()

    loaded = sum(2 * math.prod(shape.shape) for shape in shapes[len(outs) :])
    return pl.pallas_call(
        body,
        out_shape=shapes,
        in_specs=[pl.BlockSpec(memory_space=pltpu.SMEM)]
        + [pl.BlockSpec(memory_space=pl.ANY)] * n
        + [vmem] * count,
        out_specs=[vmem] * len(shapes),
        scratch_shapes=([pltpu.SemaphoreType.DMA((n * SPLIT,))] if n else []) + list(scratch),
        compiler_params=pltpu.CompilerParams(vmem_limit_bytes=limit * MIB),
        cost_estimate=pl.CostEstimate(
            flops=flops, bytes_accessed=loaded, transcendentals=0
        ),
    )(which, *[load[3] for load in loads], *ins)


def basis_stage(which, loads, blocks, held, before, columns, features, squared, narrow):
    m, k = blocks[0].shape
    start, stop = columns
    width = stop - start
    tile = 512
    count = len(blocks)
    ins = list(blocks) + [part for pair in held for part in pair]
    if before is not None:
        ins.append(before)
    ins += list(squared) + ([features] if squared else [])
    outs = [jax.ShapeDtypeStruct((2, m, width), jnp.float32)]
    if narrow:
        outs.append(jax.ShapeDtypeStruct((2, m, width), jnp.bfloat16))
    if squared:
        outs.append(jax.ShapeDtypeStruct((features.shape[0], 128), jnp.float32))

    def compute(inputs, results, extra):
        refs = list(inputs)
        lhs = extra[0]
        rows = [refs.pop(0) for _ in range(count)]
        weights = [(refs.pop(0), refs.pop(0)) for _ in range(count)]
        old = refs.pop(0) if before is not None else None
        for index, ref in enumerate(rows):
            gain = ref[m - SMALL + 4 : m - SMALL + 5, :].astype(jnp.float32)
            lhs[index] = (ref[...].astype(jnp.float32) * gain).astype(jnp.bfloat16)

        @pl.loop(0, width // tile)
        def _(j):
            at = pl.ds(pl.multiple_of(start + j * tile, tile), tile)
            to = pl.ds(pl.multiple_of(j * tile, tile), tile)
            for side in range(2):
                total = old[side, :, at] if old is not None else None
                for index in range(count):
                    term = jnp.dot(
                        lhs[index],
                        weights[index][side][:, at],
                        preferred_element_type=jnp.float32,
                    )
                    total = term if total is None else total + term
                results[0][side, :, to] = total
                if narrow:
                    results[1][side, :, to] = total.astype(jnp.bfloat16)

        if squared:
            feature_rows = refs.pop()
            part = None
            for ref in refs:
                wide = jnp.dot(feature_rows[...], ref[...], preferred_element_type=jnp.float32)
                wide = wide.astype(jnp.bfloat16).astype(jnp.float32)
                wide = wide * wide
                for at in range(0, k, 128):
                    piece = wide[:, at : at + 128]
                    part = piece if part is None else part + piece
            results[-1][...] = part

    return stage(
        which,
        loads,
        ins,
        outs,
        compute,
        [pltpu.VMEM((count, m, k), jnp.bfloat16)],
        flops=4 * m * k * width * count,
    )


def hidden_stage(which, loads, own, other, features, square_own, square_other, width):
    _, m, units = own.shape
    rows = features.shape[0]
    tile = 512

    def compute(inputs, results, extra):
        own, other, features, square_own, square_other = inputs
        squares = jnp.sum(square_own[...] + square_other[...], axis=1, keepdims=True)
        scale = lax.rsqrt(squares / width + epsilon)

        @pl.loop(0, units // tile)
        def _(j):
            at = pl.ds(pl.multiple_of(j * tile, tile), tile)
            sums = []
            for side in range(2):
                basis = own[side, :, at] + other[side, :, at].astype(jnp.float32)
                sums.append(
                    scale
                    * jnp.dot(
                        features[...],
                        basis.astype(jnp.bfloat16),
                        preferred_element_type=jnp.float32,
                    )
                )
            gate, up = sums
            results[0][:, at] = (gate / (1.0 + jnp.exp(-gate)) * up).astype(jnp.bfloat16)

    return stage(
        which,
        loads,
        [own, other, features, square_own, square_other],
        [jax.ShapeDtypeStruct((rows, units), jnp.bfloat16)],
        compute,
        flops=4 * m * rows * units,
    )


def down_body(places, cols, hidden, weights, outs):
    half = hidden[0].shape[0] // 2
    tile = 512
    for rows, which, targets in places:
        low, high = rows[0] * half, rows[-1] * half + half
        for j in range(cols // tile):
            at = j * tile
            total = None
            depth_at = 0
            for ref in hidden:
                depth = ref.shape[1]
                term = jnp.dot(
                    ref[low:high, :],
                    weights[which][depth_at : depth_at + depth, at : at + tile],
                    preferred_element_type=jnp.float32,
                )
                total = term if total is None else total + term
                depth_at += depth
            total = total.astype(jnp.bfloat16)
            for index, (out, column) in enumerate(targets):
                to = column + j * tile
                outs[out][:, to : to + tile] = total[index * half : (index + 1) * half]


def down_products(hidden, weights, cols, places, widths, copies=()):
    rows = hidden[0].shape[0]
    depth = weights[0].shape[0]
    flops = sum(len(r) * rows * depth * cols for r, *_ in places)
    vmem = pl.BlockSpec(memory_space=pltpu.VMEM)
    counts = (len(hidden), len(weights), len(copies))

    def body(*refs):
        groups, at = [], 0
        for count in counts:
            groups.append(refs[at : at + count])
            at += count
        outs = refs[at:]
        down_body(places, cols, groups[0], groups[1], outs)
        for source, (_, out) in zip(groups[2], copies):
            outs[out][:, : source.shape[1]] = source[...]

    return pl.pallas_call(
        body,
        out_shape=[jax.ShapeDtypeStruct((rows // 2, width), jnp.bfloat16) for width in widths],
        in_specs=[vmem] * sum(counts),
        out_specs=[vmem] * len(widths),
        compiler_params=pltpu.CompilerParams(vmem_limit_bytes=6 * MIB),
        cost_estimate=pl.CostEstimate(flops=flops // 16, bytes_accessed=0, transcendentals=0),
    )(*hidden, *weights, *[c[0] for c in copies])


def piece_body(flags, weight, states, gain, seeds, piece, rows):
    half = weight.shape[0] // 2
    count = states.shape[0]
    piece[:half, :] = weight[pl.ds(pl.multiple_of(flags[4] * half, 16), half), :]
    rows[...] = jnp.zeros_like(rows)
    rows[:count, :] = states[...].astype(jnp.float32)
    rows[count : count + 1, :] = gain[...].reshape(1, -1)
    high = lax.shift_right_logical(seeds[...], 8)
    low = seeds[...] - high * 256
    width = seeds.shape[1]
    rows[count + 1 : 2 * count + 1, :width] = high.astype(jnp.float32)
    rows[2 * count + 1 : 3 * count + 1, :width] = low.astype(jnp.float32)
    piece[half:, :] = rows[...].astype(jnp.bfloat16)


def block_body(count, cands, flags, piece, first, second, weight, states, mean, spread, gain, value,
               block, features, inputs, head, rows):
    f32, bf16 = jnp.float32, jnp.bfloat16
    half = weight.shape[0] // 2
    act = weight.shape[0]
    lower, home = flags[4] == 0, flags[5] == 1
    same = jnp.where(home, piece[...], first[...])
    other = jnp.where(home, first[...], second[...])
    low = jnp.where(lower, same, other)
    high = jnp.where(lower, other, same)
    block[:half, :] = low[:half]
    block[half:act, :] = high[:half]
    parts = [low[half:].astype(f32), high[half:].astype(f32)]
    rows[...] = jnp.zeros_like(rows)
    for index, part in enumerate(parts):
        rows[index * count : (index + 1) * count, :] = part[:count]
    rows[2 * count : 2 * count + 1, :] = parts[0][count : count + 1]
    block[act:, :] = rows[...].astype(bf16)

    harmonic = (lax.broadcasted_iota(jnp.int32, (cands, act), 1) + 1).astype(f32)
    diagonal = lax.broadcasted_iota(jnp.int32, (cands, cands), 0) == lax.broadcasted_iota(
        jnp.int32, (cands, cands), 1
    )
    states_at = lax.broadcasted_iota(jnp.int32, (cands, SMALL), 1)
    made = []
    for state in range(2 * count):
        part, at = parts[state // count], state % count
        seed = (
            part[count + 1 + at : count + 2 + at, :cands] * 256.0
            + part[2 * count + 1 + at : 2 * count + 2 + at, :cands]
        )
        column = jnp.sum(jnp.where(diagonal, seed, 0.0), axis=1, keepdims=True)
        product = column * harmonic
        rest = product - modulus * jnp.floor(product * (1.0 / modulus))
        rest = jnp.where(rest < 0.0, rest + modulus, rest)
        rest = jnp.where(rest >= modulus, rest - modulus, rest)
        wave = jnp.cos(rest * (2.0 * math.pi / modulus))
        value_rows = (mean[...].reshape(1, -1) + spread[...].reshape(1, -1) * wave).astype(bf16)
        made.append(value_rows)
        to = slice(state * cands, (state + 1) * cands)
        features[to, :act] = value_rows
        features[to, act:] = (states_at == state).astype(f32).astype(bf16)
    for at in range(count):
        own = jnp.where(lower, made[at], made[count + at])
        wide = jnp.dot(own, weight[...], preferred_element_type=f32)
        wide = wide + states[at : at + 1, :].astype(f32)
        inputs[at * cands : (at + 1) * cands, :] = wide.astype(bf16)
    head[...] = (gain[...] * value[...]).reshape(1, -1)


def whole_call(body, outs, scratch, after, *operands):
    whole = lambda array: pl.BlockSpec(array.shape, lambda i: (0,) * len(array.shape))
    count = len(after)
    return pl.pallas_call(
        lambda *refs: body(refs[count], *refs[count + 1 :]),
        out_shape=outs,
        grid=(1,),
        in_specs=[pl.BlockSpec(memory_space=pl.ANY)] * count
        + [pl.BlockSpec(memory_space=pltpu.SMEM)]
        + [whole(array) for array in operands[1:]],
        out_specs=[whole(array) for array in outs],
        scratch_shapes=scratch,
        compiler_params=pltpu.CompilerParams(vmem_limit_bytes=6 * MIB),
        cost_estimate=pl.CostEstimate(flops=1000000, bytes_accessed=1000000, transcendentals=0),
    )(*after, *operands)


def local_blocks(
    state_hidden,
    action_seeds,
    action_mean,
    action_spread,
    action_weight,
    norm_gain,
    gate_weight,
    up_weight,
    down_weight,
    head_gain,
    value_weight,
):
    f32, bf16 = jnp.float32, jnp.bfloat16
    states, cands = action_seeds.shape
    rows = states * cands
    act, cols = action_weight.shape
    half = act // 2
    units = gate_weight.shape[1]
    full_width = gate_weight.shape[0] * 2
    tp, dp = lax.axis_index("tp"), lax.axis_index("dp")
    home = tp // 4 == dp
    place = tp % 4
    every = [(t, d) for t in range(TP) for d in range(2)]
    swap_core = [((t, d), (t, 1 - d)) for t, d in every]

    flags = jnp.stack([place, place ^ 1, place ^ 2, place ^ 3, dp, home.astype(jnp.int32)])
    flags = flags.astype(jnp.int32)
    out = jax.ShapeDtypeStruct
    (piece,) = whole_call(
        piece_body,
        [out((half + SMALL, cols), bf16)],
        [pltpu.VMEM((SMALL, cols), f32)],
        [],
        flags,
        *[
            pltpu.with_memory_space_constraint(array, pltpu.HBM)
            for array in (action_weight, state_hidden, norm_gain, action_seeds)
        ],
    )

    first = send(
        piece,
        [((t, t // 4), (t ^ 4, t // 4)) for t in range(TP)]
        + [((t, 1 - t // 4), (t, t // 4)) for t in range(TP)],
    )
    second = send(piece, [((t, 1 - t // 4), (t ^ 4, t // 4)) for t in range(TP)])

    gate_weight, up_weight, down_weight = (
        pltpu.with_memory_space_constraint(weight, pltpu.HBM)
        for weight in (gate_weight, up_weight, down_weight)
    )
    pair = lambda k: [("rows", cols, k, gate_weight), ("rows", cols, k, up_weight)]
    column = lambda k: ("cols", cols, k, down_weight)
    held = stage(flags, pair(0), [], [], None)

    block, features, inputs_local, head = whole_call(
        functools.partial(block_body, states, cands),
        [
            out((act + SMALL, cols), bf16),
            out((2 * rows, act + SMALL), bf16),
            out((rows, cols), bf16),
            out((1, cols), f32),
        ],
        [pltpu.VMEM((SMALL, cols), f32)],
        held,
        flags,
        piece,
        first,
        second,
        action_weight,
        state_hidden,
        action_mean,
        action_spread,
        head_gain,
        value_weight,
    )

    step = lambda array, k: send(array, [((t, d), (t ^ k, d)) for t, d in every])
    near = {k: step(block, k) for k in (2, 1, 3)}

    basis, *later = basis_stage(
        flags, pair(2) + pair(1), [block], [held], None, (0, units), features, [], False
    )
    near_two = [near[2], near[1]]
    basis, square, *held = basis_stage(
        flags,
        pair(3),
        near_two,
        [later[:2], later[2:]],
        basis,
        (0, units),
        features,
        [block] + near_two,
        False,
    )
    cut = units // 2
    own_a, narrow_a, square_last = basis_stage(
        flags, [], [near[3]], [held], basis, (0, cut), features, [near[3]], True
    )
    other_a = send(narrow_a, swap_core)
    square = square + square_last
    other_square = send(square, swap_core)
    own_b, narrow_b = basis_stage(
        flags, [], [near[3]], [held], basis, (cut, units), features, [], True
    )
    other_b = send(narrow_b, swap_core)
    down_first = stage(flags, [column(3), column(1)], [], [], None)
    hidden_a, down_z = hidden_stage(
        flags, [column(2)], own_a, other_a, features, square, other_square, full_width
    )
    hidden_b, down_own = hidden_stage(
        flags, [column(0)], own_b, other_b, features, square, other_square, full_width
    )
    hidden = [hidden_a, hidden_b]

    both, lower, upper = (0, 1), (0,), (1,)
    x_pair, diagonal_upper = down_products(
        hidden,
        down_first,
        cols,
        [(both, 0, [(0, 0), (1, 0)]), (lower, 1, [(0, cols)])],
        [2 * cols, cols],
    )
    got_x = step(x_pair, 1)
    (z_pair,) = down_products(
        hidden,
        [down_z],
        cols,
        [(upper, 0, [(0, cols)])],
        [2 * cols],
        [(diagonal_upper, 0)],
    )
    got_z = step(z_pair, 2)
    z_lower, x_upper, own_lower, own_upper = down_products(
        hidden,
        [down_z, down_first[1], down_own],
        cols,
        [(lower, 0, [(0, 0)]), (upper, 1, [(1, 0)]), (both, 2, [(2, 0), (3, 0)])],
        [cols] * 4,
    )
    add = lambda *parts: sum(part.astype(f32) for part in parts).astype(bf16)
    got_lower = step(add(z_lower, got_x[:, :cols]), 2)
    got_upper = step(add(x_upper, got_z[:, :cols]), 1)
    sums = [
        add(own_lower, got_x[:, cols:], got_lower),
        add(own_upper, got_z[:, cols:], got_upper),
    ]
    far = [
        send(sums[part], [((t, 1 - t // 4), (t ^ 4, part)) for t in range(TP)])
        for part in range(2)
    ]
    crossed = send(
        jnp.where(dp == 0, sums[1], sums[0]), [((t, t // 4), (t, 1 - t // 4)) for t in range(TP)]
    )
    mine = jnp.where(home, jnp.where(dp == 0, sums[0], sums[1]), crossed).astype(f32)
    summed = mine + jnp.where(dp == 0, far[0], far[1]).astype(f32)
    output_local = (inputs_local.astype(f32) + summed).astype(bf16)

    wide_out = output_local.astype(f32)
    totals = jnp.stack(
        [
            jnp.sum(wide_out * wide_out, axis=1),
            jnp.sum(wide_out * head, axis=1),
        ]
    )
    for k in (1, 2, 4):
        totals = totals + step(totals, k)
    values = totals[1] * lax.rsqrt(totals[0] / full_width + epsilon)
    return (
        output_local.reshape(states, cands, cols),
        values.reshape(states, cands),
    )


def solution(mesh):
    local = local_blocks if mesh.shape["tp"] == TP and mesh.shape["dp"] == 2 else local_gathered
    return jax.shard_map(
        local,
        mesh=mesh,
        in_specs=(
            P(("rep", "dp"), "tp"),
            P(("rep", "dp"), None),
            P("rep"),
            P("rep"),
            P(None, "tp"),
            P("tp"),
            P("dp", "tp"),
            P("dp", "tp"),
            P("tp", "dp"),
            P("tp"),
            P("tp"),
        ),
        out_specs=(P(("rep", "dp"), None, "tp"), P(("rep", "dp"), None)),
        check_vma=False,
    )
```

```python
import functools
import math

import jax
import jax.numpy as jnp
from jax import lax
from jax.experimental import pallas as pl
from jax.experimental.pallas import tpu as pltpu
from jax.sharding import PartitionSpec as P

epsilon = 1e-05
modulus = 251


def action_features(action_seeds, action_mean, action_spread):
    harmonic = jnp.arange(1, action_mean.shape[0] + 1, dtype=jnp.int32)
    phases = action_seeds[:, :, None] * harmonic % modulus
    angles = phases.astype(jnp.float32) * (2.0 * math.pi / modulus)
    return (action_mean + action_spread * jnp.cos(angles)).astype(jnp.bfloat16)


def head_value(output_rows, head_gain, value_weight):
    wide_out = output_rows.astype(jnp.float32)
    scale = lax.rsqrt(jnp.mean(wide_out * wide_out, axis=1) + epsilon)
    return jnp.sum(wide_out * (head_gain * value_weight), axis=1) * scale


def local_gathered(
    state_hidden,
    action_seeds,
    action_mean,
    action_spread,
    action_weight,
    norm_gain,
    gate_weight,
    up_weight,
    down_weight,
    head_gain,
    value_weight,
):
    state_count, cand_count = action_seeds.shape
    row_count = state_count * cand_count
    local_cols = action_weight.shape[1]
    features = action_features(action_seeds, action_mean, action_spread)
    embedded = jnp.dot(
        features.reshape(row_count, features.shape[2]),
        action_weight,
        preferred_element_type=jnp.float32,
    )
    inputs_local = (
        (
            state_hidden.astype(jnp.float32)[:, None, :]
            + embedded.reshape(state_count, cand_count, local_cols)
        )
        .reshape(row_count, local_cols)
        .astype(jnp.bfloat16)
    )
    gathered, gain_full = (
        lax.all_gather(inputs_local, "tp", axis=1, tiled=True),
        lax.all_gather(norm_gain.astype(jnp.bfloat16), "tp", axis=0, tiled=True).astype(
            norm_gain.dtype
        ),
    )
    scale = lax.rsqrt(
        jnp.mean(jnp.square(gathered.astype(jnp.float32)), axis=1, keepdims=True) + epsilon
    )
    normed = (gathered.astype(jnp.float32) * scale * gain_full).astype(jnp.bfloat16)
    gate_sum = jnp.dot(
        normed,
        lax.all_gather(gate_weight, "dp", axis=0, tiled=True),
        preferred_element_type=jnp.float32,
    )
    up_sum = jnp.dot(
        normed,
        lax.all_gather(up_weight, "dp", axis=0, tiled=True),
        preferred_element_type=jnp.float32,
    )
    hidden = (jax.nn.silu(gate_sum) * up_sum).astype(jnp.bfloat16)
    partial_terms = jnp.dot(
        hidden,
        lax.all_gather(down_weight, "dp", axis=1, tiled=True),
        preferred_element_type=jnp.float32,
    )
    summed_local = lax.psum_scatter(partial_terms, "tp", scatter_dimension=1, tiled=True)
    output_local = (inputs_local.astype(jnp.float32) + summed_local).astype(jnp.bfloat16)
    output_full, head_full, value_full = (
        lax.all_gather(output_local, "tp", axis=1, tiled=True),
        lax.all_gather(head_gain.astype(jnp.bfloat16), "tp", axis=0, tiled=True).astype(
            head_gain.dtype
        ),
        lax.all_gather(value_weight.astype(jnp.bfloat16), "tp", axis=0, tiled=True).astype(
            value_weight.dtype
        ),
    )
    values = head_value(output_full, head_full, value_full)
    return (
        output_local.reshape(state_count, cand_count, local_cols),
        values.reshape(state_count, cand_count),
    )


TP = 8
SMALL = 16
MIB = 1024 * 1024


def send(array, pairs):
    return lax.ppermute(
        array, ("tp", "dp"), [(2 * st + sd, 2 * dt + dd) for (st, sd), (dt, dd) in pairs]
    )


SPLIT = 8


def copies_of(which, loads, sources, targets, arrived):
    made = []
    for at, (kind, size, place) in enumerate(loads):
        source, target = sources[at], targets[at]
        part = target.shape[0] // SPLIT
        for cut in range(SPLIT):
            rows = pl.ds(cut * part, part)
            if kind == "rows":
                begin = pl.multiple_of(which[place] * size + cut * part, 16)
                view = source.at[pl.ds(begin, part), :]
            else:
                view = source.at[rows, pl.ds(pl.multiple_of(which[place] * size, 128), size)]
            made.append(
                pltpu.make_async_copy(view, target.at[rows, :], arrived.at[at * SPLIT + cut])
            )
    return made


def stage(which, loads, ins, outs, compute, scratch=(), limit=3, flops=0, alias=None):
    vmem = pl.BlockSpec(memory_space=pltpu.VMEM)
    n, count = len(loads), len(ins)
    kinds = [load[:3] for load in loads]
    shapes = list(outs)
    for kind, size, _, array in loads:
        shape = (size, array.shape[1]) if kind == "rows" else (array.shape[0], size)
        shapes.append(jax.ShapeDtypeStruct(shape, array.dtype))

    def body(which_ref, *refs):
        sources, inputs = refs[:n], refs[n : n + count]
        results = refs[n + count : n + count + len(outs)]
        targets = refs[n + count + len(outs) : n + count + len(shapes)]
        extra = refs[n + count + len(shapes) :]
        made = copies_of(which_ref, kinds, sources, targets, extra[0]) if n else []
        for copy in made:
            copy.start()
        if compute is not None:
            compute(inputs, results, extra[1:] if n else extra)
        for copy in made:
            copy.wait()

    loaded = sum(2 * math.prod(shape.shape) for shape in shapes[len(outs) :])
    return pl.pallas_call(
        body,
        out_shape=shapes,
        in_specs=[pl.BlockSpec(memory_space=pltpu.SMEM)]
        + [pl.BlockSpec(memory_space=pl.ANY)] * n
        + [vmem] * count,
        out_specs=[vmem] * len(shapes),
        scratch_shapes=([pltpu.SemaphoreType.DMA((n * SPLIT,))] if n else []) + list(scratch),
        input_output_aliases={} if alias is None else {1 + n + alias: 0},
        compiler_params=pltpu.CompilerParams(vmem_limit_bytes=limit * MIB),
        cost_estimate=pl.CostEstimate(
            flops=flops, bytes_accessed=loaded, transcendentals=0
        ),
    )(which, *[load[3] for load in loads], *ins)


def to_row(column):
    size = column.shape[0]
    rows = lax.broadcasted_iota(jnp.int32, (size, size), 0)
    cols = lax.broadcasted_iota(jnp.int32, (size, size), 1)
    return jnp.sum(jnp.where(rows == cols, column, 0.0), axis=0, keepdims=True)


def to_column(row):
    size = row.shape[1]
    rows = lax.broadcasted_iota(jnp.int32, (size, size), 0)
    cols = lax.broadcasted_iota(jnp.int32, (size, size), 1)
    return jnp.sum(jnp.where(rows == cols, row, 0.0), axis=1, keepdims=True)


def basis_stage(
    which, loads, block, held, before, columns, features, squares, narrow, keep=()
):
    m, k = block.shape
    start, stop = columns
    width = stop - start
    tile = 512
    ins = [block, *held] + ([] if before is None else [before])
    summed = squares is not None
    if summed:
        ins += [features] + squares
        rows = features.shape[0]
    ins += list(keep)
    outs = [jax.ShapeDtypeStruct((2, m, width), jnp.float32)]
    if narrow:
        outs.append(jax.ShapeDtypeStruct((2, m, width), jnp.bfloat16))
    if summed:
        outs.append(jax.ShapeDtypeStruct((rows, 128), jnp.float32))

    def compute(inputs, results, extra):
        ref, *weights = inputs[:3]
        rest = list(inputs[3 : len(inputs) - len(keep)])
        lhs = extra[0]
        old = rest.pop(0) if before is not None else None
        gain = ref[m - SMALL + 4 : m - SMALL + 5, :].astype(jnp.float32)
        lhs[...] = (ref[...].astype(jnp.float32) * gain).astype(jnp.bfloat16)

        @pl.loop(0, width // tile)
        def _(j):
            at = pl.ds(pl.multiple_of(start + j * tile, tile), tile)
            to = pl.ds(pl.multiple_of(j * tile, tile), tile)
            for side in range(2):
                total = jnp.dot(lhs[...], weights[side][:, at], preferred_element_type=jnp.float32)
                if old is not None:
                    total = old[side, :, at] + total
                results[0][side, :, to] = total
                if narrow:
                    results[1][side, :, to] = total.astype(jnp.bfloat16)

        if summed:
            feature_rows, *parts = rest
            wide = jnp.dot(feature_rows[...], ref[...], preferred_element_type=jnp.float32)
            wide = wide.astype(jnp.bfloat16).astype(jnp.float32)
            wide = wide * wide
            total = None
            for at in range(0, k, 128):
                piece = wide[:, at : at + 128]
                total = piece if total is None else total + piece
            for part in parts:
                total = total + part[...]
            results[-1][...] = total
            if narrow:
                row = to_row(jnp.sum(total, axis=1, keepdims=True))
                high = row.astype(jnp.bfloat16).astype(jnp.float32)
                last = results[1][0, m - SMALL :, :rows].astype(jnp.float32)
                line = lax.broadcasted_iota(jnp.int32, last.shape, 0)
                last = jnp.where(line == SMALL - 2, high, last)
                last = jnp.where(line == SMALL - 1, row - high, last)
                results[1][0, m - SMALL :, :rows] = last.astype(jnp.bfloat16)

    return stage(
        which,
        loads,
        ins,
        outs,
        compute,
        [pltpu.VMEM((m, k), jnp.bfloat16)],
        flops=4 * m * k * width,
        alias=None if before is None or narrow else 3,
    )


def hidden_stage(which, loads, own, other, features, square, scale, width):
    _, m, units = own.shape
    rows = features.shape[0]
    tile = 512
    first = scale is None
    outs = [jax.ShapeDtypeStruct((rows, units), jnp.bfloat16)]
    if first:
        outs.append(jax.ShapeDtypeStruct((rows, 128), jnp.float32))

    def compute(inputs, results, extra):
        own, other, features, last = inputs
        if first:
            lines = other[0, m - SMALL :, :rows].astype(jnp.float32)
            row = lines[SMALL - 2 : SMALL - 1] + lines[SMALL - 1 :]
            squares = jnp.sum(last[...], axis=1, keepdims=True) + to_column(row)
            factor = lax.rsqrt(squares / width + epsilon)
            results[1][...] = jnp.broadcast_to(factor, results[1].shape)
        else:
            factor = last[:, :1]

        @pl.loop(0, units // tile)
        def _(j):
            at = pl.ds(pl.multiple_of(j * tile, tile), tile)
            sums = []
            for side in range(2):
                basis = own[side, :, at] + other[side, :, at].astype(jnp.float32)
                sums.append(
                    factor
                    * jnp.dot(
                        features[...],
                        basis.astype(jnp.bfloat16),
                        preferred_element_type=jnp.float32,
                    )
                )
            gate, up = sums
            results[0][:, at] = (gate / (1.0 + jnp.exp(-gate)) * up).astype(jnp.bfloat16)

    return stage(
        which,
        loads,
        [own, other, features, square if first else scale],
        outs,
        compute,
        flops=4 * m * rows * units,
    )


def down_body(places, cols, hidden, weights, outs):
    half = hidden[0].shape[0] // 2
    tile = 512
    for rows, which, targets in places:
        low, high = rows[0] * half, rows[-1] * half + half
        for j in range(cols // tile):
            at = j * tile
            total = None
            depth_at = 0
            for ref in hidden:
                depth = ref.shape[1]
                term = jnp.dot(
                    ref[low:high, :],
                    weights[which][depth_at : depth_at + depth, at : at + tile],
                    preferred_element_type=jnp.float32,
                )
                total = term if total is None else total + term
                depth_at += depth
            total = total.astype(jnp.bfloat16)
            for index, (out, column) in enumerate(targets):
                to = column + j * tile
                outs[out][:, to : to + tile] = total[index * half : (index + 1) * half]


def down_products(hidden, weights, cols, places, widths, copies=()):
    rows = hidden[0].shape[0]
    depth = weights[0].shape[0]
    flops = sum(len(r) * rows * depth * cols for r, *_ in places)
    vmem = pl.BlockSpec(memory_space=pltpu.VMEM)
    counts = (len(hidden), len(weights), len(copies))

    def body(*refs):
        groups, at = [], 0
        for count in counts:
            groups.append(refs[at : at + count])
            at += count
        outs = refs[at:]
        down_body(places, cols, groups[0], groups[1], outs)
        for source, (_, out) in zip(groups[2], copies):
            outs[out][:, : source.shape[1]] = source[...]

    return pl.pallas_call(
        body,
        out_shape=[jax.ShapeDtypeStruct((rows // 2, width), jnp.bfloat16) for width in widths],
        in_specs=[vmem] * sum(counts),
        out_specs=[vmem] * len(widths),
        compiler_params=pltpu.CompilerParams(vmem_limit_bytes=6 * MIB),
        cost_estimate=pl.CostEstimate(flops=flops // 16, bytes_accessed=0, transcendentals=0),
    )(*hidden, *weights, *[c[0] for c in copies])


def piece_body(flags, weight, states, gain, seeds, piece, rows):
    half = weight.shape[0] // 2
    count = states.shape[0]
    piece[:half, :] = weight[pl.ds(pl.multiple_of(flags[4] * half, 16), half), :]
    rows[...] = jnp.zeros_like(rows)
    rows[:count, :] = states[...].astype(jnp.float32)
    rows[count : count + 1, :] = gain[...].reshape(1, -1)
    high = lax.shift_right_logical(seeds[...], 8)
    low = seeds[...] - high * 256
    width = seeds.shape[1]
    rows[count + 1 : 2 * count + 1, :width] = high.astype(jnp.float32)
    rows[2 * count + 1 : 3 * count + 1, :width] = low.astype(jnp.float32)
    piece[half:, :] = rows[...].astype(jnp.bfloat16)


def block_body(count, cands, flags, piece, first, second, weight, states, mean, spread, gain, value,
               block, features, inputs, head, rows):
    f32, bf16 = jnp.float32, jnp.bfloat16
    half = weight.shape[0] // 2
    act = weight.shape[0]
    lower, home = flags[4] == 0, flags[5] == 1
    same = jnp.where(home, piece[...], first[...])
    other = jnp.where(home, first[...], second[...])
    low = jnp.where(lower, same, other)
    high = jnp.where(lower, other, same)
    block[:half, :] = low[:half]
    block[half:act, :] = high[:half]
    parts = [low[half:].astype(f32), high[half:].astype(f32)]
    rows[...] = jnp.zeros_like(rows)
    for index, part in enumerate(parts):
        rows[index * count : (index + 1) * count, :] = part[:count]
    rows[2 * count : 2 * count + 1, :] = parts[0][count : count + 1]
    block[act:, :] = rows[...].astype(bf16)

    harmonic = (lax.broadcasted_iota(jnp.int32, (cands, act), 1) + 1).astype(f32)
    diagonal = lax.broadcasted_iota(jnp.int32, (cands, cands), 0) == lax.broadcasted_iota(
        jnp.int32, (cands, cands), 1
    )
    states_at = lax.broadcasted_iota(jnp.int32, (cands, SMALL), 1)
    made = []
    for state in range(2 * count):
        part, at = parts[state // count], state % count
        seed = (
            part[count + 1 + at : count + 2 + at, :cands] * 256.0
            + part[2 * count + 1 + at : 2 * count + 2 + at, :cands]
        )
        column = jnp.sum(jnp.where(diagonal, seed, 0.0), axis=1, keepdims=True)
        product = column * harmonic
        rest = product - modulus * jnp.floor(product * (1.0 / modulus))
        rest = jnp.where(rest < 0.0, rest + modulus, rest)
        rest = jnp.where(rest >= modulus, rest - modulus, rest)
        wave = jnp.cos(rest * (2.0 * math.pi / modulus))
        value_rows = (mean[...].reshape(1, -1) + spread[...].reshape(1, -1) * wave).astype(bf16)
        made.append(value_rows)
        to = slice(state * cands, (state + 1) * cands)
        features[to, :act] = value_rows
        features[to, act:] = (states_at == state).astype(f32).astype(bf16)
    for at in range(count):
        own = jnp.where(lower, made[at], made[count + at])
        wide = jnp.dot(own, weight[...], preferred_element_type=f32)
        wide = wide + states[at : at + 1, :].astype(f32)
        inputs[at * cands : (at + 1) * cands, :] = wide.astype(bf16)
    head[...] = (gain[...] * value[...]).reshape(1, -1)


def whole_call(body, outs, scratch, after, *operands):
    whole = lambda array: pl.BlockSpec(array.shape, lambda i: (0,) * len(array.shape))
    count = len(after)
    return pl.pallas_call(
        lambda *refs: body(refs[count], *refs[count + 1 :]),
        out_shape=outs,
        grid=(1,),
        in_specs=[pl.BlockSpec(memory_space=pl.ANY)] * count
        + [pl.BlockSpec(memory_space=pltpu.SMEM)]
        + [whole(array) for array in operands[1:]],
        out_specs=[whole(array) for array in outs],
        scratch_shapes=scratch,
        compiler_params=pltpu.CompilerParams(vmem_limit_bytes=6 * MIB),
        cost_estimate=pl.CostEstimate(flops=1000000, bytes_accessed=1000000, transcendentals=0),
    )(*after, *operands)


def local_blocks(
    state_hidden,
    action_seeds,
    action_mean,
    action_spread,
    action_weight,
    norm_gain,
    gate_weight,
    up_weight,
    down_weight,
    head_gain,
    value_weight,
):
    f32, bf16 = jnp.float32, jnp.bfloat16
    states, cands = action_seeds.shape
    rows = states * cands
    act, cols = action_weight.shape
    half = act // 2
    units = gate_weight.shape[1]
    full_width = gate_weight.shape[0] * 2
    tp, dp = lax.axis_index("tp"), lax.axis_index("dp")
    home = tp // 4 == dp
    place = tp % 4
    every = [(t, d) for t in range(TP) for d in range(2)]
    swap_core = [((t, d), (t, 1 - d)) for t, d in every]

    flags = jnp.stack([place, place ^ 1, place ^ 2, place ^ 3, dp, home.astype(jnp.int32)])
    flags = flags.astype(jnp.int32)
    out = jax.ShapeDtypeStruct
    (piece,) = whole_call(
        piece_body,
        [out((half + SMALL, cols), bf16)],
        [pltpu.VMEM((SMALL, cols), f32)],
        [],
        flags,
        *[
            pltpu.with_memory_space_constraint(array, pltpu.HBM)
            for array in (action_weight, state_hidden, norm_gain, action_seeds)
        ],
    )

    first = send(
        piece,
        [((t, t // 4), (t ^ 4, t // 4)) for t in range(TP)]
        + [((t, 1 - t // 4), (t, t // 4)) for t in range(TP)],
    )
    second = send(piece, [((t, 1 - t // 4), (t ^ 4, t // 4)) for t in range(TP)])

    gate_weight, up_weight, down_weight = (
        pltpu.with_memory_space_constraint(weight, pltpu.HBM)
        for weight in (gate_weight, up_weight, down_weight)
    )
    pair = lambda k: [("rows", cols, k, gate_weight), ("rows", cols, k, up_weight)]
    column = lambda k: ("cols", cols, k, down_weight)
    held = stage(flags, pair(0), [], [], None)

    block, features, inputs_local, head = whole_call(
        functools.partial(block_body, states, cands),
        [
            out((act + SMALL, cols), bf16),
            out((2 * rows, act + SMALL), bf16),
            out((rows, cols), bf16),
            out((1, cols), f32),
        ],
        [pltpu.VMEM((SMALL, cols), f32)],
        held,
        flags,
        piece,
        first,
        second,
        action_weight,
        state_hidden,
        action_mean,
        action_spread,
        head_gain,
        value_weight,
    )

    step = lambda array, k: send(array, [((t, d), (t ^ k, d)) for t, d in every])
    near = {k: step(block, k) for k in (2, 1, 3)}

    span = (0, units)
    basis, square, *later = basis_stage(
        flags, pair(2), block, held, None, span, features, [], False
    )
    basis, square, *later = basis_stage(
        flags, pair(1), near[2], later, basis, span, features, [square], False
    )
    basis, square, *last = basis_stage(
        flags, pair(3), near[1], later, basis, span, features, [square], False
    )
    cut = units // 2
    own_a, narrow_a, square, down_diagonal = basis_stage(
        flags, [column(3)], near[3], last, basis, (0, cut), features, [square], True
    )
    other_a = send(narrow_a, swap_core)
    own_b, narrow_b, down_x = basis_stage(
        flags, [column(1)], near[3], last, basis, (cut, units), features, None, True
    )
    other_b = send(narrow_b, swap_core)
    hidden_a, scale, down_z = hidden_stage(
        flags, [column(2)], own_a, other_a, features, square, None, full_width
    )
    hidden_b, down_own = hidden_stage(
        flags, [column(0)], own_b, other_b, features, None, scale, full_width
    )
    hidden = [hidden_a, hidden_b]

    both, lower, upper = (0, 1), (0,), (1,)
    x_pair, diagonal_upper = down_products(
        hidden,
        [down_diagonal, down_x],
        cols,
        [(both, 0, [(0, 0), (1, 0)]), (lower, 1, [(0, cols)])],
        [2 * cols, cols],
    )
    got_x = step(x_pair, 1)
    (z_pair,) = down_products(
        hidden,
        [down_z],
        cols,
        [(upper, 0, [(0, cols)])],
        [2 * cols],
        [(diagonal_upper, 0)],
    )
    got_z = step(z_pair, 2)
    z_lower, x_upper, own_lower, own_upper = down_products(
        hidden,
        [down_z, down_x, down_own],
        cols,
        [(lower, 0, [(0, 0)]), (upper, 1, [(1, 0)]), (both, 2, [(2, 0), (3, 0)])],
        [cols] * 4,
    )
    add = lambda *parts: sum(part.astype(f32) for part in parts).astype(bf16)
    got_lower = step(add(z_lower, got_x[:, :cols]), 2)
    got_upper = step(add(x_upper, got_z[:, :cols]), 1)
    sums = [
        lax.optimization_barrier(add(own_lower, got_x[:, cols:], got_lower)),
        lax.optimization_barrier(add(own_upper, got_z[:, cols:], got_upper)),
    ]
    far = [
        send(sums[part], [((t, 1 - t // 4), (t ^ 4, part)) for t in range(TP)])
        for part in range(2)
    ]
    crossed = send(
        jnp.where(dp == 0, sums[1], sums[0]), [((t, t // 4), (t, 1 - t // 4)) for t in range(TP)]
    )
    mine = jnp.where(home, jnp.where(dp == 0, sums[0], sums[1]), crossed).astype(f32)
    summed = mine + jnp.where(dp == 0, far[0], far[1]).astype(f32)
    output_local = (inputs_local.astype(f32) + summed).astype(bf16)

    wide_out = output_local.astype(f32)
    totals = jnp.stack(
        [
            jnp.sum(wide_out * wide_out, axis=1),
            jnp.sum(wide_out * head, axis=1),
        ]
    )
    for k in (1, 2, 4):
        totals = totals + step(totals, k)
    values = totals[1] * lax.rsqrt(totals[0] / full_width + epsilon)
    return (
        output_local.reshape(states, cands, cols),
        values.reshape(states, cands),
    )


def solution(mesh):
    local = local_blocks if mesh.shape["tp"] == TP and mesh.shape["dp"] == 2 else local_gathered
    return jax.shard_map(
        local,
        mesh=mesh,
        in_specs=(
            P(("rep", "dp"), "tp"),
            P(("rep", "dp"), None),
            P("rep"),
            P("rep"),
            P(None, "tp"),
            P("tp"),
            P("dp", "tp"),
            P("dp", "tp"),
            P("tp", "dp"),
            P("tp"),
            P("tp"),
        ),
        out_specs=(P(("rep", "dp"), None, "tp"), P(("rep", "dp"), None)),
        check_vma=False,
    )
```

```python
import functools
import math

import jax
import jax.numpy as jnp
from jax import lax
from jax.experimental import pallas as pl
from jax.experimental.pallas import tpu as pltpu
from jax.sharding import PartitionSpec as P

epsilon = 1e-05
modulus = 251


def action_features(action_seeds, action_mean, action_spread):
    harmonic = jnp.arange(1, action_mean.shape[0] + 1, dtype=jnp.int32)
    phases = action_seeds[:, :, None] * harmonic % modulus
    angles = phases.astype(jnp.float32) * (2.0 * math.pi / modulus)
    return (action_mean + action_spread * jnp.cos(angles)).astype(jnp.bfloat16)


def head_value(output_rows, head_gain, value_weight):
    wide_out = output_rows.astype(jnp.float32)
    scale = lax.rsqrt(jnp.mean(wide_out * wide_out, axis=1) + epsilon)
    return jnp.sum(wide_out * (head_gain * value_weight), axis=1) * scale


def local_gathered(
    state_hidden,
    action_seeds,
    action_mean,
    action_spread,
    action_weight,
    norm_gain,
    gate_weight,
    up_weight,
    down_weight,
    head_gain,
    value_weight,
):
    state_count, cand_count = action_seeds.shape
    row_count = state_count * cand_count
    local_cols = action_weight.shape[1]
    features = action_features(action_seeds, action_mean, action_spread)
    embedded = jnp.dot(
        features.reshape(row_count, features.shape[2]),
        action_weight,
        preferred_element_type=jnp.float32,
    )
    inputs_local = (
        (
            state_hidden.astype(jnp.float32)[:, None, :]
            + embedded.reshape(state_count, cand_count, local_cols)
        )
        .reshape(row_count, local_cols)
        .astype(jnp.bfloat16)
    )
    gathered, gain_full = (
        lax.all_gather(inputs_local, "tp", axis=1, tiled=True),
        lax.all_gather(norm_gain.astype(jnp.bfloat16), "tp", axis=0, tiled=True).astype(
            norm_gain.dtype
        ),
    )
    scale = lax.rsqrt(
        jnp.mean(jnp.square(gathered.astype(jnp.float32)), axis=1, keepdims=True) + epsilon
    )
    normed = (gathered.astype(jnp.float32) * scale * gain_full).astype(jnp.bfloat16)
    gate_sum = jnp.dot(
        normed,
        lax.all_gather(gate_weight, "dp", axis=0, tiled=True),
        preferred_element_type=jnp.float32,
    )
    up_sum = jnp.dot(
        normed,
        lax.all_gather(up_weight, "dp", axis=0, tiled=True),
        preferred_element_type=jnp.float32,
    )
    hidden = (jax.nn.silu(gate_sum) * up_sum).astype(jnp.bfloat16)
    partial_terms = jnp.dot(
        hidden,
        lax.all_gather(down_weight, "dp", axis=1, tiled=True),
        preferred_element_type=jnp.float32,
    )
    summed_local = lax.psum_scatter(partial_terms, "tp", scatter_dimension=1, tiled=True)
    output_local = (inputs_local.astype(jnp.float32) + summed_local).astype(jnp.bfloat16)
    output_full, head_full, value_full = (
        lax.all_gather(output_local, "tp", axis=1, tiled=True),
        lax.all_gather(head_gain.astype(jnp.bfloat16), "tp", axis=0, tiled=True).astype(
            head_gain.dtype
        ),
        lax.all_gather(value_weight.astype(jnp.bfloat16), "tp", axis=0, tiled=True).astype(
            value_weight.dtype
        ),
    )
    values = head_value(output_full, head_full, value_full)
    return (
        output_local.reshape(state_count, cand_count, local_cols),
        values.reshape(state_count, cand_count),
    )


TP = 8
SMALL = 16
MIB = 1024 * 1024


def send(array, pairs):
    return lax.ppermute(
        array, ("tp", "dp"), [(2 * st + sd, 2 * dt + dd) for (st, sd), (dt, dd) in pairs]
    )


SPLIT = 8


def stage(which, loads, ins, outs, compute, scratch=(), limit=6, flops=0, alias=None):
    vmem = pl.BlockSpec(memory_space=pltpu.VMEM)
    count = len(ins)
    shapes, sources, flat = list(outs), [], []
    for kind, parts in loads:
        array, total = parts[0][0], sum(part[4] for part in parts)
        shape = (total, array.shape[1]) if kind == "rows" else (array.shape[0], total)
        shapes.append(jax.ShapeDtypeStruct(shape, array.dtype))
        sources += [part[0] for part in parts]
        flat.append((kind, parts))
    n = len(sources)

    def body(which_ref, *refs):
        inputs = refs[n : n + count]
        results = refs[n + count : n + count + len(outs)]
        targets = refs[n + count + len(outs) : n + count + len(shapes)]
        extra = refs[n + count + len(shapes) :]
        made, at = [], 0
        for (kind, parts), target in zip(flat, targets):
            filled = 0
            for _, place, unit, offset, size in parts:
                block = which_ref[place] * unit + offset
                length = size if kind == "rows" else target.shape[0]
                piece = length // SPLIT
                for cut in range(SPLIT):
                    if kind == "rows":
                        begin = pl.multiple_of(block + cut * piece, 16)
                        view = refs[at].at[pl.ds(begin, piece), :]
                        to = target.at[pl.ds(filled + cut * piece, piece), :]
                    else:
                        rows = pl.ds(cut * piece, piece)
                        view = refs[at].at[rows, pl.ds(pl.multiple_of(block, 128), size)]
                        to = target.at[rows, pl.ds(filled, size)]
                    made.append(pltpu.make_async_copy(view, to, extra[0].at[len(made)]))
                filled += size
                at += 1
        for copy in made:
            copy.start()
        if compute is not None:
            compute(inputs, results, extra[1:] if n else extra)
        for copy in made:
            copy.wait()

    loaded = sum(2 * math.prod(shape.shape) for shape in shapes[len(outs) :])
    return pl.pallas_call(
        body,
        out_shape=shapes,
        in_specs=[pl.BlockSpec(memory_space=pltpu.SMEM)]
        + [pl.BlockSpec(memory_space=pl.ANY)] * n
        + [vmem] * count,
        out_specs=[vmem] * len(shapes),
        scratch_shapes=([pltpu.SemaphoreType.DMA((n * SPLIT,))] if n else []) + list(scratch),
        input_output_aliases={} if alias is None else {1 + n + alias: 0},
        compiler_params=pltpu.CompilerParams(vmem_limit_bytes=limit * MIB),
        cost_estimate=pl.CostEstimate(flops=flops, bytes_accessed=loaded, transcendentals=0),
    )(which, *sources, *ins)


def to_row(column):
    size = column.shape[0]
    rows = lax.broadcasted_iota(jnp.int32, (size, size), 0)
    cols = lax.broadcasted_iota(jnp.int32, (size, size), 1)
    return jnp.sum(jnp.where(rows == cols, column, 0.0), axis=0, keepdims=True)


def to_column(row):
    size = row.shape[1]
    rows = lax.broadcasted_iota(jnp.int32, (size, size), 0)
    cols = lax.broadcasted_iota(jnp.int32, (size, size), 1)
    return jnp.sum(jnp.where(rows == cols, row, 0.0), axis=1, keepdims=True)


def basis_stage(which, loads, blocks, held, before, columns, features, squares, narrow):
    m, k = blocks[0].shape
    count = len(blocks)
    start, stop = columns
    width = stop - start
    tile = 512
    ins = [*blocks, *held] + ([] if before is None else [before])
    summed = squares is not None
    if summed:
        ins += [features] + squares
        rows = features.shape[0]
    outs = [jax.ShapeDtypeStruct((2, m, width), jnp.float32)]
    if narrow:
        outs.append(jax.ShapeDtypeStruct((2, m, width), jnp.bfloat16))
    if summed:
        outs.append(jax.ShapeDtypeStruct((rows, 128), jnp.float32))

    def compute(inputs, results, extra):
        refs, weights = inputs[:count], inputs[count : 3 * count]
        rest = list(inputs[3 * count :])
        lhs = extra[0]
        old = rest.pop(0) if before is not None else None
        for index, ref in enumerate(refs):
            gain = ref[m - SMALL + 4 : m - SMALL + 5, :].astype(jnp.float32)
            lhs[index] = (ref[...].astype(jnp.float32) * gain).astype(jnp.bfloat16)

        @pl.loop(0, width // tile)
        def _(j):
            at = pl.ds(pl.multiple_of(start + j * tile, tile), tile)
            to = pl.ds(pl.multiple_of(j * tile, tile), tile)
            for side in range(2):
                total = old[side, :, at] if old is not None else None
                for index in range(count):
                    term = jnp.dot(
                        lhs[index],
                        weights[2 * index + side][:, at],
                        preferred_element_type=jnp.float32,
                    )
                    total = term if total is None else total + term
                results[0][side, :, to] = total
                if narrow:
                    results[1][side, :, to] = total.astype(jnp.bfloat16)

        if summed:
            feature_rows, *parts = rest
            total = None
            for ref in refs:
                wide = jnp.dot(feature_rows[...], ref[...], preferred_element_type=jnp.float32)
                wide = wide.astype(jnp.bfloat16).astype(jnp.float32)
                wide = wide * wide
                for at in range(0, k, 128):
                    piece = wide[:, at : at + 128]
                    total = piece if total is None else total + piece
            for part in parts:
                total = total + part[...]
            results[-1][...] = total
            if narrow:
                row = to_row(jnp.sum(total, axis=1, keepdims=True))
                high = row.astype(jnp.bfloat16).astype(jnp.float32)
                last = results[1][0, m - SMALL :, :rows].astype(jnp.float32)
                line = lax.broadcasted_iota(jnp.int32, last.shape, 0)
                last = jnp.where(line == SMALL - 2, high, last)
                last = jnp.where(line == SMALL - 1, row - high, last)
                results[1][0, m - SMALL :, :rows] = last.astype(jnp.bfloat16)

    return stage(
        which,
        loads,
        ins,
        outs,
        compute,
        [pltpu.VMEM((count, m, k), jnp.bfloat16)],
        flops=4 * m * k * width * count,
        alias=None,
    )


def hidden_stage(which, loads, own, other, features, square, scale, width):
    _, m, units = own.shape
    rows = features.shape[0]
    tile = 512
    first = scale is None
    outs = [jax.ShapeDtypeStruct((rows, units), jnp.bfloat16)]
    if first:
        outs.append(jax.ShapeDtypeStruct((rows, 128), jnp.float32))

    def compute(inputs, results, extra):
        own, other, features, last = inputs
        if first:
            lines = other[0, m - SMALL :, :rows].astype(jnp.float32)
            row = lines[SMALL - 2 : SMALL - 1] + lines[SMALL - 1 :]
            squares = jnp.sum(last[...], axis=1, keepdims=True) + to_column(row)
            factor = lax.rsqrt(squares / width + epsilon)
            results[1][...] = jnp.broadcast_to(factor, results[1].shape)
        else:
            factor = last[:, :1]

        @pl.loop(0, units // tile)
        def _(j):
            at = pl.ds(pl.multiple_of(j * tile, tile), tile)
            sums = []
            for side in range(2):
                basis = own[side, :, at] + other[side, :, at].astype(jnp.float32)
                sums.append(
                    factor
                    * jnp.dot(
                        features[...],
                        basis.astype(jnp.bfloat16),
                        preferred_element_type=jnp.float32,
                    )
                )
            gate, up = sums
            results[0][:, at] = (gate / (1.0 + jnp.exp(-gate)) * up).astype(jnp.bfloat16)

    return stage(
        which,
        loads,
        [own, other, features, square if first else scale],
        outs,
        compute,
        flops=4 * m * rows * units,
    )


def down_body(places, cols, hidden, weights, outs):
    half = hidden[0].shape[0] // 2
    tile = 512
    for rows, tiles, targets in places:
        low, high = rows[0] * half, rows[-1] * half + half
        for j, (which, at) in enumerate(tiles):
            total = None
            depth_at = 0
            for ref in hidden:
                depth = ref.shape[1]
                term = jnp.dot(
                    ref[low:high, :],
                    weights[which][depth_at : depth_at + depth, at : at + tile],
                    preferred_element_type=jnp.float32,
                )
                total = term if total is None else total + term
                depth_at += depth
            total = total.astype(jnp.bfloat16)
            for index, (out, column) in enumerate(targets):
                to = column + j * tile
                outs[out][:, to : to + tile] = total[index * half : (index + 1) * half]


def down_products(hidden, weights, cols, places, widths, copies=()):
    rows = hidden[0].shape[0]
    depth = weights[0].shape[0]
    flops = sum(len(r) * rows * depth * cols for r, *_ in places)
    vmem = pl.BlockSpec(memory_space=pltpu.VMEM)
    counts = (len(hidden), len(weights), len(copies))

    def body(*refs):
        groups, at = [], 0
        for count in counts:
            groups.append(refs[at : at + count])
            at += count
        outs = refs[at:]
        down_body(places, cols, groups[0], groups[1], outs)
        for source, (_, out) in zip(groups[2], copies):
            outs[out][:, : source.shape[1]] = source[...]

    return pl.pallas_call(
        body,
        out_shape=[jax.ShapeDtypeStruct((rows // 2, width), jnp.bfloat16) for width in widths],
        in_specs=[vmem] * sum(counts),
        out_specs=[vmem] * len(widths),
        compiler_params=pltpu.CompilerParams(vmem_limit_bytes=6 * MIB),
        cost_estimate=pl.CostEstimate(flops=flops // 16, bytes_accessed=0, transcendentals=0),
    )(*hidden, *weights, *[c[0] for c in copies])


def piece_body(flags, weight, states, gain, seeds, piece, rows):
    half = weight.shape[0] // 2
    count = states.shape[0]
    piece[:half, :] = weight[pl.ds(pl.multiple_of(flags[4] * half, 16), half), :]
    rows[...] = jnp.zeros_like(rows)
    rows[:count, :] = states[...].astype(jnp.float32)
    rows[count : count + 1, :] = gain[...].reshape(1, -1)
    high = lax.shift_right_logical(seeds[...], 8)
    low = seeds[...] - high * 256
    width = seeds.shape[1]
    rows[count + 1 : 2 * count + 1, :width] = high.astype(jnp.float32)
    rows[2 * count + 1 : 3 * count + 1, :width] = low.astype(jnp.float32)
    piece[half:, :] = rows[...].astype(jnp.bfloat16)


def block_body(count, cands, flags, piece, first, second, weight, states, mean, spread, gain, value,
               block, features, inputs, head, rows):
    f32, bf16 = jnp.float32, jnp.bfloat16
    half = weight.shape[0] // 2
    act = weight.shape[0]
    lower, home = flags[4] == 0, flags[5] == 1
    same = jnp.where(home, piece[...], first[...])
    other = jnp.where(home, first[...], second[...])
    low = jnp.where(lower, same, other)
    high = jnp.where(lower, other, same)
    block[:half, :] = low[:half]
    block[half:act, :] = high[:half]
    parts = [low[half:].astype(f32), high[half:].astype(f32)]
    rows[...] = jnp.zeros_like(rows)
    for index, part in enumerate(parts):
        rows[index * count : (index + 1) * count, :] = part[:count]
    rows[2 * count : 2 * count + 1, :] = parts[0][count : count + 1]
    block[act:, :] = rows[...].astype(bf16)

    harmonic = (lax.broadcasted_iota(jnp.int32, (cands, act), 1) + 1).astype(f32)
    diagonal = lax.broadcasted_iota(jnp.int32, (cands, cands), 0) == lax.broadcasted_iota(
        jnp.int32, (cands, cands), 1
    )
    states_at = lax.broadcasted_iota(jnp.int32, (cands, SMALL), 1)
    made = []
    for state in range(2 * count):
        part, at = parts[state // count], state % count
        seed = (
            part[count + 1 + at : count + 2 + at, :cands] * 256.0
            + part[2 * count + 1 + at : 2 * count + 2 + at, :cands]
        )
        column = jnp.sum(jnp.where(diagonal, seed, 0.0), axis=1, keepdims=True)
        product = column * harmonic
        rest = product - modulus * jnp.floor(product * (1.0 / modulus))
        rest = jnp.where(rest < 0.0, rest + modulus, rest)
        rest = jnp.where(rest >= modulus, rest - modulus, rest)
        wave = jnp.cos(rest * (2.0 * math.pi / modulus))
        value_rows = (mean[...].reshape(1, -1) + spread[...].reshape(1, -1) * wave).astype(bf16)
        made.append(value_rows)
        to = slice(state * cands, (state + 1) * cands)
        features[to, :act] = value_rows
        features[to, act:] = (states_at == state).astype(f32).astype(bf16)
    for at in range(count):
        own = jnp.where(lower, made[at], made[count + at])
        wide = jnp.dot(own, weight[...], preferred_element_type=f32)
        wide = wide + states[at : at + 1, :].astype(f32)
        inputs[at * cands : (at + 1) * cands, :] = wide.astype(bf16)
    head[...] = (gain[...] * value[...]).reshape(1, -1)


def whole_call(body, outs, scratch, after, *operands):
    whole = lambda array: pl.BlockSpec(array.shape, lambda i: (0,) * len(array.shape))
    count = len(after)
    return pl.pallas_call(
        lambda *refs: body(refs[count], *refs[count + 1 :]),
        out_shape=outs,
        grid=(1,),
        in_specs=[pl.BlockSpec(memory_space=pl.ANY)] * count
        + [pl.BlockSpec(memory_space=pltpu.SMEM)]
        + [whole(array) for array in operands[1:]],
        out_specs=[whole(array) for array in outs],
        scratch_shapes=scratch,
        compiler_params=pltpu.CompilerParams(vmem_limit_bytes=6 * MIB),
        cost_estimate=pl.CostEstimate(flops=1000000, bytes_accessed=1000000, transcendentals=0),
    )(*after, *operands)


def local_blocks(
    state_hidden,
    action_seeds,
    action_mean,
    action_spread,
    action_weight,
    norm_gain,
    gate_weight,
    up_weight,
    down_weight,
    head_gain,
    value_weight,
):
    f32, bf16 = jnp.float32, jnp.bfloat16
    states, cands = action_seeds.shape
    rows = states * cands
    act, cols = action_weight.shape
    half = act // 2
    units = gate_weight.shape[1]
    full_width = gate_weight.shape[0] * 2
    tp, dp = lax.axis_index("tp"), lax.axis_index("dp")
    home = tp // 4 == dp
    place = tp % 4
    every = [(t, d) for t in range(TP) for d in range(2)]
    swap_core = [((t, d), (t, 1 - d)) for t, d in every]

    flags = jnp.stack([place, place ^ 1, place ^ 2, place ^ 3, dp, home.astype(jnp.int32)])
    flags = flags.astype(jnp.int32)
    out = jax.ShapeDtypeStruct
    (piece,) = whole_call(
        piece_body,
        [out((half + SMALL, cols), bf16)],
        [pltpu.VMEM((SMALL, cols), f32)],
        [],
        flags,
        *[
            pltpu.with_memory_space_constraint(array, pltpu.HBM)
            for array in (action_weight, state_hidden, norm_gain, action_seeds)
        ],
    )

    first = send(
        piece,
        [((t, t // 4), (t ^ 4, t // 4)) for t in range(TP)]
        + [((t, 1 - t // 4), (t, t // 4)) for t in range(TP)],
    )
    second = send(piece, [((t, 1 - t // 4), (t ^ 4, t // 4)) for t in range(TP)])

    gate_weight, up_weight, down_weight = (
        pltpu.with_memory_space_constraint(weight, pltpu.HBM)
        for weight in (gate_weight, up_weight, down_weight)
    )
    pair = lambda k: [("rows", [(w, k, cols, 0, cols)]) for w in (gate_weight, up_weight)]
    column = lambda k: ("cols", [(down_weight, k, cols, 0, cols)])
    tile = cols // 2
    held = stage(flags, pair(0), [], [], None)

    block, features, inputs_local, head = whole_call(
        functools.partial(block_body, states, cands),
        [
            out((act + SMALL, cols), bf16),
            out((2 * rows, act + SMALL), bf16),
            out((rows, cols), bf16),
            out((1, cols), f32),
        ],
        [pltpu.VMEM((SMALL, cols), f32)],
        held,
        flags,
        piece,
        first,
        second,
        action_weight,
        state_hidden,
        action_mean,
        action_spread,
        head_gain,
        value_weight,
    )

    step = lambda array, k: send(array, [((t, d), (t ^ k, d)) for t, d in every])
    near = {k: step(block, k) for k in (2, 1)}

    span = (0, units)
    basis, square, *later = basis_stage(
        flags, pair(2) + pair(1), [block], held, None, span, features, [], False
    )
    late_block, square = lax.optimization_barrier((block, square))
    near[3] = step(late_block, 3)
    basis, square, *last = basis_stage(
        flags, pair(3), [near[2], near[1]], later, basis, span, features, [square], False
    )
    cut = units // 2
    own_a, narrow_a, square, down_diagonal = basis_stage(
        flags, [column(3)], [near[3]], last, basis, (0, cut), features, [square], True
    )
    other_a = send(narrow_a, swap_core)
    own_b, narrow_b, down_x = basis_stage(
        flags, [column(1)], [near[3]], last, basis, (cut, units), features, None, True
    )
    other_b = send(narrow_b, swap_core)
    hidden_a, scale, down_z = hidden_stage(
        flags, [column(2)], own_a, other_a, features, square, None, full_width
    )
    hidden_b, down_own = hidden_stage(
        flags, [column(0)], own_b, other_b, features, None, scale, full_width
    )
    hidden = [hidden_a, hidden_b]

    both, lower, upper = (0, 1), (0,), (1,)
    x_pair, diagonal_upper = down_products(
        hidden,
        [down_diagonal, down_x],
        cols,
        [
            (both, [(0, 0), (0, tile)], [(0, 0), (1, 0)]),
            (lower, [(1, 0), (1, tile)], [(0, cols)]),
        ],
        [2 * cols, cols],
    )
    got_x = step(x_pair, 1)
    (z_pair,) = down_products(
        hidden,
        [down_z],
        cols,
        [(upper, [(0, 0), (0, tile)], [(0, cols)])],
        [2 * cols],
        [(diagonal_upper, 0)],
    )
    got_z = step(z_pair, 2)
    z_lower, x_upper, own_lower, own_upper = down_products(
        hidden,
        [down_z, down_x, down_own],
        cols,
        [
            (lower, [(0, 0), (0, tile)], [(0, 0)]),
            (upper, [(1, 0), (1, tile)], [(1, 0)]),
            (both, [(2, 0), (2, tile)], [(2, 0), (3, 0)]),
        ],
        [cols] * 4,
    )
    add = lambda *parts: sum(part.astype(f32) for part in parts).astype(bf16)
    got_lower = step(add(z_lower, got_x[:, :cols]), 2)
    got_upper = step(add(x_upper, got_z[:, :cols]), 1)
    sums = [
        lax.optimization_barrier(add(own_lower, got_x[:, cols:], got_lower)),
        lax.optimization_barrier(add(own_upper, got_z[:, cols:], got_upper)),
    ]
    far = []
    for part in range(2):
        pairs = [((t, 1 - t // 4), (t ^ 4, part)) for t in range(TP)]
        pairs += [((t, part), (t, 1 - part)) for t in range(TP) if t // 4 == part]
        far.append(send(jnp.where(home, sums[1 - part], sums[part]), pairs))
    mine = jnp.where(
        home,
        jnp.where(dp == 0, sums[0], sums[1]),
        jnp.where(dp == 0, far[1], far[0]),
    )
    summed = mine.astype(f32) + jnp.where(dp == 0, far[0], far[1]).astype(f32)
    output_local = (inputs_local.astype(f32) + summed).astype(bf16)

    wide_out = output_local.astype(f32)
    totals = jnp.stack(
        [
            jnp.sum(wide_out * wide_out, axis=1),
            jnp.sum(wide_out * head, axis=1),
        ]
    )
    for k in (1, 2, 4):
        totals = totals + step(totals, k)
    values = totals[1] * lax.rsqrt(totals[0] / full_width + epsilon)
    return (
        output_local.reshape(states, cands, cols),
        values.reshape(states, cands),
    )


def solution(mesh):
    local = local_blocks if mesh.shape["tp"] == TP and mesh.shape["dp"] == 2 else local_gathered
    return jax.shard_map(
        local,
        mesh=mesh,
        in_specs=(
            P(("rep", "dp"), "tp"),
            P(("rep", "dp"), None),
            P("rep"),
            P("rep"),
            P(None, "tp"),
            P("tp"),
            P("dp", "tp"),
            P("dp", "tp"),
            P("tp", "dp"),
            P("tp"),
            P("tp"),
        ),
        out_specs=(P(("rep", "dp"), None, "tp"), P(("rep", "dp"), None)),
        check_vma=False,
    )
```

```python
import functools
import math

import jax
import jax.numpy as jnp
from jax import lax
from jax.experimental import pallas as pl
from jax.experimental.pallas import tpu as pltpu
from jax.sharding import PartitionSpec as P

epsilon = 1e-05
modulus = 251


def action_features(action_seeds, action_mean, action_spread):
    harmonic = jnp.arange(1, action_mean.shape[0] + 1, dtype=jnp.int32)
    phases = action_seeds[:, :, None] * harmonic % modulus
    angles = phases.astype(jnp.float32) * (2.0 * math.pi / modulus)
    return (action_mean + action_spread * jnp.cos(angles)).astype(jnp.bfloat16)


def head_value(output_rows, head_gain, value_weight):
    wide_out = output_rows.astype(jnp.float32)
    scale = lax.rsqrt(jnp.mean(wide_out * wide_out, axis=1) + epsilon)
    return jnp.sum(wide_out * (head_gain * value_weight), axis=1) * scale


def local_gathered(
    state_hidden,
    action_seeds,
    action_mean,
    action_spread,
    action_weight,
    norm_gain,
    gate_weight,
    up_weight,
    down_weight,
    head_gain,
    value_weight,
):
    state_count, cand_count = action_seeds.shape
    row_count = state_count * cand_count
    local_cols = action_weight.shape[1]
    features = action_features(action_seeds, action_mean, action_spread)
    embedded = jnp.dot(
        features.reshape(row_count, features.shape[2]),
        action_weight,
        preferred_element_type=jnp.float32,
    )
    inputs_local = (
        (
            state_hidden.astype(jnp.float32)[:, None, :]
            + embedded.reshape(state_count, cand_count, local_cols)
        )
        .reshape(row_count, local_cols)
        .astype(jnp.bfloat16)
    )
    gathered, gain_full = (
        lax.all_gather(inputs_local, "tp", axis=1, tiled=True),
        lax.all_gather(norm_gain.astype(jnp.bfloat16), "tp", axis=0, tiled=True).astype(
            norm_gain.dtype
        ),
    )
    scale = lax.rsqrt(
        jnp.mean(jnp.square(gathered.astype(jnp.float32)), axis=1, keepdims=True) + epsilon
    )
    normed = (gathered.astype(jnp.float32) * scale * gain_full).astype(jnp.bfloat16)
    gate_sum = jnp.dot(
        normed,
        lax.all_gather(gate_weight, "dp", axis=0, tiled=True),
        preferred_element_type=jnp.float32,
    )
    up_sum = jnp.dot(
        normed,
        lax.all_gather(up_weight, "dp", axis=0, tiled=True),
        preferred_element_type=jnp.float32,
    )
    hidden = (jax.nn.silu(gate_sum) * up_sum).astype(jnp.bfloat16)
    partial_terms = jnp.dot(
        hidden,
        lax.all_gather(down_weight, "dp", axis=1, tiled=True),
        preferred_element_type=jnp.float32,
    )
    summed_local = lax.psum_scatter(partial_terms, "tp", scatter_dimension=1, tiled=True)
    output_local = (inputs_local.astype(jnp.float32) + summed_local).astype(jnp.bfloat16)
    output_full, head_full, value_full = (
        lax.all_gather(output_local, "tp", axis=1, tiled=True),
        lax.all_gather(head_gain.astype(jnp.bfloat16), "tp", axis=0, tiled=True).astype(
            head_gain.dtype
        ),
        lax.all_gather(value_weight.astype(jnp.bfloat16), "tp", axis=0, tiled=True).astype(
            value_weight.dtype
        ),
    )
    values = head_value(output_full, head_full, value_full)
    return (
        output_local.reshape(state_count, cand_count, local_cols),
        values.reshape(state_count, cand_count),
    )


TP = 8
SMALL = 16
MIB = 1024 * 1024


def send(array, pairs):
    return lax.ppermute(
        array, ("tp", "dp"), [(2 * st + sd, 2 * dt + dd) for (st, sd), (dt, dd) in pairs]
    )


SPLIT = 8


def stage(which, loads, ins, outs, compute, scratch=(), limit=3, flops=0, alias=None, manual=False):
    vmem = pl.BlockSpec(memory_space=pltpu.VMEM)
    count = len(ins)
    shapes, sources, flat = list(outs), [], []
    for kind, parts in loads:
        array, total = parts[0][0], sum(part[4] for part in parts)
        shape = (total, array.shape[1]) if kind == "rows" else (array.shape[0], total)
        shapes.append(jax.ShapeDtypeStruct(shape, array.dtype))
        sources += [part[0] for part in parts]
        flat.append((kind, parts))
    n = len(sources)

    def body(which_ref, *refs):
        inputs = refs[n : n + count]
        results = refs[n + count : n + count + len(outs)]
        targets = refs[n + count + len(outs) : n + count + len(shapes)]
        extra = refs[n + count + len(shapes) :]
        made, at = [], 0
        for (kind, parts), target in zip(flat, targets):
            filled = 0
            for _, place, unit, offset, size in parts:
                block = which_ref[place] * unit + offset
                length = size if kind == "rows" else target.shape[0]
                piece = length // SPLIT
                for cut in range(SPLIT):
                    if kind == "rows":
                        begin = pl.multiple_of(block + cut * piece, 16)
                        view = refs[at].at[pl.ds(begin, piece), :]
                        to = target.at[pl.ds(filled + cut * piece, piece), :]
                    else:
                        rows = pl.ds(cut * piece, piece)
                        view = refs[at].at[rows, pl.ds(pl.multiple_of(block, 128), size)]
                        to = target.at[rows, pl.ds(filled, size)]
                    made.append(pltpu.make_async_copy(view, to, extra[0].at[len(made)]))
                filled += size
                at += 1
        for copy in made:
            copy.start()
        waited = []

        def wait():
            if not waited:
                waited.append(True)
                for copy in made:
                    copy.wait()

        if manual:
            compute(inputs, results, extra, list(targets), wait)
        elif compute is not None:
            compute(inputs, results, extra[1:] if n else extra)
        wait()

    loaded = sum(2 * math.prod(shape.shape) for shape in shapes[len(outs) :])
    return pl.pallas_call(
        body,
        out_shape=shapes,
        in_specs=[pl.BlockSpec(memory_space=pltpu.SMEM)]
        + [pl.BlockSpec(memory_space=pl.ANY)] * n
        + [vmem] * count,
        out_specs=[vmem] * len(shapes),
        scratch_shapes=([pltpu.SemaphoreType.DMA((n * SPLIT,))] if n else []) + list(scratch),
        input_output_aliases={} if alias is None else {1 + n + alias: 0},
        compiler_params=pltpu.CompilerParams(vmem_limit_bytes=limit * MIB),
        cost_estimate=pl.CostEstimate(flops=flops, bytes_accessed=loaded, transcendentals=0),
    )(which, *sources, *ins)


def to_row(column):
    size = column.shape[0]
    rows = lax.broadcasted_iota(jnp.int32, (size, size), 0)
    cols = lax.broadcasted_iota(jnp.int32, (size, size), 1)
    return jnp.sum(jnp.where(rows == cols, column, 0.0), axis=0, keepdims=True)


def to_column(row):
    size = row.shape[1]
    rows = lax.broadcasted_iota(jnp.int32, (size, size), 0)
    cols = lax.broadcasted_iota(jnp.int32, (size, size), 1)
    return jnp.sum(jnp.where(rows == cols, row, 0.0), axis=1, keepdims=True)


def basis_stage(which, loads, blocks, held, before, columns, features, squares, narrow):
    m, k = blocks[0].shape
    count = len(blocks)
    start, stop = columns
    width = stop - start
    tile = 512
    ins = [*blocks, *held] + ([] if before is None else [before])
    summed = squares is not None
    if summed:
        ins += [features] + squares
        rows = features.shape[0]
    outs = [jax.ShapeDtypeStruct((2, m, width), jnp.float32)]
    if narrow:
        outs.append(jax.ShapeDtypeStruct((2, m, width), jnp.bfloat16))
    if summed:
        outs.append(jax.ShapeDtypeStruct((rows, 128), jnp.float32))

    def compute(inputs, results, extra):
        refs, weights = inputs[:count], inputs[count : 3 * count]
        rest = list(inputs[3 * count :])
        lhs = extra[0]
        old = rest.pop(0) if before is not None else None
        for index, ref in enumerate(refs):
            gain = ref[m - SMALL + 4 : m - SMALL + 5, :].astype(jnp.float32)
            lhs[index] = (ref[...].astype(jnp.float32) * gain).astype(jnp.bfloat16)

        @pl.loop(0, width // tile)
        def _(j):
            at = pl.ds(pl.multiple_of(start + j * tile, tile), tile)
            to = pl.ds(pl.multiple_of(j * tile, tile), tile)
            for side in range(2):
                total = old[side, :, at] if old is not None else None
                for index in range(count):
                    term = jnp.dot(
                        lhs[index],
                        weights[2 * index + side][:, at],
                        preferred_element_type=jnp.float32,
                    )
                    total = term if total is None else total + term
                results[0][side, :, to] = total
                if narrow:
                    results[1][side, :, to] = total.astype(jnp.bfloat16)

        if summed:
            feature_rows, *parts = rest
            total = None
            for ref in refs:
                wide = jnp.dot(feature_rows[...], ref[...], preferred_element_type=jnp.float32)
                wide = wide.astype(jnp.bfloat16).astype(jnp.float32)
                wide = wide * wide
                for at in range(0, k, 128):
                    piece = wide[:, at : at + 128]
                    total = piece if total is None else total + piece
            for part in parts:
                total = total + part[...]
            results[-1][...] = total
            if narrow:
                row = to_row(jnp.sum(total, axis=1, keepdims=True))
                high = row.astype(jnp.bfloat16).astype(jnp.float32)
                last = results[1][0, m - SMALL :, :rows].astype(jnp.float32)
                line = lax.broadcasted_iota(jnp.int32, last.shape, 0)
                last = jnp.where(line == SMALL - 2, high, last)
                last = jnp.where(line == SMALL - 1, row - high, last)
                results[1][0, m - SMALL :, :rows] = last.astype(jnp.bfloat16)

    return stage(
        which,
        loads,
        ins,
        outs,
        compute,
        [pltpu.VMEM((count, m, k), jnp.bfloat16)],
        flops=4 * m * k * width * count,
        alias=None if before is None or narrow else 3 * count,
    )


def hidden_stage(which, loads, own, other, features, square, scale, width):
    _, m, units = own.shape
    rows = features.shape[0]
    tile = 512
    first = scale is None
    outs = [jax.ShapeDtypeStruct((rows, units), jnp.bfloat16)]
    if first:
        outs.append(jax.ShapeDtypeStruct((rows, 128), jnp.float32))

    def compute(inputs, results, extra):
        own, other, features, last = inputs
        if first:
            lines = other[0, m - SMALL :, :rows].astype(jnp.float32)
            row = lines[SMALL - 2 : SMALL - 1] + lines[SMALL - 1 :]
            squares = jnp.sum(last[...], axis=1, keepdims=True) + to_column(row)
            factor = lax.rsqrt(squares / width + epsilon)
            results[1][...] = jnp.broadcast_to(factor, results[1].shape)
        else:
            factor = last[:, :1]

        @pl.loop(0, units // tile)
        def _(j):
            at = pl.ds(pl.multiple_of(j * tile, tile), tile)
            sums = []
            for side in range(2):
                basis = own[side, :, at] + other[side, :, at].astype(jnp.float32)
                sums.append(
                    factor
                    * jnp.dot(
                        features[...],
                        basis.astype(jnp.bfloat16),
                        preferred_element_type=jnp.float32,
                    )
                )
            gate, up = sums
            results[0][:, at] = (gate / (1.0 + jnp.exp(-gate)) * up).astype(jnp.bfloat16)

    return stage(
        which,
        loads,
        [own, other, features, square if first else scale],
        outs,
        compute,
        flops=4 * m * rows * units,
    )


def down_stage(which, loads, hidden, weights, tile, places, widths, copies=()):
    rows = hidden[0].shape[0]
    depth = weights[0].shape[0]
    half = rows // 2
    flops = sum(2 * len(r) * half * depth * tile * len(tiles) for r, tiles, _ in places)
    counts = (len(hidden), len(weights))

    def compute(inputs, results, extra, loaded, wait):
        hidden = inputs[: counts[0]]
        weights = list(inputs[counts[0] : sum(counts)])
        sources = inputs[sum(counts) :]
        for parts, tiles, targets in places:
            low, high = parts[0] * half, parts[-1] * half + half
            for j, (index, at) in enumerate(tiles):
                if index == len(weights):
                    wait()
                    weights += loaded
                total = None
                depth_at = 0
                for ref in hidden:
                    size = ref.shape[1]
                    term = jnp.dot(
                        ref[low:high, :],
                        weights[index][depth_at : depth_at + size, at : at + tile],
                        preferred_element_type=jnp.float32,
                    )
                    total = term if total is None else total + term
                    depth_at += size
                total = total.astype(jnp.bfloat16)
                for part, (out, column) in enumerate(targets):
                    to = column + j * tile
                    results[out][:, to : to + tile] = total[part * half : (part + 1) * half]
        for source, (_, out) in zip(sources, copies):
            results[out][:, : source.shape[1]] = source[...]

    return stage(
        which,
        loads,
        [*hidden, *weights, *[copy[0] for copy in copies]],
        [jax.ShapeDtypeStruct((half, width), jnp.bfloat16) for width in widths],
        compute,
        limit=6,
        flops=flops // 16,
        manual=True,
    )


def piece_body(flags, weight, states, gain, seeds, piece, rows):
    half = weight.shape[0] // 2
    count = states.shape[0]
    piece[:half, :] = weight[pl.ds(pl.multiple_of(flags[4] * half, 16), half), :]
    rows[...] = jnp.zeros_like(rows)
    rows[:count, :] = states[...].astype(jnp.float32)
    rows[count : count + 1, :] = gain[...].reshape(1, -1)
    high = lax.shift_right_logical(seeds[...], 8)
    low = seeds[...] - high * 256
    width = seeds.shape[1]
    rows[count + 1 : 2 * count + 1, :width] = high.astype(jnp.float32)
    rows[2 * count + 1 : 3 * count + 1, :width] = low.astype(jnp.float32)
    piece[half:, :] = rows[...].astype(jnp.bfloat16)


def block_body(count, cands, flags, piece, first, second, weight, states, mean, spread, gain, value,
               block, features, inputs, head, rows):
    f32, bf16 = jnp.float32, jnp.bfloat16
    half = weight.shape[0] // 2
    act = weight.shape[0]
    lower, home = flags[4] == 0, flags[5] == 1
    same = jnp.where(home, piece[...], first[...])
    other = jnp.where(home, first[...], second[...])
    low = jnp.where(lower, same, other)
    high = jnp.where(lower, other, same)
    block[:half, :] = low[:half]
    block[half:act, :] = high[:half]
    parts = [low[half:].astype(f32), high[half:].astype(f32)]
    rows[...] = jnp.zeros_like(rows)
    for index, part in enumerate(parts):
        rows[index * count : (index + 1) * count, :] = part[:count]
    rows[2 * count : 2 * count + 1, :] = parts[0][count : count + 1]
    block[act:, :] = rows[...].astype(bf16)

    harmonic = (lax.broadcasted_iota(jnp.int32, (cands, act), 1) + 1).astype(f32)
    diagonal = lax.broadcasted_iota(jnp.int32, (cands, cands), 0) == lax.broadcasted_iota(
        jnp.int32, (cands, cands), 1
    )
    states_at = lax.broadcasted_iota(jnp.int32, (cands, SMALL), 1)
    made = []
    for state in range(2 * count):
        part, at = parts[state // count], state % count
        seed = (
            part[count + 1 + at : count + 2 + at, :cands] * 256.0
            + part[2 * count + 1 + at : 2 * count + 2 + at, :cands]
        )
        column = jnp.sum(jnp.where(diagonal, seed, 0.0), axis=1, keepdims=True)
        product = column * harmonic
        rest = product - modulus * jnp.floor(product * (1.0 / modulus))
        rest = jnp.where(rest < 0.0, rest + modulus, rest)
        rest = jnp.where(rest >= modulus, rest - modulus, rest)
        wave = jnp.cos(rest * (2.0 * math.pi / modulus))
        value_rows = (mean[...].reshape(1, -1) + spread[...].reshape(1, -1) * wave).astype(bf16)
        made.append(value_rows)
        to = slice(state * cands, (state + 1) * cands)
        features[to, :act] = value_rows
        features[to, act:] = (states_at == state).astype(f32).astype(bf16)
    for at in range(count):
        own = jnp.where(lower, made[at], made[count + at])
        wide = jnp.dot(own, weight[...], preferred_element_type=f32)
        wide = wide + states[at : at + 1, :].astype(f32)
        inputs[at * cands : (at + 1) * cands, :] = wide.astype(bf16)
    head[...] = (gain[...] * value[...]).reshape(1, -1)


def whole_call(body, outs, scratch, after, *operands):
    whole = lambda array: pl.BlockSpec(array.shape, lambda i: (0,) * len(array.shape))
    count = len(after)
    return pl.pallas_call(
        lambda *refs: body(refs[count], *refs[count + 1 :]),
        out_shape=outs,
        grid=(1,),
        in_specs=[pl.BlockSpec(memory_space=pl.ANY)] * count
        + [pl.BlockSpec(memory_space=pltpu.SMEM)]
        + [whole(array) for array in operands[1:]],
        out_specs=[whole(array) for array in outs],
        scratch_shapes=scratch,
        compiler_params=pltpu.CompilerParams(vmem_limit_bytes=6 * MIB),
        cost_estimate=pl.CostEstimate(flops=1000000, bytes_accessed=1000000, transcendentals=0),
    )(*after, *operands)


def local_blocks(
    state_hidden,
    action_seeds,
    action_mean,
    action_spread,
    action_weight,
    norm_gain,
    gate_weight,
    up_weight,
    down_weight,
    head_gain,
    value_weight,
):
    f32, bf16 = jnp.float32, jnp.bfloat16
    states, cands = action_seeds.shape
    rows = states * cands
    act, cols = action_weight.shape
    half = act // 2
    units = gate_weight.shape[1]
    full_width = gate_weight.shape[0] * 2
    tp, dp = lax.axis_index("tp"), lax.axis_index("dp")
    home = tp // 4 == dp
    place = tp % 4
    every = [(t, d) for t in range(TP) for d in range(2)]
    swap_core = [((t, d), (t, 1 - d)) for t, d in every]

    flags = jnp.stack([place, place ^ 1, place ^ 2, place ^ 3, dp, home.astype(jnp.int32)])
    flags = flags.astype(jnp.int32)
    out = jax.ShapeDtypeStruct
    (piece,) = whole_call(
        piece_body,
        [out((half + SMALL, cols), bf16)],
        [pltpu.VMEM((SMALL, cols), f32)],
        [],
        flags,
        *[
            pltpu.with_memory_space_constraint(array, pltpu.HBM)
            for array in (action_weight, state_hidden, norm_gain, action_seeds)
        ],
    )

    first = send(
        piece,
        [((t, t // 4), (t ^ 4, t // 4)) for t in range(TP)]
        + [((t, 1 - t // 4), (t, t // 4)) for t in range(TP)],
    )
    second = send(piece, [((t, 1 - t // 4), (t ^ 4, t // 4)) for t in range(TP)])

    gate_weight, up_weight, down_weight = (
        pltpu.with_memory_space_constraint(weight, pltpu.HBM)
        for weight in (gate_weight, up_weight, down_weight)
    )
    pair = lambda k: [("rows", [(w, k, cols, 0, cols)]) for w in (gate_weight, up_weight)]
    column = lambda k: ("cols", [(down_weight, k, cols, 0, cols)])
    tile = cols // 2
    held = stage(flags, pair(0), [], [], None)

    block, features, inputs_local, head = whole_call(
        functools.partial(block_body, states, cands),
        [
            out((act + SMALL, cols), bf16),
            out((2 * rows, act + SMALL), bf16),
            out((rows, cols), bf16),
            out((1, cols), f32),
        ],
        [pltpu.VMEM((SMALL, cols), f32)],
        held,
        flags,
        piece,
        first,
        second,
        action_weight,
        state_hidden,
        action_mean,
        action_spread,
        head_gain,
        value_weight,
    )

    step = lambda array, k: send(array, [((t, d), (t ^ k, d)) for t, d in every])
    near = {k: step(block, k) for k in (2, 1, 3)}

    span = (0, units)
    basis, square, *held = basis_stage(
        flags, pair(2), [block], held, None, span, features, [], False
    )
    basis, square, *held = basis_stage(
        flags, pair(1), [near[2]], held, basis, span, features, [square], False
    )
    basis, square, *held = basis_stage(
        flags, pair(3), [near[1]], held, basis, span, features, [square], False
    )
    cut = units // 2
    own_a, narrow_a, square, down_diagonal = basis_stage(
        flags, [column(3)], [near[3]], held, basis, (0, cut), features, [square], True
    )
    other_a = send(narrow_a, swap_core)
    own_b, narrow_b, down_x = basis_stage(
        flags, [column(1)], [near[3]], held, basis, (cut, units), features, None, True
    )
    other_b = send(narrow_b, swap_core)
    hidden_a, scale = hidden_stage(
        flags, [], own_a, other_a, features, square, None, full_width
    )
    (hidden_b,) = hidden_stage(flags, [], own_b, other_b, features, None, scale, full_width)
    hidden = [hidden_a, hidden_b]

    both, lower, upper = (0, 1), (0,), (1,)
    x_pair, diagonal_upper, down_z = down_stage(
        flags,
        [column(2)],
        hidden,
        [down_diagonal, down_x],
        tile,
        [
            (both, [(0, 0), (0, tile)], [(0, 0), (1, 0)]),
            (lower, [(1, 0), (1, tile)], [(0, cols)]),
        ],
        [2 * cols, cols],
    )
    got_x = step(x_pair, 1)
    (z_pair,) = down_stage(
        flags,
        [],
        hidden,
        [down_z],
        tile,
        [(upper, [(0, 0), (0, tile)], [(0, cols)])],
        [2 * cols],
        [(diagonal_upper, 0)],
    )
    got_z = step(z_pair, 2)
    z_lower, x_upper, own_lower, own_upper, _ = down_stage(
        flags,
        [column(0)],
        hidden,
        [down_z, down_x],
        tile,
        [
            (lower, [(0, 0), (0, tile)], [(0, 0)]),
            (upper, [(1, 0), (1, tile)], [(1, 0)]),
            (both, [(2, 0), (2, tile)], [(2, 0), (3, 0)]),
        ],
        [cols] * 4,
    )
    add = lambda *parts: sum(part.astype(f32) for part in parts).astype(bf16)
    got_lower = step(add(z_lower, got_x[:, :cols]), 2)
    got_upper = step(add(x_upper, got_z[:, :cols]), 1)
    sums = [
        lax.optimization_barrier(add(own_lower, got_x[:, cols:], got_lower)),
        lax.optimization_barrier(add(own_upper, got_z[:, cols:], got_upper)),
    ]
    far = [
        send(sums[part], [((t, 1 - t // 4), (t ^ 4, part)) for t in range(TP)])
        for part in range(2)
    ]
    crossed = send(
        jnp.where(dp == 0, sums[1], sums[0]), [((t, t // 4), (t, 1 - t // 4)) for t in range(TP)]
    )
    mine = jnp.where(home, jnp.where(dp == 0, sums[0], sums[1]), crossed).astype(f32)
    summed = mine + jnp.where(dp == 0, far[0], far[1]).astype(f32)
    output_local = (inputs_local.astype(f32) + summed).astype(bf16)

    wide_out = output_local.astype(f32)
    totals = jnp.stack(
        [
            jnp.sum(wide_out * wide_out, axis=1),
            jnp.sum(wide_out * head, axis=1),
        ]
    )
    for k in (1, 2, 4):
        totals = totals + step(totals, k)
    values = totals[1] * lax.rsqrt(totals[0] / full_width + epsilon)
    return (
        output_local.reshape(states, cands, cols),
        values.reshape(states, cands),
    )


def solution(mesh):
    local = local_blocks if mesh.shape["tp"] == TP and mesh.shape["dp"] == 2 else local_gathered
    return jax.shard_map(
        local,
        mesh=mesh,
        in_specs=(
            P(("rep", "dp"), "tp"),
            P(("rep", "dp"), None),
            P("rep"),
            P("rep"),
            P(None, "tp"),
            P("tp"),
            P("dp", "tp"),
            P("dp", "tp"),
            P("tp", "dp"),
            P("tp"),
            P("tp"),
        ),
        out_specs=(P(("rep", "dp"), None, "tp"), P(("rep", "dp"), None)),
        check_vma=False,
    )
```

```python
import functools
import math

import jax
import jax.numpy as jnp
from jax import lax
from jax.experimental import pallas as pl
from jax.experimental.pallas import tpu as pltpu
from jax.sharding import PartitionSpec as P

epsilon = 1e-05
modulus = 251


def action_features(action_seeds, action_mean, action_spread):
    harmonic = jnp.arange(1, action_mean.shape[0] + 1, dtype=jnp.int32)
    phases = action_seeds[:, :, None] * harmonic % modulus
    angles = phases.astype(jnp.float32) * (2.0 * math.pi / modulus)
    return (action_mean + action_spread * jnp.cos(angles)).astype(jnp.bfloat16)


def head_value(output_rows, head_gain, value_weight):
    wide_out = output_rows.astype(jnp.float32)
    scale = lax.rsqrt(jnp.mean(wide_out * wide_out, axis=1) + epsilon)
    return jnp.sum(wide_out * (head_gain * value_weight), axis=1) * scale


def local_gathered(
    state_hidden,
    action_seeds,
    action_mean,
    action_spread,
    action_weight,
    norm_gain,
    gate_weight,
    up_weight,
    down_weight,
    head_gain,
    value_weight,
):
    state_count, cand_count = action_seeds.shape
    row_count = state_count * cand_count
    local_cols = action_weight.shape[1]
    features = action_features(action_seeds, action_mean, action_spread)
    embedded = jnp.dot(
        features.reshape(row_count, features.shape[2]),
        action_weight,
        preferred_element_type=jnp.float32,
    )
    inputs_local = (
        (
            state_hidden.astype(jnp.float32)[:, None, :]
            + embedded.reshape(state_count, cand_count, local_cols)
        )
        .reshape(row_count, local_cols)
        .astype(jnp.bfloat16)
    )
    gathered, gain_full = (
        lax.all_gather(inputs_local, "tp", axis=1, tiled=True),
        lax.all_gather(norm_gain.astype(jnp.bfloat16), "tp", axis=0, tiled=True).astype(
            norm_gain.dtype
        ),
    )
    scale = lax.rsqrt(
        jnp.mean(jnp.square(gathered.astype(jnp.float32)), axis=1, keepdims=True) + epsilon
    )
    normed = (gathered.astype(jnp.float32) * scale * gain_full).astype(jnp.bfloat16)
    gate_sum = jnp.dot(
        normed,
        lax.all_gather(gate_weight, "dp", axis=0, tiled=True),
        preferred_element_type=jnp.float32,
    )
    up_sum = jnp.dot(
        normed,
        lax.all_gather(up_weight, "dp", axis=0, tiled=True),
        preferred_element_type=jnp.float32,
    )
    hidden = (jax.nn.silu(gate_sum) * up_sum).astype(jnp.bfloat16)
    partial_terms = jnp.dot(
        hidden,
        lax.all_gather(down_weight, "dp", axis=1, tiled=True),
        preferred_element_type=jnp.float32,
    )
    summed_local = lax.psum_scatter(partial_terms, "tp", scatter_dimension=1, tiled=True)
    output_local = (inputs_local.astype(jnp.float32) + summed_local).astype(jnp.bfloat16)
    output_full, head_full, value_full = (
        lax.all_gather(output_local, "tp", axis=1, tiled=True),
        lax.all_gather(head_gain.astype(jnp.bfloat16), "tp", axis=0, tiled=True).astype(
            head_gain.dtype
        ),
        lax.all_gather(value_weight.astype(jnp.bfloat16), "tp", axis=0, tiled=True).astype(
            value_weight.dtype
        ),
    )
    values = head_value(output_full, head_full, value_full)
    return (
        output_local.reshape(state_count, cand_count, local_cols),
        values.reshape(state_count, cand_count),
    )


TP = 8
SMALL = 16
MIB = 1024 * 1024


def send(array, pairs):
    return lax.ppermute(
        array, ("tp", "dp"), [(2 * st + sd, 2 * dt + dd) for (st, sd), (dt, dd) in pairs]
    )


SPLIT = 8


def near_place(k):
    place = lax.rem(lax.axis_index("tp"), 4)
    if k == 1:
        return place + 1 - 2 * lax.rem(place, 2)
    if k == 2:
        return lax.rem(place + 2, 4)
    return place if k == 0 else 3 - place


def stage(loads, ins, outs, compute, scratch=(), limit=3, flops=0, alias=None, manual=False):
    vmem = pl.BlockSpec(memory_space=pltpu.VMEM)
    count = len(ins)
    shapes, sources, flat = list(outs), [], []
    for kind, parts in loads:
        array, total = parts[0][0], sum(part[4] for part in parts)
        shape = (total, array.shape[1]) if kind == "rows" else (array.shape[0], total)
        shapes.append(jax.ShapeDtypeStruct(shape, array.dtype))
        sources += [part[0] for part in parts]
        flat.append((kind, parts))
    n = len(sources)

    def body(*refs):
        inputs = refs[n : n + count]
        results = refs[n + count : n + count + len(outs)]
        targets = refs[n + count + len(outs) : n + count + len(shapes)]
        extra = refs[n + count + len(shapes) :]
        made, at = [], 0
        for (kind, parts), target in zip(flat, targets):
            filled = 0
            for _, place, unit, offset, size in parts:
                block = near_place(place) * unit + offset
                length = size if kind == "rows" else target.shape[0]
                piece = length // SPLIT
                for cut in range(SPLIT):
                    if kind == "rows":
                        begin = pl.multiple_of(block + cut * piece, 16)
                        view = refs[at].at[pl.ds(begin, piece), :]
                        to = target.at[pl.ds(filled + cut * piece, piece), :]
                    else:
                        rows = pl.ds(cut * piece, piece)
                        view = refs[at].at[rows, pl.ds(pl.multiple_of(block, 128), size)]
                        to = target.at[rows, pl.ds(filled, size)]
                    made.append(pltpu.make_async_copy(view, to, extra[0].at[len(made)]))
                filled += size
                at += 1
        for copy in made:
            copy.start()
        waited = []

        def wait():
            if not waited:
                waited.append(True)
                for copy in made:
                    copy.wait()

        if manual:
            compute(inputs, results, extra, list(targets), wait)
        elif compute is not None:
            compute(inputs, results, extra[1:] if n else extra)
        wait()

    loaded = sum(2 * math.prod(shape.shape) for shape in shapes[len(outs) :])
    return pl.pallas_call(
        body,
        out_shape=shapes,
        in_specs=[pl.BlockSpec(memory_space=pl.ANY)] * n + [vmem] * count,
        out_specs=[vmem] * len(shapes),
        scratch_shapes=([pltpu.SemaphoreType.DMA((n * SPLIT,))] if n else []) + list(scratch),
        input_output_aliases={} if alias is None else {n + alias: 0},
        compiler_params=pltpu.CompilerParams(vmem_limit_bytes=limit * MIB),
        cost_estimate=pl.CostEstimate(flops=flops, bytes_accessed=loaded, transcendentals=0),
    )(*sources, *ins)


def to_row(column):
    size = column.shape[0]
    rows = lax.broadcasted_iota(jnp.int32, (size, size), 0)
    cols = lax.broadcasted_iota(jnp.int32, (size, size), 1)
    return jnp.sum(jnp.where(rows == cols, column, 0.0), axis=0, keepdims=True)


def to_column(row):
    size = row.shape[1]
    rows = lax.broadcasted_iota(jnp.int32, (size, size), 0)
    cols = lax.broadcasted_iota(jnp.int32, (size, size), 1)
    return jnp.sum(jnp.where(rows == cols, row, 0.0), axis=1, keepdims=True)


def basis_stage(loads, blocks, held, before, columns, features, squares, narrow):
    m, k = blocks[0].shape
    count = len(blocks)
    start, stop = columns
    width = stop - start
    tile = 512
    ins = [*blocks, *held] + ([] if before is None else [before])
    summed = squares is not None
    if summed:
        ins += [features] + squares
        rows = features.shape[0]
    outs = [jax.ShapeDtypeStruct((2, m, width), jnp.float32)]
    if narrow:
        outs.append(jax.ShapeDtypeStruct((2, m, width), jnp.bfloat16))
    if summed:
        outs.append(jax.ShapeDtypeStruct((rows, 128), jnp.float32))

    def compute(inputs, results, extra):
        refs, weights = inputs[:count], inputs[count : 3 * count]
        rest = list(inputs[3 * count :])
        lhs = extra[0]
        old = rest.pop(0) if before is not None else None
        for index, ref in enumerate(refs):
            gain = ref[m - SMALL + 4 : m - SMALL + 5, :].astype(jnp.float32)
            lhs[index] = (ref[...].astype(jnp.float32) * gain).astype(jnp.bfloat16)

        @pl.loop(0, width // tile)
        def _(j):
            at = pl.ds(pl.multiple_of(start + j * tile, tile), tile)
            to = pl.ds(pl.multiple_of(j * tile, tile), tile)
            for side in range(2):
                total = old[side, :, at] if old is not None else None
                for index in range(count):
                    term = jnp.dot(
                        lhs[index],
                        weights[2 * index + side][:, at],
                        preferred_element_type=jnp.float32,
                    )
                    total = term if total is None else total + term
                results[0][side, :, to] = total
                if narrow:
                    results[1][side, :, to] = total.astype(jnp.bfloat16)

        if summed:
            feature_rows, *parts = rest
            total = None
            for ref in refs:
                wide = jnp.dot(feature_rows[...], ref[...], preferred_element_type=jnp.float32)
                wide = wide.astype(jnp.bfloat16).astype(jnp.float32)
                wide = wide * wide
                for at in range(0, k, 128):
                    piece = wide[:, at : at + 128]
                    total = piece if total is None else total + piece
            for part in parts:
                total = total + part[...]
            results[-1][...] = total
            if narrow:
                row = to_row(jnp.sum(total, axis=1, keepdims=True))
                high = row.astype(jnp.bfloat16).astype(jnp.float32)
                last = results[1][0, m - SMALL :, :rows].astype(jnp.float32)
                line = lax.broadcasted_iota(jnp.int32, last.shape, 0)
                last = jnp.where(line == SMALL - 2, high, last)
                last = jnp.where(line == SMALL - 1, row - high, last)
                results[1][0, m - SMALL :, :rows] = last.astype(jnp.bfloat16)

    return stage(
        loads,
        ins,
        outs,
        compute,
        [pltpu.VMEM((count, m, k), jnp.bfloat16)],
        flops=4 * m * k * width * count,
        alias=None if before is None or narrow else 3 * count,
    )


def hidden_stage(loads, own, other, features, square, scale, width):
    _, m, units = own.shape
    rows = features.shape[0]
    tile = 512
    first = scale is None
    outs = [jax.ShapeDtypeStruct((rows, units), jnp.bfloat16)]
    if first:
        outs.append(jax.ShapeDtypeStruct((rows, 128), jnp.float32))

    def compute(inputs, results, extra):
        own, other, features, last = inputs
        if first:
            lines = other[0, m - SMALL :, :rows].astype(jnp.float32)
            row = lines[SMALL - 2 : SMALL - 1] + lines[SMALL - 1 :]
            squares = jnp.sum(last[...], axis=1, keepdims=True) + to_column(row)
            factor = lax.rsqrt(squares / width + epsilon)
            results[1][...] = jnp.broadcast_to(factor, results[1].shape)
        else:
            factor = last[:, :1]

        @pl.loop(0, units // tile)
        def _(j):
            at = pl.ds(pl.multiple_of(j * tile, tile), tile)
            sums = []
            for side in range(2):
                basis = own[side, :, at] + other[side, :, at].astype(jnp.float32)
                sums.append(
                    factor
                    * jnp.dot(
                        features[...],
                        basis.astype(jnp.bfloat16),
                        preferred_element_type=jnp.float32,
                    )
                )
            gate, up = sums
            results[0][:, at] = (gate / (1.0 + jnp.exp(-gate)) * up).astype(jnp.bfloat16)

    return stage(
        loads,
        [own, other, features, square if first else scale],
        outs,
        compute,
        flops=4 * m * rows * units,
    )


def down_stage(loads, hidden, weights, tile, places, widths, copies=()):
    rows = hidden[0].shape[0]
    depth = weights[0].shape[0]
    half = rows // 2
    flops = sum(2 * len(r) * half * depth * tile * len(tiles) for r, tiles, _ in places)
    counts = (len(hidden), len(weights))

    def compute(inputs, results, extra, loaded, wait):
        hidden = inputs[: counts[0]]
        weights = list(inputs[counts[0] : sum(counts)])
        sources = inputs[sum(counts) :]
        for parts, tiles, targets in places:
            low, high = parts[0] * half, parts[-1] * half + half
            for j, (index, at) in enumerate(tiles):
                if index == len(weights):
                    wait()
                    weights += loaded
                total = None
                depth_at = 0
                for ref in hidden:
                    size = ref.shape[1]
                    term = jnp.dot(
                        ref[low:high, :],
                        weights[index][depth_at : depth_at + size, at : at + tile],
                        preferred_element_type=jnp.float32,
                    )
                    total = term if total is None else total + term
                    depth_at += size
                total = total.astype(jnp.bfloat16)
                for part, (out, column) in enumerate(targets):
                    to = column + j * tile
                    results[out][:, to : to + tile] = total[part * half : (part + 1) * half]
        for source, (_, out) in zip(sources, copies):
            results[out][:, : source.shape[1]] = source[...]

    return stage(
        loads,
        [*hidden, *weights, *[copy[0] for copy in copies]],
        [jax.ShapeDtypeStruct((half, width), jnp.bfloat16) for width in widths],
        compute,
        limit=6,
        flops=flops // 16,
        manual=True,
    )


def piece_body(weight, states, gain, seeds, piece, rows):
    half = weight.shape[0] // 2
    count = states.shape[0]
    piece[:half, :] = weight[pl.ds(pl.multiple_of(lax.axis_index("dp") * half, 16), half), :]
    rows[...] = jnp.zeros_like(rows)
    rows[:count, :] = states[...].astype(jnp.float32)
    rows[count : count + 1, :] = gain[...].reshape(1, -1)
    high = lax.shift_right_logical(seeds[...], 8)
    low = seeds[...] - high * 256
    width = seeds.shape[1]
    rows[count + 1 : 2 * count + 1, :width] = high.astype(jnp.float32)
    rows[2 * count + 1 : 3 * count + 1, :width] = low.astype(jnp.float32)
    piece[half:, :] = rows[...].astype(jnp.bfloat16)


def block_body(count, cands, piece, first, second, weight, states, mean, spread, gain, value,
               block, features, inputs, head, rows):
    f32, bf16 = jnp.float32, jnp.bfloat16
    half = weight.shape[0] // 2
    act = weight.shape[0]
    core = lax.axis_index("dp")
    lower = core == 0
    home = lax.div(lax.axis_index("tp"), 4) == core
    same = jnp.where(home, piece[...], first[...])
    other = jnp.where(home, first[...], second[...])
    low = jnp.where(lower, same, other)
    high = jnp.where(lower, other, same)
    block[:half, :] = low[:half]
    block[half:act, :] = high[:half]
    parts = [low[half:].astype(f32), high[half:].astype(f32)]
    rows[...] = jnp.zeros_like(rows)
    for index, part in enumerate(parts):
        rows[index * count : (index + 1) * count, :] = part[:count]
    rows[2 * count : 2 * count + 1, :] = parts[0][count : count + 1]
    block[act:, :] = rows[...].astype(bf16)

    harmonic = (lax.broadcasted_iota(jnp.int32, (cands, act), 1) + 1).astype(f32)
    diagonal = lax.broadcasted_iota(jnp.int32, (cands, cands), 0) == lax.broadcasted_iota(
        jnp.int32, (cands, cands), 1
    )
    states_at = lax.broadcasted_iota(jnp.int32, (cands, SMALL), 1)
    made = []
    for state in range(2 * count):
        part, at = parts[state // count], state % count
        seed = (
            part[count + 1 + at : count + 2 + at, :cands] * 256.0
            + part[2 * count + 1 + at : 2 * count + 2 + at, :cands]
        )
        column = jnp.sum(jnp.where(diagonal, seed, 0.0), axis=1, keepdims=True)
        product = column * harmonic
        rest = product - modulus * jnp.floor(product * (1.0 / modulus))
        rest = jnp.where(rest < 0.0, rest + modulus, rest)
        rest = jnp.where(rest >= modulus, rest - modulus, rest)
        wave = jnp.cos(rest * (2.0 * math.pi / modulus))
        value_rows = (mean[...].reshape(1, -1) + spread[...].reshape(1, -1) * wave).astype(bf16)
        made.append(value_rows)
        to = slice(state * cands, (state + 1) * cands)
        features[to, :act] = value_rows
        features[to, act:] = (states_at == state).astype(f32).astype(bf16)
    for at in range(count):
        own = jnp.where(lower, made[at], made[count + at])
        wide = jnp.dot(own, weight[...], preferred_element_type=f32)
        wide = wide + states[at : at + 1, :].astype(f32)
        inputs[at * cands : (at + 1) * cands, :] = wide.astype(bf16)
    head[...] = (gain[...] * value[...]).reshape(1, -1)


def whole_call(body, outs, scratch, after, *operands):
    whole = lambda array: pl.BlockSpec(array.shape, lambda i: (0,) * len(array.shape))
    count = len(after)
    return pl.pallas_call(
        lambda *refs: body(*refs[count:]),
        out_shape=outs,
        grid=(1,),
        in_specs=[pl.BlockSpec(memory_space=pl.ANY)] * count
        + [whole(array) for array in operands],
        out_specs=[whole(array) for array in outs],
        scratch_shapes=scratch,
        compiler_params=pltpu.CompilerParams(vmem_limit_bytes=6 * MIB),
        cost_estimate=pl.CostEstimate(flops=1000000, bytes_accessed=1000000, transcendentals=0),
    )(*after, *operands)


def local_blocks(
    state_hidden,
    action_seeds,
    action_mean,
    action_spread,
    action_weight,
    norm_gain,
    gate_weight,
    up_weight,
    down_weight,
    head_gain,
    value_weight,
):
    f32, bf16 = jnp.float32, jnp.bfloat16
    states, cands = action_seeds.shape
    rows = states * cands
    act, cols = action_weight.shape
    half = act // 2
    units = gate_weight.shape[1]
    full_width = gate_weight.shape[0] * 2
    tp, dp = lax.axis_index("tp"), lax.axis_index("dp")
    home = tp // 4 == dp
    every = [(t, d) for t in range(TP) for d in range(2)]
    swap_core = [((t, d), (t, 1 - d)) for t, d in every]

    out = jax.ShapeDtypeStruct
    (piece,) = whole_call(
        piece_body,
        [out((half + SMALL, cols), bf16)],
        [pltpu.VMEM((SMALL, cols), f32)],
        [],
        *[
            pltpu.with_memory_space_constraint(array, pltpu.HBM)
            for array in (action_weight, state_hidden, norm_gain, action_seeds)
        ],
    )

    first = send(
        piece,
        [((t, t // 4), (t ^ 4, t // 4)) for t in range(TP)]
        + [((t, 1 - t // 4), (t, t // 4)) for t in range(TP)],
    )
    second = send(piece, [((t, 1 - t // 4), (t ^ 4, t // 4)) for t in range(TP)])

    gate_weight, up_weight, down_weight = (
        pltpu.with_memory_space_constraint(weight, pltpu.HBM)
        for weight in (gate_weight, up_weight, down_weight)
    )
    pair = lambda k: [("rows", [(w, k, cols, 0, cols)]) for w in (gate_weight, up_weight)]
    column = lambda k: ("cols", [(down_weight, k, cols, 0, cols)])
    tile = cols // 2
    held = stage(pair(0), [], [], None)

    block, features, inputs_local, head = whole_call(
        functools.partial(block_body, states, cands),
        [
            out((act + SMALL, cols), bf16),
            out((2 * rows, act + SMALL), bf16),
            out((rows, cols), bf16),
            out((1, cols), f32),
        ],
        [pltpu.VMEM((SMALL, cols), f32)],
        held,
        piece,
        first,
        second,
        action_weight,
        state_hidden,
        action_mean,
        action_spread,
        head_gain,
        value_weight,
    )

    step = lambda array, k: send(array, [((t, d), (t ^ k, d)) for t, d in every])
    near = {k: step(block, k) for k in (2, 1, 3)}

    span = (0, units)
    basis, square, *held = basis_stage(
        pair(2), [block], held, None, span, features, [], False
    )
    basis, square, *held = basis_stage(
        pair(1), [near[2]], held, basis, span, features, [square], False
    )
    basis, square, *held = basis_stage(
        pair(3), [near[1]], held, basis, span, features, [square], False
    )
    cut = units // 2
    own_a, narrow_a, square, down_diagonal = basis_stage(
        [column(3)], [near[3]], held, basis, (0, cut), features, [square], True
    )
    other_a = send(narrow_a, swap_core)
    own_b, narrow_b, down_x = basis_stage(
        [column(1)], [near[3]], held, basis, (cut, units), features, None, True
    )
    other_b = send(narrow_b, swap_core)
    hidden_a, scale, down_z = hidden_stage(
        [column(2)], own_a, other_a, features, square, None, full_width
    )
    (hidden_b,) = hidden_stage([], own_b, other_b, features, None, scale, full_width)
    hidden = [hidden_a, hidden_b]

    both, lower, upper = (0, 1), (0,), (1,)
    x_pair, diagonal_upper = down_stage(
        [],
        hidden,
        [down_diagonal, down_x],
        tile,
        [
            (both, [(0, 0), (0, tile)], [(0, 0), (1, 0)]),
            (lower, [(1, 0), (1, tile)], [(0, cols)]),
        ],
        [2 * cols, cols],
    )
    got_x = step(x_pair, 1)
    (z_pair,) = down_stage(
        [],
        hidden,
        [down_z],
        tile,
        [(upper, [(0, 0), (0, tile)], [(0, cols)])],
        [2 * cols],
        [(diagonal_upper, 0)],
    )
    got_z = step(z_pair, 2)
    z_lower, x_upper, own_lower, own_upper, _ = down_stage(
        [column(0)],
        hidden,
        [down_z, down_x],
        tile,
        [
            (lower, [(0, 0), (0, tile)], [(0, 0)]),
            (upper, [(1, 0), (1, tile)], [(1, 0)]),
            (both, [(2, 0), (2, tile)], [(2, 0), (3, 0)]),
        ],
        [cols] * 4,
    )
    add = lambda *parts: sum(part.astype(f32) for part in parts).astype(bf16)
    got_lower = step(add(z_lower, got_x[:, :cols]), 2)
    got_upper = step(add(x_upper, got_z[:, :cols]), 1)
    sums = [
        lax.optimization_barrier(add(own_lower, got_x[:, cols:], got_lower)),
        lax.optimization_barrier(add(own_upper, got_z[:, cols:], got_upper)),
    ]
    far = [
        send(sums[part], [((t, 1 - t // 4), (t ^ 4, part)) for t in range(TP)])
        for part in range(2)
    ]
    crossed = send(
        jnp.where(dp == 0, sums[1], sums[0]), [((t, t // 4), (t, 1 - t // 4)) for t in range(TP)]
    )
    mine = jnp.where(home, jnp.where(dp == 0, sums[0], sums[1]), crossed).astype(f32)
    summed = mine + jnp.where(dp == 0, far[0], far[1]).astype(f32)
    output_local = (inputs_local.astype(f32) + summed).astype(bf16)

    wide_out = output_local.astype(f32)
    totals = jnp.stack(
        [
            jnp.sum(wide_out * wide_out, axis=1),
            jnp.sum(wide_out * head, axis=1),
        ]
    )
    for k in (1, 2, 4):
        totals = totals + step(totals, k)
    values = totals[1] * lax.rsqrt(totals[0] / full_width + epsilon)
    return (
        output_local.reshape(states, cands, cols),
        values.reshape(states, cands),
    )


def solution(mesh):
    local = local_blocks if mesh.shape["tp"] == TP and mesh.shape["dp"] == 2 else local_gathered
    return jax.shard_map(
        local,
        mesh=mesh,
        in_specs=(
            P(("rep", "dp"), "tp"),
            P(("rep", "dp"), None),
            P("rep"),
            P("rep"),
            P(None, "tp"),
            P("tp"),
            P("dp", "tp"),
            P("dp", "tp"),
            P("tp", "dp"),
            P("tp"),
            P("tp"),
        ),
        out_specs=(P(("rep", "dp"), None, "tp"), P(("rep", "dp"), None)),
        check_vma=False,
    )
```

```python
import functools
import math

import jax
import jax.numpy as jnp
from jax import lax
from jax.experimental import pallas as pl
from jax.experimental.pallas import tpu as pltpu
from jax.sharding import PartitionSpec as P

epsilon = 1e-05
modulus = 251


def action_features(action_seeds, action_mean, action_spread):
    harmonic = jnp.arange(1, action_mean.shape[0] + 1, dtype=jnp.int32)
    phases = action_seeds[:, :, None] * harmonic % modulus
    angles = phases.astype(jnp.float32) * (2.0 * math.pi / modulus)
    return (action_mean + action_spread * jnp.cos(angles)).astype(jnp.bfloat16)


def head_value(output_rows, head_gain, value_weight):
    wide_out = output_rows.astype(jnp.float32)
    scale = lax.rsqrt(jnp.mean(wide_out * wide_out, axis=1) + epsilon)
    return jnp.sum(wide_out * (head_gain * value_weight), axis=1) * scale


def local_gathered(
    state_hidden,
    action_seeds,
    action_mean,
    action_spread,
    action_weight,
    norm_gain,
    gate_weight,
    up_weight,
    down_weight,
    head_gain,
    value_weight,
):
    state_count, cand_count = action_seeds.shape
    row_count = state_count * cand_count
    local_cols = action_weight.shape[1]
    features = action_features(action_seeds, action_mean, action_spread)
    embedded = jnp.dot(
        features.reshape(row_count, features.shape[2]),
        action_weight,
        preferred_element_type=jnp.float32,
    )
    inputs_local = (
        (
            state_hidden.astype(jnp.float32)[:, None, :]
            + embedded.reshape(state_count, cand_count, local_cols)
        )
        .reshape(row_count, local_cols)
        .astype(jnp.bfloat16)
    )
    gathered, gain_full = (
        lax.all_gather(inputs_local, "tp", axis=1, tiled=True),
        lax.all_gather(norm_gain.astype(jnp.bfloat16), "tp", axis=0, tiled=True).astype(
            norm_gain.dtype
        ),
    )
    scale = lax.rsqrt(
        jnp.mean(jnp.square(gathered.astype(jnp.float32)), axis=1, keepdims=True) + epsilon
    )
    normed = (gathered.astype(jnp.float32) * scale * gain_full).astype(jnp.bfloat16)
    gate_sum = jnp.dot(
        normed,
        lax.all_gather(gate_weight, "dp", axis=0, tiled=True),
        preferred_element_type=jnp.float32,
    )
    up_sum = jnp.dot(
        normed,
        lax.all_gather(up_weight, "dp", axis=0, tiled=True),
        preferred_element_type=jnp.float32,
    )
    hidden = (jax.nn.silu(gate_sum) * up_sum).astype(jnp.bfloat16)
    partial_terms = jnp.dot(
        hidden,
        lax.all_gather(down_weight, "dp", axis=1, tiled=True),
        preferred_element_type=jnp.float32,
    )
    summed_local = lax.psum_scatter(partial_terms, "tp", scatter_dimension=1, tiled=True)
    output_local = (inputs_local.astype(jnp.float32) + summed_local).astype(jnp.bfloat16)
    output_full, head_full, value_full = (
        lax.all_gather(output_local, "tp", axis=1, tiled=True),
        lax.all_gather(head_gain.astype(jnp.bfloat16), "tp", axis=0, tiled=True).astype(
            head_gain.dtype
        ),
        lax.all_gather(value_weight.astype(jnp.bfloat16), "tp", axis=0, tiled=True).astype(
            value_weight.dtype
        ),
    )
    values = head_value(output_full, head_full, value_full)
    return (
        output_local.reshape(state_count, cand_count, local_cols),
        values.reshape(state_count, cand_count),
    )


TP = 8
SMALL = 16
MIB = 1024 * 1024


def send(array, pairs):
    return lax.ppermute(
        array, ("tp", "dp"), [(2 * st + sd, 2 * dt + dd) for (st, sd), (dt, dd) in pairs]
    )


SPLIT = 8


def near_place(k):
    place = lax.rem(lax.axis_index("tp"), 4)
    if k == 1:
        return place + 1 - 2 * lax.rem(place, 2)
    if k == 2:
        return lax.rem(place + 2, 4)
    return place if k == 0 else 3 - place


def stage(loads, ins, outs, compute, scratch=(), limit=2, flops=0, alias=None, manual=False):
    vmem = pl.BlockSpec(memory_space=pltpu.VMEM)
    count = len(ins)
    shapes, sources, flat = list(outs), [], []
    for kind, parts in loads:
        array, total = parts[0][0], sum(part[4] for part in parts)
        shape = (total, array.shape[1]) if kind == "rows" else (array.shape[0], total)
        shapes.append(jax.ShapeDtypeStruct(shape, array.dtype))
        sources += [part[0] for part in parts]
        flat.append((kind, parts))
    n = len(sources)

    def body(*refs):
        inputs = refs[n : n + count]
        results = refs[n + count : n + count + len(outs)]
        targets = refs[n + count + len(outs) : n + count + len(shapes)]
        extra = refs[n + count + len(shapes) :]
        made, at = [], 0
        for (kind, parts), target in zip(flat, targets):
            filled = 0
            for _, place, unit, offset, size in parts:
                block = near_place(place) * unit + offset
                length = size if kind == "rows" else target.shape[0]
                piece = length // SPLIT
                for cut in range(SPLIT):
                    if kind == "rows":
                        begin = pl.multiple_of(block + cut * piece, 16)
                        view = refs[at].at[pl.ds(begin, piece), :]
                        to = target.at[pl.ds(filled + cut * piece, piece), :]
                    else:
                        rows = pl.ds(cut * piece, piece)
                        view = refs[at].at[rows, pl.ds(pl.multiple_of(block, 128), size)]
                        to = target.at[rows, pl.ds(filled, size)]
                    made.append(pltpu.make_async_copy(view, to, extra[0].at[len(made)]))
                filled += size
                at += 1
        for copy in made:
            copy.start()
        waited = []

        def wait():
            if not waited:
                waited.append(True)
                for copy in made:
                    copy.wait()

        if manual:
            compute(inputs, results, extra, list(targets), wait)
        elif compute is not None:
            compute(inputs, results, extra[1:] if n else extra)
        wait()

    loaded = sum(2 * math.prod(shape.shape) for shape in shapes[len(outs) :])
    return pl.pallas_call(
        body,
        out_shape=shapes,
        in_specs=[pl.BlockSpec(memory_space=pl.ANY)] * n + [vmem] * count,
        out_specs=[vmem] * len(shapes),
        scratch_shapes=([pltpu.SemaphoreType.DMA((n * SPLIT,))] if n else []) + list(scratch),
        input_output_aliases={} if alias is None else {n + alias: 0},
        compiler_params=pltpu.CompilerParams(vmem_limit_bytes=limit * MIB),
        cost_estimate=pl.CostEstimate(
            flops=flops, bytes_accessed=0 if manual else loaded, transcendentals=0
        ),
    )(*sources, *ins)


def to_row(column):
    size = column.shape[0]
    rows = lax.broadcasted_iota(jnp.int32, (size, size), 0)
    cols = lax.broadcasted_iota(jnp.int32, (size, size), 1)
    return jnp.sum(jnp.where(rows == cols, column, 0.0), axis=0, keepdims=True)


def to_column(row):
    size = row.shape[1]
    rows = lax.broadcasted_iota(jnp.int32, (size, size), 0)
    cols = lax.broadcasted_iota(jnp.int32, (size, size), 1)
    return jnp.sum(jnp.where(rows == cols, row, 0.0), axis=1, keepdims=True)


def basis_stage(loads, blocks, held, before, columns, features, squares, narrow):
    m, k = blocks[0].shape
    count = len(blocks)
    start, stop = columns
    width = stop - start
    tile = 512
    ins = [*blocks, *held] + ([] if before is None else [before])
    summed = squares is not None
    if summed:
        ins += [features] + squares
        rows = features.shape[0]
    outs = [jax.ShapeDtypeStruct((2, m, width), jnp.float32)]
    if narrow:
        outs.append(jax.ShapeDtypeStruct((2, m, width), jnp.bfloat16))
    if summed:
        outs.append(jax.ShapeDtypeStruct((rows, 128), jnp.float32))

    def compute(inputs, results, extra):
        refs, weights = inputs[:count], inputs[count : 3 * count]
        rest = list(inputs[3 * count :])
        lhs = extra[0]
        old = rest.pop(0) if before is not None else None
        for index, ref in enumerate(refs):
            gain = ref[m - SMALL + 4 : m - SMALL + 5, :].astype(jnp.float32)
            lhs[index] = (ref[...].astype(jnp.float32) * gain).astype(jnp.bfloat16)

        @pl.loop(0, width // tile)
        def _(j):
            at = pl.ds(pl.multiple_of(start + j * tile, tile), tile)
            to = pl.ds(pl.multiple_of(j * tile, tile), tile)
            for side in range(2):
                total = old[side, :, at] if old is not None else None
                for index in range(count):
                    term = jnp.dot(
                        lhs[index],
                        weights[2 * index + side][:, at],
                        preferred_element_type=jnp.float32,
                    )
                    total = term if total is None else total + term
                results[0][side, :, to] = total
                if narrow:
                    results[1][side, :, to] = total.astype(jnp.bfloat16)

        if summed:
            feature_rows, *parts = rest
            total = None
            for ref in refs:
                wide = jnp.dot(feature_rows[...], ref[...], preferred_element_type=jnp.float32)
                wide = wide.astype(jnp.bfloat16).astype(jnp.float32)
                wide = wide * wide
                for at in range(0, k, 128):
                    piece = wide[:, at : at + 128]
                    total = piece if total is None else total + piece
            for part in parts:
                total = total + part[...]
            results[-1][...] = total
            if narrow:
                row = to_row(jnp.sum(total, axis=1, keepdims=True))
                high = row.astype(jnp.bfloat16).astype(jnp.float32)
                last = results[1][0, m - SMALL :, :rows].astype(jnp.float32)
                line = lax.broadcasted_iota(jnp.int32, last.shape, 0)
                last = jnp.where(line == SMALL - 2, high, last)
                last = jnp.where(line == SMALL - 1, row - high, last)
                results[1][0, m - SMALL :, :rows] = last.astype(jnp.bfloat16)

    return stage(
        loads,
        ins,
        outs,
        compute,
        [pltpu.VMEM((count, m, k), jnp.bfloat16)],
        flops=4 * m * k * width * count,
        alias=None if before is None or narrow else 3 * count,
    )


def hidden_stage(loads, own, other, features, square, scale, width):
    _, m, units = own.shape
    rows = features.shape[0]
    tile = 512
    first = scale is None
    outs = [jax.ShapeDtypeStruct((rows, units), jnp.bfloat16)]
    if first:
        outs.append(jax.ShapeDtypeStruct((rows, 128), jnp.float32))

    def compute(inputs, results, extra):
        own, other, features, last = inputs
        if first:
            lines = other[0, m - SMALL :, :rows].astype(jnp.float32)
            row = lines[SMALL - 2 : SMALL - 1] + lines[SMALL - 1 :]
            squares = jnp.sum(last[...], axis=1, keepdims=True) + to_column(row)
            factor = lax.rsqrt(squares / width + epsilon)
            results[1][...] = jnp.broadcast_to(factor, results[1].shape)
        else:
            factor = last[:, :1]

        @pl.loop(0, units // tile)
        def _(j):
            at = pl.ds(pl.multiple_of(j * tile, tile), tile)
            sums = []
            for side in range(2):
                basis = own[side, :, at] + other[side, :, at].astype(jnp.float32)
                sums.append(
                    factor
                    * jnp.dot(
                        features[...],
                        basis.astype(jnp.bfloat16),
                        preferred_element_type=jnp.float32,
                    )
                )
            gate, up = sums
            results[0][:, at] = (gate / (1.0 + jnp.exp(-gate)) * up).astype(jnp.bfloat16)

    return stage(
        loads,
        [own, other, features, square if first else scale],
        outs,
        compute,
        flops=4 * m * rows * units,
    )


def down_stage(loads, hidden, weights, tile, places, widths, copies=()):
    rows = hidden[0].shape[0]
    depth = weights[0].shape[0]
    half = rows // 2
    flops = sum(2 * len(r) * half * depth * tile * len(tiles) for r, tiles, _ in places)
    counts = (len(hidden), len(weights))

    def compute(inputs, results, extra, loaded, wait):
        hidden = inputs[: counts[0]]
        weights = list(inputs[counts[0] : sum(counts)])
        sources = inputs[sum(counts) :]
        for parts, tiles, targets in places:
            low, high = parts[0] * half, parts[-1] * half + half
            for j, (index, at) in enumerate(tiles):
                if index == len(weights):
                    wait()
                    weights += loaded
                total = None
                depth_at = 0
                for ref in hidden:
                    size = ref.shape[1]
                    term = jnp.dot(
                        ref[low:high, :],
                        weights[index][depth_at : depth_at + size, at : at + tile],
                        preferred_element_type=jnp.float32,
                    )
                    total = term if total is None else total + term
                    depth_at += size
                total = total.astype(jnp.bfloat16)
                for part, (out, column) in enumerate(targets):
                    to = column + j * tile
                    results[out][:, to : to + tile] = total[part * half : (part + 1) * half]
        for source, (_, out) in zip(sources, copies):
            results[out][:, : source.shape[1]] = source[...]

    return stage(
        loads,
        [*hidden, *weights, *[copy[0] for copy in copies]],
        [jax.ShapeDtypeStruct((half, width), jnp.bfloat16) for width in widths],
        compute,
        limit=6,
        flops=flops // 16,
        manual=True,
    )


def piece_body(weight, states, gain, seeds, piece, rows):
    half = weight.shape[0] // 2
    count = states.shape[0]
    piece[:half, :] = weight[pl.ds(pl.multiple_of(lax.axis_index("dp") * half, 16), half), :]
    rows[...] = jnp.zeros_like(rows)
    rows[:count, :] = states[...].astype(jnp.float32)
    rows[count : count + 1, :] = gain[...].reshape(1, -1)
    high = lax.shift_right_logical(seeds[...], 8)
    low = seeds[...] - high * 256
    width = seeds.shape[1]
    rows[count + 1 : 2 * count + 1, :width] = high.astype(jnp.float32)
    rows[2 * count + 1 : 3 * count + 1, :width] = low.astype(jnp.float32)
    piece[half:, :] = rows[...].astype(jnp.bfloat16)


def block_body(count, cands, piece, first, second, weight, states, mean, spread, gain, value,
               block, features, inputs, head, rows):
    f32, bf16 = jnp.float32, jnp.bfloat16
    half = weight.shape[0] // 2
    act = weight.shape[0]
    core = lax.axis_index("dp")
    lower = core == 0
    home = lax.div(lax.axis_index("tp"), 4) == core
    same = jnp.where(home, piece[...], first[...])
    other = jnp.where(home, first[...], second[...])
    low = jnp.where(lower, same, other)
    high = jnp.where(lower, other, same)
    block[:half, :] = low[:half]
    block[half:act, :] = high[:half]
    parts = [low[half:].astype(f32), high[half:].astype(f32)]
    rows[...] = jnp.zeros_like(rows)
    for index, part in enumerate(parts):
        rows[index * count : (index + 1) * count, :] = part[:count]
    rows[2 * count : 2 * count + 1, :] = parts[0][count : count + 1]
    block[act:, :] = rows[...].astype(bf16)

    harmonic = (lax.broadcasted_iota(jnp.int32, (cands, act), 1) + 1).astype(f32)
    diagonal = lax.broadcasted_iota(jnp.int32, (cands, cands), 0) == lax.broadcasted_iota(
        jnp.int32, (cands, cands), 1
    )
    states_at = lax.broadcasted_iota(jnp.int32, (cands, SMALL), 1)
    made = []
    for state in range(2 * count):
        part, at = parts[state // count], state % count
        seed = (
            part[count + 1 + at : count + 2 + at, :cands] * 256.0
            + part[2 * count + 1 + at : 2 * count + 2 + at, :cands]
        )
        column = jnp.sum(jnp.where(diagonal, seed, 0.0), axis=1, keepdims=True)
        product = column * harmonic
        rest = product - modulus * jnp.floor(product * (1.0 / modulus))
        rest = jnp.where(rest < 0.0, rest + modulus, rest)
        rest = jnp.where(rest >= modulus, rest - modulus, rest)
        wave = jnp.cos(rest * (2.0 * math.pi / modulus))
        value_rows = (mean[...].reshape(1, -1) + spread[...].reshape(1, -1) * wave).astype(bf16)
        made.append(value_rows)
        to = slice(state * cands, (state + 1) * cands)
        features[to, :act] = value_rows
        features[to, act:] = (states_at == state).astype(f32).astype(bf16)
    for at in range(count):
        own = jnp.where(lower, made[at], made[count + at])
        wide = jnp.dot(own, weight[...], preferred_element_type=f32)
        wide = wide + states[at : at + 1, :].astype(f32)
        inputs[at * cands : (at + 1) * cands, :] = wide.astype(bf16)
    head[...] = (gain[...] * value[...]).reshape(1, -1)


def whole_call(body, outs, scratch, after, *operands):
    whole = lambda array: pl.BlockSpec(array.shape, lambda i: (0,) * len(array.shape))
    count = len(after)
    return pl.pallas_call(
        lambda *refs: body(*refs[count:]),
        out_shape=outs,
        grid=(1,),
        in_specs=[pl.BlockSpec(memory_space=pl.ANY)] * count
        + [whole(array) for array in operands],
        out_specs=[whole(array) for array in outs],
        scratch_shapes=scratch,
        compiler_params=pltpu.CompilerParams(vmem_limit_bytes=6 * MIB),
        cost_estimate=pl.CostEstimate(flops=1000000, bytes_accessed=1000000, transcendentals=0),
    )(*after, *operands)


def local_blocks(
    state_hidden,
    action_seeds,
    action_mean,
    action_spread,
    action_weight,
    norm_gain,
    gate_weight,
    up_weight,
    down_weight,
    head_gain,
    value_weight,
):
    f32, bf16 = jnp.float32, jnp.bfloat16
    states, cands = action_seeds.shape
    rows = states * cands
    act, cols = action_weight.shape
    half = act // 2
    units = gate_weight.shape[1]
    full_width = gate_weight.shape[0] * 2
    tp, dp = lax.axis_index("tp"), lax.axis_index("dp")
    home = tp // 4 == dp
    every = [(t, d) for t in range(TP) for d in range(2)]
    swap_core = [((t, d), (t, 1 - d)) for t, d in every]

    out = jax.ShapeDtypeStruct
    (piece,) = whole_call(
        piece_body,
        [out((half + SMALL, cols), bf16)],
        [pltpu.VMEM((SMALL, cols), f32)],
        [],
        *[
            pltpu.with_memory_space_constraint(array, pltpu.HBM)
            for array in (action_weight, state_hidden, norm_gain, action_seeds)
        ],
    )

    first = send(
        piece,
        [((t, t // 4), (t ^ 4, t // 4)) for t in range(TP)]
        + [((t, 1 - t // 4), (t, t // 4)) for t in range(TP)],
    )
    second = send(piece, [((t, 1 - t // 4), (t ^ 4, t // 4)) for t in range(TP)])

    gate_weight, up_weight, down_weight = (
        pltpu.with_memory_space_constraint(weight, pltpu.HBM)
        for weight in (gate_weight, up_weight, down_weight)
    )
    pair = lambda k: [("rows", [(w, k, cols, 0, cols)]) for w in (gate_weight, up_weight)]
    column = lambda k: ("cols", [(down_weight, k, cols, 0, cols)])
    tile = cols // 2
    held = stage(pair(0), [], [], None)

    block, features, inputs_local, head = whole_call(
        functools.partial(block_body, states, cands),
        [
            out((act + SMALL, cols), bf16),
            out((2 * rows, act + SMALL), bf16),
            out((rows, cols), bf16),
            out((1, cols), f32),
        ],
        [pltpu.VMEM((SMALL, cols), f32)],
        held,
        piece,
        first,
        second,
        action_weight,
        state_hidden,
        action_mean,
        action_spread,
        head_gain,
        value_weight,
    )

    step = lambda array, k: send(array, [((t, d), (t ^ k, d)) for t, d in every])
    near = {k: step(block, k) for k in (2, 1, 3)}

    span = (0, units)
    basis, square, *held = basis_stage(
        pair(2) + pair(1), [block], held, None, span, features, [], False
    )
    basis, square, *last = basis_stage(
        pair(3), [near[2]], held[:2], basis, span, features, [square], False
    )
    basis, square, down_diagonal = basis_stage(
        [column(3)], [near[1]], held[2:], basis, span, features, [square], False
    )
    cut = units // 2
    own_a, narrow_a, square, down_x = basis_stage(
        [column(1)], [near[3]], last, basis, (0, cut), features, [square], True
    )
    other_a = send(narrow_a, swap_core)
    own_b, narrow_b, down_z = basis_stage(
        [column(2)], [near[3]], last, basis, (cut, units), features, None, True
    )
    other_b = send(narrow_b, swap_core)
    hidden_a, scale = hidden_stage(
        [], own_a, other_a, features, square, None, full_width
    )
    (hidden_b,) = hidden_stage([], own_b, other_b, features, None, scale, full_width)
    hidden = [hidden_a, hidden_b]

    both, lower, upper = (0, 1), (0,), (1,)
    x_pair, diagonal_upper = down_stage(
        [],
        hidden,
        [down_diagonal, down_x],
        tile,
        [
            (both, [(0, 0), (0, tile)], [(0, 0), (1, 0)]),
            (lower, [(1, 0), (1, tile)], [(0, cols)]),
        ],
        [2 * cols, cols],
    )
    got_x = step(x_pair, 1)
    (z_pair,) = down_stage(
        [],
        hidden,
        [down_z],
        tile,
        [(upper, [(0, 0), (0, tile)], [(0, cols)])],
        [2 * cols],
        [(diagonal_upper, 0)],
    )
    got_z = step(z_pair, 2)
    z_lower, x_upper, own_lower, own_upper, _ = down_stage(
        [column(0)],
        hidden,
        [down_z, down_x],
        tile,
        [
            (lower, [(0, 0), (0, tile)], [(0, 0)]),
            (upper, [(1, 0), (1, tile)], [(1, 0)]),
            (both, [(2, 0), (2, tile)], [(2, 0), (3, 0)]),
        ],
        [cols] * 4,
    )
    add = lambda *parts: sum(part.astype(f32) for part in parts).astype(bf16)
    got_lower = step(add(z_lower, got_x[:, :cols]), 2)
    got_upper = step(add(x_upper, got_z[:, :cols]), 1)
    sums = [
        lax.optimization_barrier(add(own_lower, got_x[:, cols:], got_lower)),
        lax.optimization_barrier(add(own_upper, got_z[:, cols:], got_upper)),
    ]
    far = [
        send(sums[part], [((t, 1 - t // 4), (t ^ 4, part)) for t in range(TP)])
        for part in range(2)
    ]
    crossed = send(
        jnp.where(dp == 0, sums[1], sums[0]), [((t, t // 4), (t, 1 - t // 4)) for t in range(TP)]
    )
    mine = jnp.where(home, jnp.where(dp == 0, sums[0], sums[1]), crossed).astype(f32)
    summed = mine + jnp.where(dp == 0, far[0], far[1]).astype(f32)
    output_local = (inputs_local.astype(f32) + summed).astype(bf16)

    wide_out = output_local.astype(f32)
    totals = jnp.stack(
        [
            jnp.sum(wide_out * wide_out, axis=1),
            jnp.sum(wide_out * head, axis=1),
        ]
    )
    for k in (1, 2, 4):
        totals = totals + step(totals, k)
    values = totals[1] * lax.rsqrt(totals[0] / full_width + epsilon)
    return (
        output_local.reshape(states, cands, cols),
        values.reshape(states, cands),
    )


def solution(mesh):
    local = local_blocks if mesh.shape["tp"] == TP and mesh.shape["dp"] == 2 else local_gathered
    return jax.shard_map(
        local,
        mesh=mesh,
        in_specs=(
            P(("rep", "dp"), "tp"),
            P(("rep", "dp"), None),
            P("rep"),
            P("rep"),
            P(None, "tp"),
            P("tp"),
            P("dp", "tp"),
            P("dp", "tp"),
            P("tp", "dp"),
            P("tp"),
            P("tp"),
        ),
        out_specs=(P(("rep", "dp"), None, "tp"), P(("rep", "dp"), None)),
        check_vma=False,
    )
```

```python
import functools
import math

import jax
import jax.numpy as jnp
from jax import lax
from jax.experimental import pallas as pl
from jax.experimental.pallas import tpu as pltpu
from jax.sharding import PartitionSpec as P

epsilon = 1e-05
modulus = 251


def action_features(action_seeds, action_mean, action_spread):
    harmonic = jnp.arange(1, action_mean.shape[0] + 1, dtype=jnp.int32)
    phases = action_seeds[:, :, None] * harmonic % modulus
    angles = phases.astype(jnp.float32) * (2.0 * math.pi / modulus)
    return (action_mean + action_spread * jnp.cos(angles)).astype(jnp.bfloat16)


def head_value(output_rows, head_gain, value_weight):
    wide_out = output_rows.astype(jnp.float32)
    scale = lax.rsqrt(jnp.mean(wide_out * wide_out, axis=1) + epsilon)
    return jnp.sum(wide_out * (head_gain * value_weight), axis=1) * scale


def local_gathered(
    state_hidden,
    action_seeds,
    action_mean,
    action_spread,
    action_weight,
    norm_gain,
    gate_weight,
    up_weight,
    down_weight,
    head_gain,
    value_weight,
):
    state_count, cand_count = action_seeds.shape
    row_count = state_count * cand_count
    local_cols = action_weight.shape[1]
    features = action_features(action_seeds, action_mean, action_spread)
    embedded = jnp.dot(
        features.reshape(row_count, features.shape[2]),
        action_weight,
        preferred_element_type=jnp.float32,
    )
    inputs_local = (
        (
            state_hidden.astype(jnp.float32)[:, None, :]
            + embedded.reshape(state_count, cand_count, local_cols)
        )
        .reshape(row_count, local_cols)
        .astype(jnp.bfloat16)
    )
    gathered, gain_full = (
        lax.all_gather(inputs_local, "tp", axis=1, tiled=True),
        lax.all_gather(norm_gain.astype(jnp.bfloat16), "tp", axis=0, tiled=True).astype(
            norm_gain.dtype
        ),
    )
    scale = lax.rsqrt(
        jnp.mean(jnp.square(gathered.astype(jnp.float32)), axis=1, keepdims=True) + epsilon
    )
    normed = (gathered.astype(jnp.float32) * scale * gain_full).astype(jnp.bfloat16)
    gate_sum = jnp.dot(
        normed,
        lax.all_gather(gate_weight, "dp", axis=0, tiled=True),
        preferred_element_type=jnp.float32,
    )
    up_sum = jnp.dot(
        normed,
        lax.all_gather(up_weight, "dp", axis=0, tiled=True),
        preferred_element_type=jnp.float32,
    )
    hidden = (jax.nn.silu(gate_sum) * up_sum).astype(jnp.bfloat16)
    partial_terms = jnp.dot(
        hidden,
        lax.all_gather(down_weight, "dp", axis=1, tiled=True),
        preferred_element_type=jnp.float32,
    )
    summed_local = lax.psum_scatter(partial_terms, "tp", scatter_dimension=1, tiled=True)
    output_local = (inputs_local.astype(jnp.float32) + summed_local).astype(jnp.bfloat16)
    output_full, head_full, value_full = (
        lax.all_gather(output_local, "tp", axis=1, tiled=True),
        lax.all_gather(head_gain.astype(jnp.bfloat16), "tp", axis=0, tiled=True).astype(
            head_gain.dtype
        ),
        lax.all_gather(value_weight.astype(jnp.bfloat16), "tp", axis=0, tiled=True).astype(
            value_weight.dtype
        ),
    )
    values = head_value(output_full, head_full, value_full)
    return (
        output_local.reshape(state_count, cand_count, local_cols),
        values.reshape(state_count, cand_count),
    )


TP = 8
SMALL = 16
MIB = 1024 * 1024


def send(array, pairs):
    return lax.ppermute(
        array, ("tp", "dp"), [(2 * st + sd, 2 * dt + dd) for (st, sd), (dt, dd) in pairs]
    )


SPLIT = 8


def near_place(k):
    place = lax.rem(lax.axis_index("tp"), 4)
    if k == 1:
        return place + 1 - 2 * lax.rem(place, 2)
    if k == 2:
        return lax.rem(place + 2, 4)
    return place if k == 0 else 3 - place


def stage(loads, ins, outs, compute, scratch=(), limit=2, flops=0, alias=None, manual=False):
    vmem = pl.BlockSpec(memory_space=pltpu.VMEM)
    count = len(ins)
    shapes, sources, flat = list(outs), [], []
    for kind, parts in loads:
        array, total = parts[0][0], sum(part[4] for part in parts)
        shape = (total, array.shape[1]) if kind == "rows" else (array.shape[0], total)
        shapes.append(jax.ShapeDtypeStruct(shape, array.dtype))
        sources += [part[0] for part in parts]
        flat.append((kind, parts))
    n = len(sources)

    def body(*refs):
        inputs = refs[n : n + count]
        results = refs[n + count : n + count + len(outs)]
        targets = refs[n + count + len(outs) : n + count + len(shapes)]
        extra = refs[n + count + len(shapes) :]
        made, at = [], 0
        for (kind, parts), target in zip(flat, targets):
            filled = 0
            for _, place, unit, offset, size in parts:
                block = near_place(place) * unit + offset
                length = size if kind == "rows" else target.shape[0]
                piece = length // SPLIT
                for cut in range(SPLIT):
                    if kind == "rows":
                        begin = pl.multiple_of(block + cut * piece, 16)
                        view = refs[at].at[pl.ds(begin, piece), :]
                        to = target.at[pl.ds(filled + cut * piece, piece), :]
                    else:
                        rows = pl.ds(cut * piece, piece)
                        view = refs[at].at[rows, pl.ds(pl.multiple_of(block, 128), size)]
                        to = target.at[rows, pl.ds(filled, size)]
                    made.append(pltpu.make_async_copy(view, to, extra[0].at[len(made)]))
                filled += size
                at += 1
        for copy in made:
            copy.start()
        waited = []

        def wait():
            if not waited:
                waited.append(True)
                for copy in made:
                    copy.wait()

        if manual:
            compute(inputs, results, extra, list(targets), wait)
        elif compute is not None:
            compute(inputs, results, extra[1:] if n else extra)
        wait()

    loaded = sum(2 * math.prod(shape.shape) for shape in shapes[len(outs) :])
    return pl.pallas_call(
        body,
        out_shape=shapes,
        in_specs=[pl.BlockSpec(memory_space=pl.ANY)] * n + [vmem] * count,
        out_specs=[vmem] * len(shapes),
        scratch_shapes=([pltpu.SemaphoreType.DMA((n * SPLIT,))] if n else []) + list(scratch),
        input_output_aliases={} if alias is None else {n + alias: 0},
        compiler_params=pltpu.CompilerParams(vmem_limit_bytes=limit * MIB),
        cost_estimate=pl.CostEstimate(
            flops=flops, bytes_accessed=loaded, transcendentals=0
        ),
    )(*sources, *ins)


def to_row(column):
    size = column.shape[0]
    rows = lax.broadcasted_iota(jnp.int32, (size, size), 0)
    cols = lax.broadcasted_iota(jnp.int32, (size, size), 1)
    return jnp.sum(jnp.where(rows == cols, column, 0.0), axis=0, keepdims=True)


def to_column(row):
    size = row.shape[1]
    rows = lax.broadcasted_iota(jnp.int32, (size, size), 0)
    cols = lax.broadcasted_iota(jnp.int32, (size, size), 1)
    return jnp.sum(jnp.where(rows == cols, row, 0.0), axis=1, keepdims=True)


def basis_stage(loads, blocks, held, before, columns, features, squares, narrow):
    m, k = blocks[0].shape
    count = len(blocks)
    start, stop = columns
    width = stop - start
    tile = 512
    ins = [*blocks, *held] + ([] if before is None else [before])
    summed = squares is not None
    if summed:
        ins += [features] + squares
        rows = features.shape[0]
    outs = [jax.ShapeDtypeStruct((2, m, width), jnp.float32)]
    if narrow:
        outs.append(jax.ShapeDtypeStruct((2, m, width), jnp.bfloat16))
    if summed:
        outs.append(jax.ShapeDtypeStruct((rows, 128), jnp.float32))

    def compute(inputs, results, extra):
        refs, weights = inputs[:count], inputs[count : 3 * count]
        rest = list(inputs[3 * count :])
        lhs = extra[0]
        old = rest.pop(0) if before is not None else None
        for index, ref in enumerate(refs):
            gain = ref[m - SMALL + 4 : m - SMALL + 5, :].astype(jnp.float32)
            lhs[index] = (ref[...].astype(jnp.float32) * gain).astype(jnp.bfloat16)

        @pl.loop(0, width // tile)
        def _(j):
            at = pl.ds(pl.multiple_of(start + j * tile, tile), tile)
            to = pl.ds(pl.multiple_of(j * tile, tile), tile)
            for side in range(2):
                total = old[side, :, at] if old is not None else None
                for index in range(count):
                    term = jnp.dot(
                        lhs[index],
                        weights[2 * index + side][:, at],
                        preferred_element_type=jnp.float32,
                    )
                    total = term if total is None else total + term
                results[0][side, :, to] = total
                if narrow:
                    results[1][side, :, to] = total.astype(jnp.bfloat16)

        if summed:
            feature_rows, *parts = rest
            total = None
            for ref in refs:
                wide = jnp.dot(feature_rows[...], ref[...], preferred_element_type=jnp.float32)
                wide = wide.astype(jnp.bfloat16).astype(jnp.float32)
                wide = wide * wide
                for at in range(0, k, 128):
                    piece = wide[:, at : at + 128]
                    total = piece if total is None else total + piece
            for part in parts:
                total = total + part[...]
            results[-1][...] = total
            if narrow:
                row = to_row(jnp.sum(total, axis=1, keepdims=True))
                high = row.astype(jnp.bfloat16).astype(jnp.float32)
                last = results[1][0, m - SMALL :, :rows].astype(jnp.float32)
                line = lax.broadcasted_iota(jnp.int32, last.shape, 0)
                last = jnp.where(line == SMALL - 2, high, last)
                last = jnp.where(line == SMALL - 1, row - high, last)
                results[1][0, m - SMALL :, :rows] = last.astype(jnp.bfloat16)

    return stage(
        loads,
        ins,
        outs,
        compute,
        [pltpu.VMEM((count, m, k), jnp.bfloat16)],
        flops=4 * m * k * width * count,
        alias=None if before is None or narrow else 3 * count,
    )


def hidden_stage(loads, own, other, features, square, scale, width):
    _, m, units = own.shape
    rows = features.shape[0]
    tile = 512
    first = scale is None
    outs = [jax.ShapeDtypeStruct((rows, units), jnp.bfloat16)]
    if first:
        outs.append(jax.ShapeDtypeStruct((rows, 128), jnp.float32))

    def compute(inputs, results, extra):
        own, other, features, last = inputs
        if first:
            lines = other[0, m - SMALL :, :rows].astype(jnp.float32)
            row = lines[SMALL - 2 : SMALL - 1] + lines[SMALL - 1 :]
            squares = jnp.sum(last[...], axis=1, keepdims=True) + to_column(row)
            factor = lax.rsqrt(squares / width + epsilon)
            results[1][...] = jnp.broadcast_to(factor, results[1].shape)
        else:
            factor = last[:, :1]

        @pl.loop(0, units // tile)
        def _(j):
            at = pl.ds(pl.multiple_of(j * tile, tile), tile)
            sums = []
            for side in range(2):
                basis = own[side, :, at] + other[side, :, at].astype(jnp.float32)
                sums.append(
                    factor
                    * jnp.dot(
                        features[...],
                        basis.astype(jnp.bfloat16),
                        preferred_element_type=jnp.float32,
                    )
                )
            gate, up = sums
            results[0][:, at] = (gate / (1.0 + jnp.exp(-gate)) * up).astype(jnp.bfloat16)

    return stage(
        loads,
        [own, other, features, square if first else scale],
        outs,
        compute,
        flops=4 * m * rows * units,
    )


def down_stage(loads, hidden, weights, tile, places, widths, copies=()):
    rows = hidden[0].shape[0]
    depth = weights[0].shape[0]
    half = rows // 2
    flops = sum(2 * len(r) * half * depth * tile * len(tiles) for r, tiles, _ in places)
    counts = (len(hidden), len(weights))

    def compute(inputs, results, extra, loaded, wait):
        hidden = inputs[: counts[0]]
        weights = list(inputs[counts[0] : sum(counts)])
        sources = inputs[sum(counts) :]
        for parts, tiles, targets in places:
            low, high = parts[0] * half, parts[-1] * half + half
            for j, (index, at) in enumerate(tiles):
                if index == len(weights):
                    wait()
                    weights += loaded
                total = None
                depth_at = 0
                for ref in hidden:
                    size = ref.shape[1]
                    term = jnp.dot(
                        ref[low:high, :],
                        weights[index][depth_at : depth_at + size, at : at + tile],
                        preferred_element_type=jnp.float32,
                    )
                    total = term if total is None else total + term
                    depth_at += size
                total = total.astype(jnp.bfloat16)
                for part, (out, column) in enumerate(targets):
                    to = column + j * tile
                    results[out][:, to : to + tile] = total[part * half : (part + 1) * half]
        for source, (_, out) in zip(sources, copies):
            results[out][:, : source.shape[1]] = source[...]

    return stage(
        loads,
        [*hidden, *weights, *[copy[0] for copy in copies]],
        [jax.ShapeDtypeStruct((half, width), jnp.bfloat16) for width in widths],
        compute,
        limit=6,
        flops=flops // 16,
        manual=True,
    )


def piece_body(weight, states, gain, seeds, piece, rows):
    half = weight.shape[0] // 2
    count = states.shape[0]
    piece[:half, :] = weight[pl.ds(pl.multiple_of(lax.axis_index("dp") * half, 16), half), :]
    rows[...] = jnp.zeros_like(rows)
    rows[:count, :] = states[...].astype(jnp.float32)
    rows[count : count + 1, :] = gain[...].reshape(1, -1)
    high = lax.shift_right_logical(seeds[...], 8)
    low = seeds[...] - high * 256
    width = seeds.shape[1]
    rows[count + 1 : 2 * count + 1, :width] = high.astype(jnp.float32)
    rows[2 * count + 1 : 3 * count + 1, :width] = low.astype(jnp.float32)
    piece[half:, :] = rows[...].astype(jnp.bfloat16)


def block_body(count, cands, piece, first, second, weight, states, mean, spread, gain, value,
               block, features, inputs, head, rows):
    f32, bf16 = jnp.float32, jnp.bfloat16
    half = weight.shape[0] // 2
    act = weight.shape[0]
    core = lax.axis_index("dp")
    lower = core == 0
    home = lax.div(lax.axis_index("tp"), 4) == core
    same = jnp.where(home, piece[...], first[...])
    other = jnp.where(home, first[...], second[...])
    low = jnp.where(lower, same, other)
    high = jnp.where(lower, other, same)
    block[:half, :] = low[:half]
    block[half:act, :] = high[:half]
    parts = [low[half:].astype(f32), high[half:].astype(f32)]
    rows[...] = jnp.zeros_like(rows)
    for index, part in enumerate(parts):
        rows[index * count : (index + 1) * count, :] = part[:count]
    rows[2 * count : 2 * count + 1, :] = parts[0][count : count + 1]
    block[act:, :] = rows[...].astype(bf16)

    harmonic = (lax.broadcasted_iota(jnp.int32, (cands, act), 1) + 1).astype(f32)
    diagonal = lax.broadcasted_iota(jnp.int32, (cands, cands), 0) == lax.broadcasted_iota(
        jnp.int32, (cands, cands), 1
    )
    states_at = lax.broadcasted_iota(jnp.int32, (cands, SMALL), 1)
    made = []
    for state in range(2 * count):
        part, at = parts[state // count], state % count
        seed = (
            part[count + 1 + at : count + 2 + at, :cands] * 256.0
            + part[2 * count + 1 + at : 2 * count + 2 + at, :cands]
        )
        column = jnp.sum(jnp.where(diagonal, seed, 0.0), axis=1, keepdims=True)
        product = column * harmonic
        rest = product - modulus * jnp.floor(product * (1.0 / modulus))
        rest = jnp.where(rest < 0.0, rest + modulus, rest)
        rest = jnp.where(rest >= modulus, rest - modulus, rest)
        wave = jnp.cos(rest * (2.0 * math.pi / modulus))
        value_rows = (mean[...].reshape(1, -1) + spread[...].reshape(1, -1) * wave).astype(bf16)
        made.append(value_rows)
        to = slice(state * cands, (state + 1) * cands)
        features[to, :act] = value_rows
        features[to, act:] = (states_at == state).astype(f32).astype(bf16)
    for at in range(count):
        own = jnp.where(lower, made[at], made[count + at])
        wide = jnp.dot(own, weight[...], preferred_element_type=f32)
        wide = wide + states[at : at + 1, :].astype(f32)
        inputs[at * cands : (at + 1) * cands, :] = wide.astype(bf16)
    head[...] = (gain[...] * value[...]).reshape(1, -1)


def whole_call(body, outs, scratch, after, *operands):
    whole = lambda array: pl.BlockSpec(array.shape, lambda i: (0,) * len(array.shape))
    count = len(after)
    return pl.pallas_call(
        lambda *refs: body(*refs[count:]),
        out_shape=outs,
        grid=(1,),
        in_specs=[pl.BlockSpec(memory_space=pl.ANY)] * count
        + [whole(array) for array in operands],
        out_specs=[whole(array) for array in outs],
        scratch_shapes=scratch,
        compiler_params=pltpu.CompilerParams(vmem_limit_bytes=6 * MIB),
        cost_estimate=pl.CostEstimate(flops=1000000, bytes_accessed=1000000, transcendentals=0),
    )(*after, *operands)


def local_blocks(
    state_hidden,
    action_seeds,
    action_mean,
    action_spread,
    action_weight,
    norm_gain,
    gate_weight,
    up_weight,
    down_weight,
    head_gain,
    value_weight,
):
    f32, bf16 = jnp.float32, jnp.bfloat16
    states, cands = action_seeds.shape
    rows = states * cands
    act, cols = action_weight.shape
    half = act // 2
    units = gate_weight.shape[1]
    full_width = gate_weight.shape[0] * 2
    tp, dp = lax.axis_index("tp"), lax.axis_index("dp")
    home = tp // 4 == dp
    every = [(t, d) for t in range(TP) for d in range(2)]
    swap_core = [((t, d), (t, 1 - d)) for t, d in every]

    out = jax.ShapeDtypeStruct
    (piece,) = whole_call(
        piece_body,
        [out((half + SMALL, cols), bf16)],
        [pltpu.VMEM((SMALL, cols), f32)],
        [],
        *[
            pltpu.with_memory_space_constraint(array, pltpu.HBM)
            for array in (action_weight, state_hidden, norm_gain, action_seeds)
        ],
    )

    first = send(
        piece,
        [((t, t // 4), (t ^ 4, t // 4)) for t in range(TP)]
        + [((t, 1 - t // 4), (t, t // 4)) for t in range(TP)],
    )
    second = send(piece, [((t, 1 - t // 4), (t ^ 4, t // 4)) for t in range(TP)])

    gate_weight, up_weight, down_weight = (
        pltpu.with_memory_space_constraint(weight, pltpu.HBM)
        for weight in (gate_weight, up_weight, down_weight)
    )
    pair = lambda k: [("rows", [(w, k, cols, 0, cols)]) for w in (gate_weight, up_weight)]
    column = lambda k: ("cols", [(down_weight, k, cols, 0, cols)])
    tile = cols // 2
    held = stage(pair(0), [], [], None)

    block, features, inputs_local, head = whole_call(
        functools.partial(block_body, states, cands),
        [
            out((act + SMALL, cols), bf16),
            out((2 * rows, act + SMALL), bf16),
            out((rows, cols), bf16),
            out((1, cols), f32),
        ],
        [pltpu.VMEM((SMALL, cols), f32)],
        held,
        piece,
        first,
        second,
        action_weight,
        state_hidden,
        action_mean,
        action_spread,
        head_gain,
        value_weight,
    )

    step = lambda array, k: send(array, [((t, d), (t ^ k, d)) for t, d in every])
    near = {k: step(block, k) for k in (2, 1, 3)}

    span = (0, units)
    basis, square, *held = basis_stage(
        pair(2) + pair(1), [block], held, None, span, features, [], False
    )
    basis, square, *last = basis_stage(
        pair(3), [near[2]], held[:2], basis, span, features, [square], False
    )
    basis, square, down_diagonal = basis_stage(
        [column(3)], [near[1]], held[2:], basis, span, features, [square], False
    )
    cut = units // 2
    own_a, narrow_a, square, down_x = basis_stage(
        [column(1)], [near[3]], last, basis, (0, cut), features, [square], True
    )
    other_a = send(narrow_a, swap_core)
    own_b, narrow_b, down_z = basis_stage(
        [column(2)], [near[3]], last, basis, (cut, units), features, None, True
    )
    other_b = send(narrow_b, swap_core)
    hidden_a, scale = hidden_stage(
        [], own_a, other_a, features, square, None, full_width
    )
    (hidden_b,) = hidden_stage([], own_b, other_b, features, None, scale, full_width)
    hidden = [hidden_a, hidden_b]

    both, lower, upper = (0, 1), (0,), (1,)
    x_pair, diagonal_upper = down_stage(
        [],
        hidden,
        [down_diagonal, down_x],
        tile,
        [
            (both, [(0, 0), (0, tile)], [(0, 0), (1, 0)]),
            (lower, [(1, 0), (1, tile)], [(0, cols)]),
        ],
        [2 * cols, cols],
    )
    got_x = step(x_pair, 1)
    (z_pair,) = down_stage(
        [],
        hidden,
        [down_z],
        tile,
        [(upper, [(0, 0), (0, tile)], [(0, cols)])],
        [2 * cols],
        [(diagonal_upper, 0)],
    )
    got_z = step(z_pair, 2)
    z_lower, x_upper, own_lower, own_upper, _ = down_stage(
        [column(0)],
        hidden,
        [down_z, down_x],
        tile,
        [
            (lower, [(0, 0), (0, tile)], [(0, 0)]),
            (upper, [(1, 0), (1, tile)], [(1, 0)]),
            (both, [(2, 0), (2, tile)], [(2, 0), (3, 0)]),
        ],
        [cols] * 4,
    )
    add = lambda *parts: sum(part.astype(f32) for part in parts).astype(bf16)
    got_lower = step(add(z_lower, got_x[:, :cols]), 2)
    got_upper = step(add(x_upper, got_z[:, :cols]), 1)
    sums = [
        lax.optimization_barrier(add(own_lower, got_x[:, cols:], got_lower)),
        lax.optimization_barrier(add(own_upper, got_z[:, cols:], got_upper)),
    ]
    far = [
        send(sums[part], [((t, 1 - t // 4), (t ^ 4, part)) for t in range(TP)])
        for part in range(2)
    ]
    crossed = send(
        jnp.where(dp == 0, sums[1], sums[0]), [((t, t // 4), (t, 1 - t // 4)) for t in range(TP)]
    )
    mine = jnp.where(home, jnp.where(dp == 0, sums[0], sums[1]), crossed).astype(f32)
    summed = mine + jnp.where(dp == 0, far[0], far[1]).astype(f32)
    output_local = (inputs_local.astype(f32) + summed).astype(bf16)

    wide_out = output_local.astype(f32)
    totals = jnp.stack(
        [
            jnp.sum(wide_out * wide_out, axis=1),
            jnp.sum(wide_out * head, axis=1),
        ]
    )
    for k in (1, 2, 4):
        totals = totals + step(totals, k)
    values = totals[1] * lax.rsqrt(totals[0] / full_width + epsilon)
    return (
        output_local.reshape(states, cands, cols),
        values.reshape(states, cands),
    )


def solution(mesh):
    local = local_blocks if mesh.shape["tp"] == TP and mesh.shape["dp"] == 2 else local_gathered
    return jax.shard_map(
        local,
        mesh=mesh,
        in_specs=(
            P(("rep", "dp"), "tp"),
            P(("rep", "dp"), None),
            P("rep"),
            P("rep"),
            P(None, "tp"),
            P("tp"),
            P("dp", "tp"),
            P("dp", "tp"),
            P("tp", "dp"),
            P("tp"),
            P("tp"),
        ),
        out_specs=(P(("rep", "dp"), None, "tp"), P(("rep", "dp"), None)),
        check_vma=False,
    )
```
